32 devices in a mesh: grp: 2 (over y), slab: 4 (over z), sub: 4 (over x, core).
Axes of the slice: x: 2, y: 2, z: 4, core: 2. Of those that a mesh axis runs over, the one named last changes fastest.
Arguments:
- latent: bfloat16 [81920, 128], P(('grp', 'slab', 'sub')), parts along dimension 0, may hold values from -6 to 6
- positions: bfloat16 [3, 81920], P(None, ('grp', 'slab', 'sub')), parts along dimension 1, may hold values from -2.5 to 2.5
- target: int32 [320], P(('grp', 'slab', 'sub')), parts along dimension 0, may hold values from -1 to 127, as said below
- neighbours: int32 [320, 8], P(('grp', 'slab', 'sub')), parts along dimension 0, may hold values from 0 to 159, as said below
- w_send: bfloat16 [128, 256], replicated, may hold values from -0.5 to 0.5
- w_in: bfloat16 [256, 128], replicated, may hold values from -0.375 to 0.375
- w_out: bfloat16 [128, 128], replicated, may hold values from -0.5 to 0.5
Outputs:
- relocated: bfloat16 [65536, 128], P(('grp', 'slab', 'sub')), parts along dimension 0
The draws below stay inside these ranges and needn't reach their ends.
There are 2 independent parts, one for each index of `grp`. The reference program is written for one: setup_inputs(seed, part) draws one part's arguments, and reference() takes and returns one part's arrays. A program takes and returns all parts, laid end to end along the dimension named above; an argument that names none is the same for every part. Nothing has to cross between parts.
Inputs may be any that keep to these rules, and one draw needn't show every extreme that they name: `target`: -1 marks a slot that holds no block. A block goes to the device of the same sub index on its own slab or on the slab just below or above; every output block slot receives exactly one block; the blocks of one device that go to one neighbouring slab number at most 1, exactly 1 to the slab above on every device of the first slab, and exactly 1 to the slab below on every device of the last slab. `neighbours`: each entry is a slot that holds a block, on a device of the same slab or of the slab just below or above (any sub index), or the slot's own id.
All inputs are finite; a program needn't handle non-finite values.
Results may differ from the reference program's by a relative error of at most 0.0028.
Values may be sent and summed in bfloat16 or wider, within the bound.
No kernel may reach another device: no remote copies, remote signals or barrier semaphores. Data moves between devices by JAX's collectives and lax.ppermute only.
A program may use at most 128 MiB of HBM per device.

```python
import jax
import jax.numpy as jnp
from jax import lax

LAT = 128
P_SIZE = 256
RBF = 2
NBR = 8
MOVE = 1
OSLOTS = 8
SLOTS = 10
BLOCKS = 160
OBLOCKS = 128
NODES = 40960
ONODES = 32768
N_SLAB = 4
N_SUB = 4


def shuffled_rows(key, row_count, length):
    row_keys = jax.random.split(key, row_count)
    return jax.vmap(lambda row_key: jax.random.permutation(row_key, length))(row_keys)


def migration_plan(key):
    device_total = N_SLAB * N_SUB
    key_right, key_left, key_out, key_in = jax.random.split(key, 4)
    device_ids = jnp.arange(device_total, dtype=jnp.int32)
    slab_of = device_ids // N_SUB
    to_right = jax.random.randint(key_right, (device_total,), 0, MOVE + 1)
    to_left = jax.random.randint(key_left, (device_total,), 0, MOVE + 1)
    to_right = jnp.where(slab_of == 0, MOVE, jnp.where(slab_of == N_SLAB - 1, 0, to_right))
    to_left = jnp.where(slab_of == N_SLAB - 1, MOVE, jnp.where(slab_of == 0, 0, to_left))
    below = jnp.clip(device_ids - N_SUB, 0, device_total - 1)
    above = jnp.clip(device_ids + N_SUB, 0, device_total - 1)
    from_left = jnp.where(slab_of > 0, to_right[below], 0)
    from_right = jnp.where(slab_of < N_SLAB - 1, to_left[above], 0)
    staying = OSLOTS - from_left - from_right
    out_order = shuffled_rows(key_out, device_total, OSLOTS)
    item = jnp.arange(SLOTS, dtype=jnp.int32)[None, :]
    stay_end = staying[:, None]
    left_end = (staying + to_left)[:, None]
    right_end = (staying + to_left + to_right)[:, None]

    def lookup(device_pick, position):
        chosen = jnp.take_along_axis(out_order[device_pick], jnp.clip(position, 0, OSLOTS - 1), axis=1)
        return chosen + device_pick[:, None] * OSLOTS
    stay_target = lookup(device_ids, (from_left + from_right)[:, None] + item)
    left_target = lookup(below, from_left[below][:, None] + item - stay_end)
    right_target = lookup(above, item - left_end)
    items = jnp.where(item < stay_end, stay_target, jnp.where(item < left_end, left_target, jnp.where(item < right_end, right_target, -1)))
    in_order = shuffled_rows(key_in, device_total, SLOTS)
    placed = jnp.zeros((device_total, SLOTS), jnp.int32).at[device_ids[:, None], in_order].set(items.astype(jnp.int32))
    return placed


def draw_positions(key, part):
    key = jax.random.fold_in(key, 11)
    coords = jax.random.uniform(key, (3, NODES), jnp.float32, -2.5, 2.5)
    return coords.astype(jnp.bfloat16)


def draw_target(key, part):
    return migration_plan(key).reshape(BLOCKS).astype(jnp.int32)


def draw_neighbours(key, part):
    plan = migration_plan(key)
    key = jax.random.fold_in(key, 7)
    key_step, key_sub, key_rank = jax.random.split(key, 3)
    device_total = N_SLAB * N_SUB
    is_live = plan >= 0
    live_count = jnp.sum(is_live.astype(jnp.int32), axis=1)
    live_order = jnp.argsort((~is_live).astype(jnp.int32), axis=1, stable=True).astype(jnp.int32)
    device_ids = jnp.arange(device_total, dtype=jnp.int32)[:, None, None]
    slot_ids = jnp.arange(SLOTS, dtype=jnp.int32)[None, :, None]
    shape_all = (device_total, SLOTS, NBR)
    steps_drawn = jax.random.randint(key_step, shape_all, -1, 2)
    near_slab = jnp.clip(device_ids // N_SUB + steps_drawn, 0, N_SLAB - 1)
    near_device = near_slab * N_SUB + jax.random.randint(key_sub, shape_all, 0, N_SUB)
    near_count = live_count[near_device]
    ranks = jax.random.randint(key_rank, shape_all, 0, jnp.maximum(near_count, 1))
    near_slot = jnp.take_along_axis(live_order[near_device], ranks[..., None], axis=3)[..., 0]
    own_ids = device_ids * SLOTS + slot_ids
    result = jnp.where(near_count > 0, near_device * SLOTS + near_slot, own_ids + 0 * near_slot)
    return result.reshape(BLOCKS, NBR).astype(jnp.int32)


def block_levels(key, dims, cuts, low, top_value):
    def one(dim, parts):
        steps = jax.random.uniform(jax.random.fold_in(jax.random.fold_in(key, 6), dim), (parts,), jnp.float32, low / len(cuts), top_value / len(cuts))
        return jnp.repeat(jnp.exp(steps), dims[dim] // parts).reshape((-1,) + (1,) * (len(dims) - dim - 1))

    gain = one(*cuts[0])
    for cut in cuts[1:]:
        gain = gain * one(*cut)
    return gain


def noise(rng, extent, spread, limit, cuts=(), kind=jnp.bfloat16):
    values = spread * jax.random.normal(rng, extent, jnp.float32)
    if cuts:
        values = values * block_levels(rng, extent, cuts, -0.22, 0.18)
    return jnp.clip(values, -limit, limit).astype(kind)


def setup_inputs(seed: int = 0, part: int = 0) -> dict:
    streams_of = jax.random.split(jax.random.key(seed), 8)
    own_keys = jax.random.split(jax.random.fold_in(streams_of[7], part), 8)
    return {
        "latent": noise(own_keys[0], (NODES, LAT), 1.0, 6.0, ((0, 16),)),
        "positions": draw_positions(jax.random.fold_in(jax.random.fold_in(streams_of[7], part), 71), part),
        "target": draw_target(jax.random.fold_in(jax.random.fold_in(streams_of[7], part), 71), part),
        "neighbours": draw_neighbours(jax.random.fold_in(jax.random.fold_in(streams_of[7], part), 71), part),
        "w_send": noise(streams_of[4], (LAT, RBF * LAT), LAT ** -0.5, 0.5),
        "w_in": noise(streams_of[5], (2 * LAT, LAT), (2 * LAT) ** -0.5, 0.375),
        "w_out": noise(streams_of[6], (LAT, LAT), LAT ** -0.5, 0.5),
    }


def block_message(own_pos, near_pos, near_send, lat_width, basis_count, msg_scale):
    dist_sq = jnp.zeros((near_pos.shape[0], own_pos.shape[1], near_pos.shape[2]), jnp.float32)
    for axis_id in range(3):
        offset = own_pos[axis_id][None, :, None] - near_pos[:, axis_id][:, None, :]
        dist_sq = dist_sq + offset * offset
    summed = jnp.zeros((own_pos.shape[1], lat_width), jnp.float32)
    for basis_id in range(basis_count):
        filter_bf = jnp.exp(-0.5 * 4.0 ** basis_id * dist_sq).astype(jnp.bfloat16)
        columns = near_send[:, :, basis_id * lat_width:(basis_id + 1) * lat_width]
        summed = summed + jnp.einsum("tij,tjc->ic", filter_bf.astype(jnp.float32), columns.astype(jnp.float32))
    return (summed * msg_scale).astype(jnp.bfloat16)


def reference(latent, positions, target, neighbours, w_send, w_in, w_out):
    projected = jnp.dot(latent, w_send, preferred_element_type=jnp.float32).astype(jnp.bfloat16)
    send_blocks = projected.reshape(BLOCKS, P_SIZE, RBF * LAT)
    pos_blocks = positions.astype(jnp.float32).reshape(3, BLOCKS, P_SIZE).transpose(1, 0, 2)
    tile_ids = jnp.concatenate([jnp.arange(BLOCKS, dtype=jnp.int32)[:, None], neighbours.astype(jnp.int32)], axis=1)
    msg_scale = (P_SIZE * (NBR + 1)) ** -0.5

    def per_block(block_data):
        ids_row, pos_row = block_data
        return block_message(pos_row, pos_blocks[ids_row], send_blocks[ids_row], LAT, RBF, msg_scale)

    messages = lax.map(per_block, (tile_ids, pos_blocks)).reshape(NODES, LAT)
    joined = jnp.concatenate([latent, messages], axis=1)
    hidden = jax.nn.silu(jnp.dot(joined, w_in, preferred_element_type=jnp.float32)).astype(jnp.bfloat16)
    updated = (latent.astype(jnp.float32) + jnp.dot(hidden, w_out, preferred_element_type=jnp.float32)).astype(jnp.bfloat16)
    slot_index = jnp.where(target < 0, OBLOCKS, target).astype(jnp.int32)
    placed = jnp.zeros((OBLOCKS, P_SIZE, LAT), jnp.bfloat16).at[slot_index].set(updated.reshape(BLOCKS, P_SIZE, LAT), mode="drop")
    return placed.reshape(ONODES, LAT)
```

```python
import functools

import jax
import jax.numpy as jnp
from jax import lax
from jax.experimental import pallas as pl
from jax.experimental.pallas import tpu as pltpu
from jax.sharding import PartitionSpec as P

OSLOTS = 8
MATES = 4
GROUP = 8
FEAT = 16
LOG2_SCALE = 0.7213475204444817
VMEM_LIMIT = 28 << 20
F32, BF16 = jnp.float32, jnp.bfloat16


def head_of(kept):
    return (3 * kept + 3 + 15) // 16 * 16


def mm(left, right, left_dim=1):
    dims = (((left_dim,), (0,)), ((), ()))
    return lax.dot_general(left, right, dims, preferred_element_type=F32)


def pieces(value):
    high = value.astype(BF16).astype(F32)
    rest = value - high
    middle = rest.astype(BF16).astype(F32)
    return high, middle, rest - middle


def put(terms, index, kept, value):
    for half in range(terms.shape[0]):
        terms[half, index * kept : index * kept + value.shape[0], :] = value[
            :, half * 128 : half * 128 + 128
        ]


def features(terms, index, kept):
    halves = [
        terms[half, pl.ds(index, FEAT, stride=kept), :].astype(BF16)
        for half in range(terms.shape[0])
    ]
    return jnp.concatenate(halves, axis=1)


def first_hole(target_ref, slots):
    hole = jnp.int32(slots - 1)
    for slot in reversed(range(slots)):
        hole = jnp.where(target_ref[slot] < 0, slot, hole)
    return hole


def slot_of(row, hole, kept, slots):
    return jnp.where(row == hole, slots - 1, row) if kept < slots else row


def call(kernel, name, out_shape, in_specs, out_specs, scratch, args, flops=0, limit=VMEM_LIMIT):
    return pl.pallas_call(
        kernel,
        name=name,
        out_shape=out_shape,
        in_specs=in_specs,
        out_specs=out_specs,
        scratch_shapes=scratch,
        compiler_params=pltpu.CompilerParams(vmem_limit_bytes=limit),
        cost_estimate=pl.CostEstimate(flops=flops, bytes_accessed=flops >> 9, transcendentals=0),
    )(*args)


VM = pl.BlockSpec(memory_space=pltpu.VMEM)
SM = pl.BlockSpec(memory_space=pltpu.SMEM)
HB = pl.BlockSpec(memory_space=pltpu.HBM)


def pack_kernel(kept, slots, rows, target_in, latent, positions, pay, target, coords, head, blocks, sems):
    get_target = pltpu.make_async_copy(target_in, target, sems.at[slots + 1])
    copies = [pltpu.make_async_copy(positions, coords, sems.at[slots])]
    for slot in range(slots):
        copies.append(
            pltpu.make_async_copy(
                latent.at[slot * rows : slot * rows + rows, :], blocks.at[slot], sems.at[slot]
            )
        )
    for copy in (get_target, *copies):
        copy.start()
    get_target.wait()
    hole = first_hole(target, slots)
    sub_count = lax.axis_size("sub")
    me = lax.axis_index("slab") * sub_count + lax.axis_index("sub")
    up_tag, down_tag = jnp.int32(0), jnp.int32(0)
    for slot in range(slots):
        out_slot = target[slot]
        owner = out_slot // OSLOTS
        up_tag = jnp.where(owner == me + sub_count, out_slot - owner * OSLOTS + 1, up_tag)
        down_tag = jnp.where(
            (out_slot >= 0) & (owner == me - sub_count), out_slot - owner * OSLOTS + 1, down_tag
        )
    head[...] = jnp.zeros_like(head)
    for offset, tag in enumerate((hole, up_tag, down_tag)):
        head[pl.ds(3 * kept + offset, 1), :] = jnp.full((1, rows), tag.astype(F32))
    copies[0].wait()
    for row in range(kept):
        start = pl.multiple_of(slot_of(row, hole, kept, slots) * rows, rows)
        block = coords[:, pl.ds(start, rows)].astype(F32)
        for axis in range(3):
            head[pl.ds(axis * kept + row, 1), :] = block[axis : axis + 1, :]
    pay[0:head_of(kept), :] = head[...].astype(BF16)
    lat = latent.shape[1]
    if kept < slots:
        copies[slots].wait()
    for row in range(kept):
        copies[1 + row].wait()
        block = blocks[slot_of(row, hole, kept, slots)]
        pay[head_of(kept) + row * lat : head_of(kept) + row * lat + lat, :] = jnp.transpose(block)


def plan_kernel(kept, slots, rows, homes, phases, target, near, pay, tiles, counts, query, terms):
    hole = first_hole(target, slots)
    sub_count, slab_count = lax.axis_size("sub"), lax.axis_size("slab")
    my_slab, my_sub = lax.axis_index("slab"), lax.axis_index("sub")
    limit = slab_count * sub_count * slots
    inverse = 65536 // slots + 1
    if any(i * inverse >> 16 != i // slots for i in range(limit)):
        raise ValueError("slot ids")
    words = [sum(home << (6 * i) for i, home in enumerate(homes[at : at + 4])) for at in (0, 4, 8)]
    for phase in range(phases):
        counts[phase] = 0

    def add(phase, entry):
        place = counts[phase]
        tiles[phase, place] = entry
        counts[phase] = place + 1

    me = my_slab * sub_count + my_sub

    def per_row(row, carry):
        slot = slot_of(row, hole, kept, slots)
        stays = lax.shift_right_arithmetic(target[slot], OSLOTS.bit_length() - 1) == me
        end = jnp.where(stays, phases - 1, phases - 2)

        @pl.when(target[slot] >= 0)
        def _():
            add(homes[MATES] // 8, row * 256 + homes[MATES] % 8 * 16 + slot)
            for k in range(near.shape[1]):
                other = near[slot, k]
                device = lax.shift_right_logical(other * inverse, 16)
                step = device // sub_count - my_slab
                word = jnp.where(step < 0, words[0], jnp.where(step == 0, words[1], words[2]))
                home = lax.shift_right_logical(word, 6 * jnp.bitwise_xor(device % sub_count, my_sub))
                phase = jnp.bitwise_and(lax.shift_right_logical(home, 3), 7)
                phase = jnp.where(phase == phases - 2, end, phase)
                line = jnp.bitwise_and(home, 7)
                add(phase, row * 256 + line * 16 + other - device * slots)

        return carry

    lax.fori_loop(0, kept, per_row, 0)
    for phase in range(phases):
        for extra in range(GROUP):
            tiles[phase, counts[phase] + extra] = kept * 256

    total = jnp.zeros((kept, rows), F32)
    head = pay[0:head_of(kept), :].astype(F32)
    for axis in range(3):
        coord = head[axis * kept : axis * kept + kept, :]
        total = total + coord * coord
        for part, value in enumerate(pieces(coord * (2 * LOG2_SCALE))):
            put(terms, part * 3 + axis, kept, value)
    put(terms, 9, kept, jnp.ones((3 * kept, rows), F32))
    for part, value in enumerate(pieces(total * -LOG2_SCALE)):
        put(terms, 12 + part, kept, value)
    put(terms, 15, kept, jnp.zeros((kept, rows), F32))
    for row in range(kept):
        query[row] = features(terms, row, kept)


def gather_tiles(kept, slots, rows, lat, phase, tiles, counts, query, lines, acc, scratch):
    land, feats, terms, holes, sems = scratch
    copies = [
        pltpu.make_async_copy(ref, land.at[line], sems.at[line]) for line, ref in enumerate(lines)
    ]
    for copy in copies:
        copy.start()
    put(terms, 12, kept, jnp.ones((3 * kept, rows), F32))
    put(terms, 15, kept, jnp.zeros((kept, rows), F32))
    for line, ref in enumerate(lines):
        head = ref[0:head_of(kept), :].astype(F32)
        holes[line] = jnp.max(head[3 * kept : 3 * kept + 1, :]).astype(jnp.int32)
        total = jnp.zeros((kept, rows), F32)
        for axis in range(3):
            coord = head[axis * kept : axis * kept + kept, :]
            total = total + coord * coord
            for part in range(3):
                put(terms, part * 3 + axis, kept, coord)
        for part, value in enumerate(pieces(total * -LOG2_SCALE)):
            put(terms, 9 + part, kept, value)
        for block in range(kept):
            feats[line * kept + block] = features(terms, block, kept)
    for copy in copies:
        copy.wait()

    def per_group(group, carry):
        owns, exponents, sources = [], [], []
        for step in range(GROUP):
            entry = tiles[phase, group * GROUP + step]
            own = lax.shift_right_logical(entry, 8)
            line = jnp.bitwise_and(lax.shift_right_logical(entry, 4), 15)
            slot = jnp.bitwise_and(entry, 15)
            block = jnp.where(slot == kept, holes[line], slot) if kept < slots else slot
            owns.append(own)
            begin = pl.multiple_of(head_of(kept) + block * lat, 16)
            sources.append(land[line, pl.ds(begin, lat), :])
            exponents.append(
                mm(feats[line * kept + block], query[jnp.minimum(own, kept - 1)], left_dim=0)
            )
        results = []
        for exponent, source in zip(exponents, sources):
            wide = jnp.exp2(exponent)
            square = wide * wide
            results.append(
                (mm(source, wide.astype(BF16)), mm(source, (square * square).astype(BF16)))
            )
        for own, (first, second) in zip(owns, results):
            acc[own, 0:lat] += first
            acc[own, lat : 2 * lat] += second
        return carry

    lax.fori_loop(0, (counts[phase] + GROUP - 1) // GROUP, per_group, 0)


def tiles_kernel(kept, slots, rows, lat, phase, line_count, has_earlier, tiles, counts, query, *rest):
    earlier, rest = (rest[0], rest[1:]) if has_earlier else (None, rest)
    lines, rest = rest[:line_count], rest[line_count:]
    acc, *scratch = rest
    if has_earlier:
        acc[...] = earlier[...]
    else:
        acc[...] = jnp.zeros_like(acc)
    gather_tiles(kept, slots, rows, lat, phase, tiles, counts, query, lines, acc, scratch)


def update(lat, scale, w_send, w_in, w_out):
    send = jnp.concatenate([w_send[:, 0:lat], w_send[:, lat : 2 * lat]], axis=0)
    send = jnp.transpose(send.astype(F32)).astype(BF16)
    first = jnp.transpose(w_in[...].astype(F32)).astype(BF16)
    second = jnp.transpose(w_out[...].astype(F32)).astype(BF16)

    def of(latent, sums):
        message = (mm(send, sums.astype(BF16)) * scale).astype(BF16)
        before = mm(first, jnp.concatenate([latent, message], axis=0))
        hidden = (before / (1.0 + jnp.exp(-before))).astype(BF16)
        result = latent.astype(F32) + mm(second, hidden)
        return jnp.transpose(result).astype(BF16)

    return of


def owner_of(out_slot):
    return lax.shift_right_arithmetic(out_slot, OSLOTS.bit_length() - 1)


def moving_kernel(
    kept, slots, rows, lat, phase, line_count, scale, target, tiles, counts, query, w_send,
    w_in, w_out, pay, earlier, *rest,
):
    lines, rest = rest[:line_count], rest[line_count:]
    moving_up, moving_down, acc, *scratch = rest
    hole = first_hole(target, slots)
    me = lax.axis_index("slab") * lax.axis_size("sub") + lax.axis_index("sub")
    up_row, down_row = jnp.int32(0), jnp.int32(0)
    for row in range(kept):
        out_slot = target[slot_of(row, hole, kept, slots)]
        owner = owner_of(out_slot)
        up_row = jnp.where(owner > me, row, up_row)
        down_row = jnp.where((out_slot >= 0) & (owner < me), row, down_row)
    for row in (up_row, down_row):
        acc[row] = earlier[row]
    gather_tiles(kept, slots, rows, lat, phase, tiles, counts, query, lines, acc, scratch)
    of = update(lat, scale, w_send, w_in, w_out)
    for row, out in ((up_row, moving_up), (down_row, moving_down)):
        start = pl.multiple_of(head_of(kept) + row * lat, 16)
        out[...] = of(pay[pl.ds(start, lat), :], acc[row])


def staying_kernel(
    kept, slots, rows, lat, phase, line_count, scale, target, tiles, counts, query, w_send,
    w_in, w_out, pay, earlier, *rest,
):
    lines, rest = rest[:line_count], rest[line_count:]
    staying, acc, updated, outs, *scratch = rest
    acc[...] = earlier[...]
    gather_tiles(kept, slots, rows, lat, phase, tiles, counts, query, lines, acc, scratch)
    hole = first_hole(target, slots)
    me = lax.axis_index("slab") * lax.axis_size("sub") + lax.axis_index("sub")
    of = update(lat, scale, w_send, w_in, w_out)
    for row in range(kept):
        updated[row] = of(pay[head_of(kept) + row * lat : head_of(kept) + row * lat + lat, :], acc[row])
    sends = []
    for row in range(kept):
        out_slot = target[slot_of(row, hole, kept, slots)]
        stays = owner_of(out_slot) == me
        start = pl.multiple_of(jnp.where(stays, out_slot - me * OSLOTS, 0) * rows, rows)
        copy = pltpu.make_async_copy(
            updated.at[row], staying.at[pl.ds(start, rows), :], outs.at[row]
        )
        sends.append((stays, copy))
    for goes, copy in sends:
        pl.when(goes)(copy.start)
    for goes, copy in sends:
        pl.when(goes)(copy.wait)


def place_kernel(kept, rows, below_head, above_head, below, above, held, out, sems):
    arrived = []
    for index, (head, block) in enumerate(((below_head, below), (above_head, above))):
        at = 3 * kept + 1 + index
        tag = jnp.max(head[0 : head_of(kept), :].astype(F32)[at : at + 1, :]).astype(jnp.int32)
        start = pl.multiple_of(jnp.maximum(tag - 1, 0) * rows, rows)
        copy = pltpu.make_async_copy(block, out.at[pl.ds(start, rows), :], sems.at[index])
        arrived.append((tag > 0, copy))
    for is_there, copy in arrived:
        pl.when(is_there)(copy.start)
    for is_there, copy in arrived:
        pl.when(is_there)(copy.wait)


def on_device(latent, positions, target, neighbours, w_send, w_in, w_out):
    lat = latent.shape[1]
    slots = target.shape[0]
    rows = latent.shape[0] // slots
    near_count = neighbours.shape[1]
    slab_count = lax.axis_size("slab")
    kept = slots - 1 if slab_count <= 4 else slots
    length = head_of(kept) + kept * lat
    if lax.axis_size("sub") != MATES:
        raise ValueError("sizes")
    up = [(i, i + 1) for i in range(slab_count - 1)]
    down = [(j, i) for i, j in up]
    def mate_of(value, bit):
        return lax.ppermute(value, "sub", [(i, i ^ bit) for i in range(MATES)])

    def upward(value):
        return lax.ppermute(value, "slab", up)

    def downward(value):
        return lax.ppermute(value, "slab", down)

    pay = call(
        functools.partial(pack_kernel, kept, slots, rows),
        "pack",
        jax.ShapeDtypeStruct((length, rows), BF16),
        [HB, HB, HB],
        VM,
        [
            pltpu.SMEM((slots,), jnp.int32),
            pltpu.VMEM(positions.shape, BF16),
            pltpu.VMEM((head_of(kept), rows), F32),
            pltpu.VMEM((slots, rows, lat), BF16),
            pltpu.SemaphoreType.DMA((slots + 2,)),
        ],
        (target, latent, positions),
        limit=60 << 20,
    )
    across = mate_of(pay, 2)
    below_own, above_own = upward(pay), downward(pay)
    pair = mate_of(pay, 1)

    homes = (10, 16, 18, 24, 0, 1, 8, 9, 11, 17, 19, 25)
    phase_count = 5
    most = kept * (near_count + 1) + GROUP
    tiles, counts, query = call(
        functools.partial(plan_kernel, kept, slots, rows, homes, phase_count),
        "plan",
        (
            jax.ShapeDtypeStruct((phase_count, most), jnp.int32),
            jax.ShapeDtypeStruct((phase_count,), jnp.int32),
            jax.ShapeDtypeStruct((kept, FEAT, rows), BF16),
        ),
        [SM, SM, VM],
        (SM, SM, VM),
        [pltpu.VMEM((rows // 128, FEAT * kept, 128), F32)],
        (target, neighbours, pay),
    )

    def scratch_for(line_count):
        return [
            pltpu.VMEM((line_count, length, rows), BF16),
            pltpu.VMEM((line_count * kept, FEAT, rows), BF16),
            pltpu.VMEM((rows // 128, FEAT * kept, 128), F32),
            pltpu.SMEM((line_count,), jnp.int32),
            pltpu.SemaphoreType.DMA((line_count,)),
        ]

    sums = (kept + 1, 2 * lat, rows)

    def tiles_call(phase, lines, earlier):
        earlier = [] if earlier is None else [earlier]
        return call(
            functools.partial(
                tiles_kernel, kept, slots, rows, lat, phase, len(lines), bool(earlier)
            ),
            f"tiles{phase}",
            jax.ShapeDtypeStruct(sums, F32),
            [SM, SM, VM] + [VM] * (len(earlier) + len(lines)),
            VM,
            scratch_for(len(lines)),
            (tiles, counts, query, *earlier, *lines),
        )

    partial = tiles_call(0, [pay, pair], None)
    across, partial = lax.optimization_barrier((across, partial))
    below_far, above_far = upward(across), downward(across)
    across_pair = mate_of(across, 1)
    below_pair, above_pair = mate_of(below_own, 1), mate_of(above_own, 1)
    partial = tiles_call(1, [across, across_pair, below_own, above_own], partial)
    below_far, above_far, partial = lax.optimization_barrier((below_far, above_far, partial))
    below_last, above_last = mate_of(below_far, 1), mate_of(above_far, 1)
    partial = tiles_call(2, [below_pair, above_pair, below_far, above_far], partial)
    scale = (rows * (near_count + 1)) ** -0.5
    moving_up, moving_down = call(
        functools.partial(moving_kernel, kept, slots, rows, lat, 3, 2, scale),
        "moving",
        (jax.ShapeDtypeStruct((rows, lat), BF16), jax.ShapeDtypeStruct((rows, lat), BF16)),
        [SM, SM, SM] + [VM] * 8,
        (VM, VM),
        [pltpu.VMEM(sums, F32), *scratch_for(2)],
        (
            target, tiles, counts, query, w_send, w_in, w_out, pay, partial, below_last,
            above_last,
        ),
    )
    partial, moving_up, moving_down = lax.optimization_barrier((partial, moving_up, moving_down))
    below = upward(moving_up)
    above = downward(moving_down)
    staying = call(
        functools.partial(staying_kernel, kept, slots, rows, lat, 4, 2, scale),
        "staying",
        jax.ShapeDtypeStruct((OSLOTS * rows, lat), BF16),
        [SM, SM, SM] + [VM] * 8,
        HB,
        [pltpu.VMEM(sums, F32), pltpu.VMEM((kept, rows, lat), BF16),
         pltpu.SemaphoreType.DMA((kept,)), *scratch_for(2)],
        (
            target, tiles, counts, query, w_send, w_in, w_out, pay, partial, below_last,
            above_last,
        ),
    )
    return pl.pallas_call(
        functools.partial(place_kernel, kept, rows),
        name="place",
        out_shape=jax.ShapeDtypeStruct((OSLOTS * rows, lat), BF16),
        in_specs=[VM, VM, VM, VM, HB],
        out_specs=HB,
        scratch_shapes=[pltpu.SemaphoreType.DMA((2,))],
        input_output_aliases={4: 0},
        compiler_params=pltpu.CompilerParams(vmem_limit_bytes=VMEM_LIMIT),
    )(below_own, above_own, below, above, staying)


def solution(mesh):
    placed = (
        P(("grp", "slab", "sub"), None),
        P(None, ("grp", "slab", "sub")),
        P(("grp", "slab", "sub")),
        P(("grp", "slab", "sub"), None),
        P(),
        P(),
        P(),
    )
    return jax.shard_map(
        on_device,
        mesh=mesh,
        in_specs=placed,
        out_specs=P(("grp", "slab", "sub"), None),
        check_vma=False,
    )
```

```python
import functools

import jax
import jax.numpy as jnp
from jax import lax
from jax.experimental import pallas as pl
from jax.experimental.pallas import tpu as pltpu
from jax.sharding import PartitionSpec as P

OSLOTS = 8
MATES = 4
GROUPS = (16, 8, 4)
MOVING_GROUPS = (8, 4)
REST = 2
FEAT = 16
LOG2_SCALE = 0.7213475204444817
VMEM_LIMIT = 28 << 20
F32, BF16 = jnp.float32, jnp.bfloat16


def head_of(kept):
    return (3 * kept + 3 + 15) // 16 * 16


def mm(left, right, left_dim=1):
    dims = (((left_dim,), (0,)), ((), ()))
    return lax.dot_general(left, right, dims, preferred_element_type=F32)


def pieces(value):
    high = value.astype(BF16).astype(F32)
    rest = value - high
    middle = rest.astype(BF16).astype(F32)
    return high, middle, rest - middle


def put(terms, index, kept, value):
    for half in range(terms.shape[0]):
        terms[half, index * kept : index * kept + value.shape[0], :] = value[
            :, half * 128 : half * 128 + 128
        ]


def features(terms, index, kept):
    halves = [
        terms[half, pl.ds(index, FEAT, stride=kept), :].astype(BF16)
        for half in range(terms.shape[0])
    ]
    return jnp.concatenate(halves, axis=1)


def first_hole(target_ref, slots):
    hole = jnp.int32(slots - 1)
    for slot in reversed(range(slots)):
        hole = jnp.where(target_ref[slot] < 0, slot, hole)
    return hole


def slot_of(row, hole, kept, slots):
    return jnp.where(row == hole, slots - 1, row) if kept < slots else row


def call(kernel, name, out_shape, in_specs, out_specs, scratch, args, flops=0, limit=VMEM_LIMIT):
    return pl.pallas_call(
        kernel,
        name=name,
        out_shape=out_shape,
        in_specs=in_specs,
        out_specs=out_specs,
        scratch_shapes=scratch,
        compiler_params=pltpu.CompilerParams(vmem_limit_bytes=limit),
        cost_estimate=pl.CostEstimate(flops=flops, bytes_accessed=flops >> 9, transcendentals=0),
    )(*args)


VM = pl.BlockSpec(memory_space=pltpu.VMEM)
SM = pl.BlockSpec(memory_space=pltpu.SMEM)
HB = pl.BlockSpec(memory_space=pltpu.HBM)


def in_hbm(*arrays):
    return [pltpu.with_memory_space_constraint(array, pltpu.HBM) for array in arrays]


def pack_kernel(
    kept, slots, rows, target_in, latent, positions, pay, pay_first, pay_rest, target, coords, head,
    blocks, sems,
):
    get_target = pltpu.make_async_copy(target_in, target, sems.at[slots + 1])
    copies = [pltpu.make_async_copy(positions, coords, sems.at[slots])]
    for slot in range(slots):
        copies.append(
            pltpu.make_async_copy(
                latent.at[slot * rows : slot * rows + rows, :], blocks.at[slot], sems.at[slot]
            )
        )
    for copy in (get_target, *copies):
        copy.start()
    get_target.wait()
    hole = first_hole(target, slots)
    sub_count = lax.axis_size("sub")
    me = lax.axis_index("slab") * sub_count + lax.axis_index("sub")
    up_tag, down_tag = jnp.int32(0), jnp.int32(0)
    for slot in range(slots):
        out_slot = target[slot]
        owner = out_slot // OSLOTS
        up_tag = jnp.where(owner == me + sub_count, out_slot - owner * OSLOTS + 1, up_tag)
        down_tag = jnp.where(
            (out_slot >= 0) & (owner == me - sub_count), out_slot - owner * OSLOTS + 1, down_tag
        )
    head[...] = jnp.zeros_like(head)
    for offset, tag in enumerate((hole, up_tag, down_tag)):
        head[pl.ds(3 * kept + offset, 1), :] = jnp.full((1, rows), tag.astype(F32))
    copies[0].wait()
    for row in range(kept):
        start = pl.multiple_of(slot_of(row, hole, kept, slots) * rows, rows)
        block = coords[:, pl.ds(start, rows)].astype(F32)
        for axis in range(3):
            head[pl.ds(axis * kept + row, 1), :] = block[axis : axis + 1, :]
    pay[0:head_of(kept), :] = head[...].astype(BF16)
    pay_first[0:head_of(kept), :] = head[...].astype(BF16)
    lat = latent.shape[1]
    if kept < slots:
        copies[slots].wait()
    for row in range(kept):
        copies[1 + row].wait()
        block = blocks[slot_of(row, hole, kept, slots)]
        turned = jnp.transpose(block)
        start = head_of(kept) + row * lat
        pay[start : start + lat, :] = turned
        if row < kept - REST:
            pay_first[start : start + lat, :] = turned
        else:
            start = (row - kept + REST) * lat
            pay_rest[start : start + lat, :] = turned


def plan_kernel(
    kept, slots, rows, homes, phases, target_in, near_in, pay, w_send_in, w_in_in, tiles, counts,
    query, send_turned, in_turned, target, near, w_send, w_in, terms, sems,
):
    loads = [
        pltpu.make_async_copy(source, ref, sems.at[index])
        for index, (source, ref) in enumerate(
            ((target_in, target), (near_in, near), (w_send_in, w_send), (w_in_in, w_in))
        )
    ]
    for load in loads:
        load.start()
    total = jnp.zeros((kept, rows), F32)
    head = pay[0 : head_of(kept), :].astype(F32)
    for axis in range(3):
        coord = head[axis * kept : axis * kept + kept, :]
        total = total + coord * coord
        for part, value in enumerate(pieces(coord * (2 * LOG2_SCALE))):
            put(terms, part * 3 + axis, kept, value)
    put(terms, 9, kept, jnp.ones((3 * kept, rows), F32))
    for part, value in enumerate(pieces(total * -LOG2_SCALE)):
        put(terms, 12 + part, kept, value)
    put(terms, 15, kept, jnp.zeros((kept, rows), F32))
    for row in range(kept):
        query[row] = features(terms, row, kept)
    for load in loads:
        load.wait()
    lat = w_send.shape[0]
    send_turned[:, 0:lat] = jnp.transpose(w_send[:, 0:lat])
    send_turned[:, lat : 2 * lat] = jnp.transpose(w_send[:, lat : 2 * lat])
    in_turned[...] = jnp.transpose(w_in[...])
    hole = first_hole(target, slots)
    sub_count, slab_count = lax.axis_size("sub"), lax.axis_size("slab")
    my_slab, my_sub = lax.axis_index("slab"), lax.axis_index("sub")
    limit = slab_count * sub_count * slots
    inverse = 65536 // slots + 1
    if any(i * inverse >> 16 != i // slots for i in range(limit)):
        raise ValueError("slot ids")
    words = [sum(home << (6 * i) for i, home in enumerate(homes[at : at + 4])) for at in (0, 4, 8)]
    for phase in range(phases):
        counts[phase] = 0

    def add(phase, entry):
        place = counts[phase]
        tiles[phase, place] = entry
        counts[phase] = place + 1

    me = my_slab * sub_count + my_sub

    def per_row(row, carry):
        slot = slot_of(row, hole, kept, slots)
        stays = lax.shift_right_arithmetic(target[slot], OSLOTS.bit_length() - 1) == me
        end = jnp.where(stays, phases - 1, phases - 2)

        @pl.when(target[slot] >= 0)
        def _():
            add(homes[MATES] // 8, row * 256 + homes[MATES] % 8 * 16 + slot)
            for k in range(near.shape[0]):
                other = near[k, slot]
                device = lax.shift_right_logical(other * inverse, 16)
                step = device // sub_count - my_slab
                word = jnp.where(step < 0, words[0], jnp.where(step == 0, words[1], words[2]))
                home = lax.shift_right_logical(word, 6 * jnp.bitwise_xor(device % sub_count, my_sub))
                phase = jnp.bitwise_and(lax.shift_right_logical(home, 3), 7)
                phase = jnp.where(phase == phases - 2, end, phase)
                line = jnp.bitwise_and(home, 7)
                add(phase, row * 256 + line * 16 + other - device * slots)

        return carry

    lax.fori_loop(0, kept, per_row, 0)
    for phase in range(phases):
        for extra in range(GROUPS[0]):
            tiles[phase, counts[phase] + extra] = kept * 256


def gather_tiles(
    kept, slots, rows, lat, phase, tiles, counts, query, lines, acc, scratch, groups=GROUPS
):
    land, feats, terms, holes, sems = scratch
    copies = []
    for line, parts in enumerate(lines):
        at = 0
        for part, (ref, start, length) in enumerate(parts):
            copies.append(
                pltpu.make_async_copy(
                    ref.at[pl.ds(start, length), :],
                    land.at[line, pl.ds(at, length), :],
                    sems.at[line, part],
                )
            )
            at += length
    for copy in copies:
        copy.start()
    put(terms, 12, kept, jnp.ones((3 * kept, rows), F32))
    put(terms, 15, kept, jnp.zeros((kept, rows), F32))
    for line, parts in enumerate(lines):
        head = parts[0][0][0 : head_of(kept), :].astype(F32)
        holes[line] = jnp.max(head[3 * kept : 3 * kept + 1, :]).astype(jnp.int32)
        total = jnp.zeros((kept, rows), F32)
        for axis in range(3):
            coord = head[axis * kept : axis * kept + kept, :]
            total = total + coord * coord
            for part in range(3):
                put(terms, part * 3 + axis, kept, coord)
        for part, value in enumerate(pieces(total * -LOG2_SCALE)):
            put(terms, 9 + part, kept, value)
        for block in range(kept):
            feats[line * kept + block] = features(terms, block, kept)
    for copy in copies:
        copy.wait()

    def work(first, size):
        owns, exponents, sources = [], [], []
        for step in range(size):
            entry = tiles[phase, first + step]
            own = lax.shift_right_logical(entry, 8)
            line = jnp.bitwise_and(lax.shift_right_logical(entry, 4), 15)
            slot = jnp.bitwise_and(entry, 15)
            block = jnp.where(slot == kept, holes[line], slot) if kept < slots else slot
            owns.append(own)
            begin = pl.multiple_of(head_of(kept) + block * lat, 16)
            sources.append(land[line, pl.ds(begin, lat), :])
            exponents.append(
                mm(feats[line * kept + block], query[jnp.minimum(own, kept - 1)], left_dim=0)
            )
        results = []
        for exponent, source in zip(exponents, sources):
            wide = jnp.exp2(exponent)
            square = wide * wide
            results.append(
                (mm(source, wide.astype(BF16)), mm(source, (square * square).astype(BF16)))
            )
        for own, (first, second) in zip(owns, results):
            acc[own, 0:lat] += first
            acc[own, lat : 2 * lat] += second

    large, count = groups[0], counts[phase]
    small = groups[1] if len(groups) > 1 else 0
    whole = (count + large - 1 - small) // large
    lax.fori_loop(0, whole, lambda group, carry: work(group * large, large), None)
    left = count - whole * large
    for size, below in zip(groups[1:], (*groups[2:], 0)):
        pl.when((left > below) & (left <= size))(functools.partial(work, whole * large, size))


def lines_of(refs, parts):
    return [[(refs[index], start, length) for index, start, length in line] for line in parts]


def tiles_kernel(kept, slots, rows, lat, phase, parts, ref_count, has_earlier, tiles, counts, query, *rest):
    earlier, rest = (rest[0], rest[1:]) if has_earlier else (None, rest)
    lines, (acc, *scratch) = lines_of(rest, parts), rest[ref_count:]
    if has_earlier:
        acc[...] = earlier[...]
    else:
        acc[...] = jnp.zeros_like(acc)
    gather_tiles(kept, slots, rows, lat, phase, tiles, counts, query, lines, acc, scratch)


def update(lat, scale, send_turned, in_turned, w_out, old, turned, sums, joined, hidden, out):
    for row, (latent, total) in enumerate(zip(turned, sums)):
        message = mm(send_turned[...], total().astype(BF16)) * scale
        joined[row, 0:lat, :] = latent()
        joined[row, lat : 2 * lat, :] = message.astype(BF16)
    for row in range(len(sums)):
        before = mm(in_turned[...], joined[row])
        hidden[row] = (before / (1.0 + jnp.exp(-before))).astype(BF16)
    for row in range(len(sums)):
        change = mm(hidden[row], w_out[...], left_dim=0)
        out(row, (old[row].astype(F32) + change).astype(BF16))


def owner_of(out_slot):
    return lax.shift_right_arithmetic(out_slot, OSLOTS.bit_length() - 1)


def moving_kernel(
    kept, slots, rows, lat, phase, parts, ref_count, scale, target, tiles, counts, query,
    send_turned, in_turned, w_out, latents, pay, earlier, *rest,
):
    lines, rest = lines_of(rest, parts), rest[ref_count:]
    moving_up, moving_down, acc, old, joined, hidden, loads, *scratch = rest
    hole = first_hole(target, slots)
    me = lax.axis_index("slab") * lax.axis_size("sub") + lax.axis_index("sub")
    up_row, down_row = jnp.int32(0), jnp.int32(0)
    for row in range(kept):
        out_slot = target[slot_of(row, hole, kept, slots)]
        owner = owner_of(out_slot)
        up_row = jnp.where(owner > me, row, up_row)
        down_row = jnp.where((out_slot >= 0) & (owner < me), row, down_row)
    moved = (up_row, down_row)
    copies = []
    for index, row in enumerate(moved):
        start = pl.multiple_of(slot_of(row, hole, kept, slots) * rows, rows)
        copies.append(
            pltpu.make_async_copy(latents.at[pl.ds(start, rows), :], old.at[index], loads.at[index])
        )
    for copy in copies:
        copy.start()
    for row in moved:
        acc[row] = earlier[row]
    gather_tiles(
        kept, slots, rows, lat, phase, tiles, counts, query, lines, acc, scratch, MOVING_GROUPS
    )
    for copy in copies:
        copy.wait()

    def turned_of(row):
        return lambda: pay[pl.ds(pl.multiple_of(head_of(kept) + row * lat, 16), lat), :]

    def out(index, value):
        (moving_up, moving_down)[index][...] = value

    update(
        lat, scale, send_turned, in_turned, w_out, old, [turned_of(row) for row in moved],
        [lambda row=row: acc[row] for row in moved], joined, hidden, out,
    )


def staying_kernel(
    kept, slots, rows, lat, phase, parts, ref_count, scale, target, tiles, counts, query,
    send_turned, in_turned, w_out, latents, pay, earlier, *rest,
):
    lines, rest = lines_of(rest, parts), rest[ref_count:]
    updated, acc, old, joined, hidden, loads, *scratch = rest
    hole = first_hole(target, slots)
    copies = []
    for row in range(kept):
        start = pl.multiple_of(slot_of(row, hole, kept, slots) * rows, rows)
        copies.append(
            pltpu.make_async_copy(latents.at[pl.ds(start, rows), :], old.at[row], loads.at[row])
        )
    for copy in copies:
        copy.start()
    acc[...] = earlier[...]
    gather_tiles(kept, slots, rows, lat, phase, tiles, counts, query, lines, acc, scratch)
    for copy in copies:
        copy.wait()

    def turned_of(row):
        start = head_of(kept) + row * lat
        return lambda: pay[start : start + lat, :]

    def out(row, value):
        updated[row] = value

    update(
        lat, scale, send_turned, in_turned, w_out, old, [turned_of(row) for row in range(kept)],
        [lambda row=row: acc[row] for row in range(kept)], joined, hidden, out,
    )


def place_kernel(
    kept, slots, rows, target, below_head, above_head, below, above, updated, out, sems
):
    hole = first_hole(target, slots)
    me = lax.axis_index("slab") * lax.axis_size("sub") + lax.axis_index("sub")
    copies = []
    for row in range(kept):
        out_slot = target[slot_of(row, hole, kept, slots)]
        stays = owner_of(out_slot) == me
        start = pl.multiple_of(jnp.where(stays, out_slot - me * OSLOTS, 0) * rows, rows)
        copies.append(
            (
                stays,
                pltpu.make_async_copy(
                    updated.at[row], out.at[pl.ds(start, rows), :], sems.at[row]
                ),
            )
        )
    for index, (head, block) in enumerate(((below_head, below), (above_head, above))):
        at = 3 * kept + 1 + index
        tag = jnp.max(head[0 : head_of(kept), :].astype(F32)[at : at + 1, :]).astype(jnp.int32)
        start = pl.multiple_of(jnp.maximum(tag - 1, 0) * rows, rows)
        copies.append(
            (
                tag > 0,
                pltpu.make_async_copy(block, out.at[pl.ds(start, rows), :], sems.at[kept + index]),
            )
        )
    for goes, copy in copies:
        pl.when(goes)(copy.start)
    for goes, copy in copies:
        pl.when(goes)(copy.wait)


def on_device(latent, positions, target, neighbours, w_send, w_in, w_out):
    lat = latent.shape[1]
    slots = target.shape[0]
    rows = latent.shape[0] // slots
    near_count = neighbours.shape[1]
    slab_count = lax.axis_size("slab")
    kept = slots - 1 if slab_count <= 4 else slots
    length = head_of(kept) + kept * lat
    if lax.axis_size("sub") != MATES:
        raise ValueError("sizes")
    up = [(i, i + 1) for i in range(slab_count - 1)]
    down = [(j, i) for i, j in up]
    def mate_of(value, bit):
        return lax.ppermute(value, "sub", [(i, i ^ bit) for i in range(MATES)])

    def upward(value):
        return lax.ppermute(value, "slab", up)

    def downward(value):
        return lax.ppermute(value, "slab", down)

    cut = length - REST * lat
    pay, pay_first, pay_rest = call(
        functools.partial(pack_kernel, kept, slots, rows),
        "pack",
        (
            jax.ShapeDtypeStruct((length, rows), BF16),
            jax.ShapeDtypeStruct((cut, rows), BF16),
            jax.ShapeDtypeStruct((length - cut, rows), BF16),
        ),
        [HB, HB, HB],
        (VM, VM, VM),
        [
            pltpu.SMEM((slots,), jnp.int32),
            pltpu.VMEM(positions.shape, BF16),
            pltpu.VMEM((head_of(kept), rows), F32),
            pltpu.VMEM((slots, rows, lat), BF16),
            pltpu.SemaphoreType.DMA((slots + 2,)),
        ],
        in_hbm(target, latent, positions),
    )
    across, across_rest = mate_of(pay_first, 2), mate_of(pay_rest, 2)
    below_own, above_own = upward(pay), downward(pay)
    pair = mate_of(pay, 1)

    homes = (10, 16, 18, 24, 0, 1, 8, 9, 11, 17, 19, 25)
    phase_count = 5
    most = kept * (near_count + 1) + GROUPS[0]
    tiles, counts, query, send_turned, in_turned = call(
        functools.partial(plan_kernel, kept, slots, rows, homes, phase_count),
        "plan",
        (
            jax.ShapeDtypeStruct((phase_count, most), jnp.int32),
            jax.ShapeDtypeStruct((phase_count,), jnp.int32),
            jax.ShapeDtypeStruct((kept, FEAT, rows), BF16),
            jax.ShapeDtypeStruct((lat, 2 * lat), BF16),
            jax.ShapeDtypeStruct((lat, 2 * lat), BF16),
        ),
        [HB, HB, VM, HB, HB],
        (SM, SM, VM, VM, VM),
        [
            pltpu.SMEM((slots,), jnp.int32),
            pltpu.SMEM((near_count, slots), jnp.int32),
            pltpu.VMEM(w_send.shape, BF16),
            pltpu.VMEM(w_in.shape, BF16),
            pltpu.VMEM((rows // 128, FEAT * kept, 128), F32),
            pltpu.SemaphoreType.DMA((4,)),
        ],
        (*in_hbm(target, neighbours.T), pay, *in_hbm(w_send, w_in)),
    )

    def scratch_for(parts):
        return [
            pltpu.VMEM((len(parts), length, rows), BF16),
            pltpu.VMEM((len(parts) * kept, FEAT, rows), BF16),
            pltpu.VMEM((rows // 128, FEAT * kept, 128), F32),
            pltpu.SMEM((len(parts),), jnp.int32),
            pltpu.SemaphoreType.DMA((len(parts), 2)),
        ]

    sums = (kept + 1, 2 * lat, rows)
    whole = lambda index: ((index, 0, length),)
    split = lambda index, other, start=0: ((index, 0, cut), (other, start, length - cut))

    def tiles_call(phase, parts, refs, earlier):
        earlier = [] if earlier is None else [earlier]
        return call(
            functools.partial(
                tiles_kernel, kept, slots, rows, lat, phase, parts, len(refs), bool(earlier)
            ),
            f"tiles{phase}",
            jax.ShapeDtypeStruct(sums, F32),
            [SM, SM, VM] + [VM] * (len(earlier) + len(refs)),
            VM,
            scratch_for(parts),
            (tiles, counts, query, *earlier, *refs),
        )

    partial = tiles_call(0, (whole(0), whole(1)), [pay, pair], None)
    across, partial = lax.optimization_barrier((across, partial))
    below_far, above_far = upward(across), downward(across)
    across_pair, across_rest_pair = mate_of(across, 1), mate_of(across_rest, 1)
    far_rest = mate_of(jnp.concatenate([below_own[cut:], above_own[cut:]], axis=0), 2)
    below_pair, above_pair = mate_of(below_own, 1), mate_of(above_own, 1)
    partial = tiles_call(
        1,
        (split(0, 1), split(2, 3), whole(4), whole(5)),
        [across, across_rest, across_pair, across_rest_pair, below_own, above_own],
        partial,
    )
    below_far, above_far, partial = lax.optimization_barrier((below_far, above_far, partial))
    below_last, above_last = mate_of(below_far, 1), mate_of(above_far, 1)
    far_rest, below_far = lax.optimization_barrier((far_rest, below_far))
    last_rest = mate_of(far_rest, 1)
    partial = tiles_call(
        2,
        (whole(0), whole(1), split(2, 4), split(3, 4, length - cut)),
        [below_pair, above_pair, below_far, above_far, far_rest],
        partial,
    )
    scale = (rows * (near_count + 1)) ** -0.5
    last = (split(0, 2), split(1, 2, length - cut))
    last_args = (
        target, tiles, counts, query, send_turned, in_turned, w_out, latent, pay, partial,
        below_last, above_last, last_rest,
    )
    last_specs = [SM, SM, SM, VM, VM, VM, VM, HB, VM, VM, VM, VM, VM]

    def update_scratch(count):
        return [
            pltpu.VMEM(sums, F32),
            pltpu.VMEM((count, rows, lat), BF16),
            pltpu.VMEM((count, 2 * lat, rows), BF16),
            pltpu.VMEM((count, lat, rows), BF16),
            pltpu.SemaphoreType.DMA((count,)),
            *scratch_for(last),
        ]

    moving_up, moving_down = call(
        functools.partial(moving_kernel, kept, slots, rows, lat, 3, last, 3, scale),
        "moving",
        (jax.ShapeDtypeStruct((rows, lat), BF16), jax.ShapeDtypeStruct((rows, lat), BF16)),
        last_specs,
        (VM, VM),
        update_scratch(2),
        last_args,
    )
    partial, moving_up, moving_down = lax.optimization_barrier((partial, moving_up, moving_down))
    below, above = upward(moving_up), downward(moving_down)
    updated = call(
        functools.partial(staying_kernel, kept, slots, rows, lat, 4, last, 3, scale),
        "staying",
        jax.ShapeDtypeStruct((kept, rows, lat), BF16),
        last_specs,
        VM,
        update_scratch(kept),
        (*last_args[:9], partial, *last_args[10:]),
    )
    return call(
        functools.partial(place_kernel, kept, slots, rows),
        "place",
        jax.ShapeDtypeStruct((OSLOTS * rows, lat), BF16),
        [SM, VM, VM, VM, VM, VM],
        HB,
        [pltpu.SemaphoreType.DMA((kept + 2,))],
        (target, below_own, above_own, below, above, updated),
    )


def solution(mesh):
    placed = (
        P(("grp", "slab", "sub"), None),
        P(None, ("grp", "slab", "sub")),
        P(("grp", "slab", "sub")),
        P(("grp", "slab", "sub"), None),
        P(),
        P(),
        P(),
    )
    return jax.shard_map(
        on_device,
        mesh=mesh,
        in_specs=placed,
        out_specs=P(("grp", "slab", "sub"), None),
        check_vma=False,
    )
```

```python
import functools

import jax
import jax.numpy as jnp
from jax import lax
from jax.experimental import pallas as pl
from jax.experimental.pallas import tpu as pltpu
from jax.sharding import PartitionSpec as P

OSLOTS = 8
MATES = 4
GROUPS = (16, 8, 4)
MOVING_GROUPS = (8, 4)
REST_UP, REST = 3, 2
FEAT = 16
LOG2_SCALE = 0.7213475204444817
VMEM_LIMIT = 28 << 20
F32, BF16 = jnp.float32, jnp.bfloat16


def head_of(kept):
    return (3 * kept + 3 + 15) // 16 * 16


def mm(left, right, left_dim=1):
    dims = (((left_dim,), (0,)), ((), ()))
    return lax.dot_general(left, right, dims, preferred_element_type=F32)


def pieces(value):
    high = value.astype(BF16).astype(F32)
    rest = value - high
    middle = rest.astype(BF16).astype(F32)
    return high, middle, rest - middle


def put(terms, index, kept, value):
    for half in range(terms.shape[0]):
        terms[half, index * kept : index * kept + value.shape[0], :] = value[
            :, half * 128 : half * 128 + 128
        ]


def features(terms, index, kept):
    halves = [
        terms[half, pl.ds(index, FEAT, stride=kept), :].astype(BF16)
        for half in range(terms.shape[0])
    ]
    return jnp.concatenate(halves, axis=1)


def first_hole(target_ref, slots):
    hole = jnp.int32(slots - 1)
    for slot in reversed(range(slots)):
        hole = jnp.where(target_ref[slot] < 0, slot, hole)
    return hole


def slot_of(row, hole, kept, slots):
    return jnp.where(row == hole, slots - 1, row) if kept < slots else row


def call(kernel, name, out_shape, in_specs, out_specs, scratch, args, flops=0, limit=VMEM_LIMIT):
    return pl.pallas_call(
        kernel,
        name=name,
        out_shape=out_shape,
        in_specs=in_specs,
        out_specs=out_specs,
        scratch_shapes=scratch,
        compiler_params=pltpu.CompilerParams(vmem_limit_bytes=limit),
        cost_estimate=pl.CostEstimate(flops=flops, bytes_accessed=flops >> 9, transcendentals=0),
    )(*args)


VM = pl.BlockSpec(memory_space=pltpu.VMEM)
SM = pl.BlockSpec(memory_space=pltpu.SMEM)
HB = pl.BlockSpec(memory_space=pltpu.HBM)


def in_hbm(*arrays):
    return [pltpu.with_memory_space_constraint(array, pltpu.HBM) for array in arrays]


def pack_kernel(
    kept, slots, rows, target_in, latent, positions, pay, target, coords, head, blocks, sems,
):
    get_target = pltpu.make_async_copy(target_in, target, sems.at[slots + 1])
    copies = [pltpu.make_async_copy(positions, coords, sems.at[slots])]
    for slot in range(slots):
        copies.append(
            pltpu.make_async_copy(
                latent.at[slot * rows : slot * rows + rows, :], blocks.at[slot], sems.at[slot]
            )
        )
    for copy in (get_target, *copies):
        copy.start()
    get_target.wait()
    hole = first_hole(target, slots)
    sub_count = lax.axis_size("sub")
    me = lax.axis_index("slab") * sub_count + lax.axis_index("sub")
    up_tag, down_tag = jnp.int32(0), jnp.int32(0)
    for slot in range(slots):
        out_slot = target[slot]
        owner = out_slot // OSLOTS
        up_tag = jnp.where(owner == me + sub_count, out_slot - owner * OSLOTS + 1, up_tag)
        down_tag = jnp.where(
            (out_slot >= 0) & (owner == me - sub_count), out_slot - owner * OSLOTS + 1, down_tag
        )
    head[...] = jnp.zeros_like(head)
    for offset, tag in enumerate((hole, up_tag, down_tag)):
        head[pl.ds(3 * kept + offset, 1), :] = jnp.full((1, rows), tag.astype(F32))
    copies[0].wait()
    for row in range(kept):
        start = pl.multiple_of(slot_of(row, hole, kept, slots) * rows, rows)
        block = coords[:, pl.ds(start, rows)].astype(F32)
        for axis in range(3):
            head[pl.ds(axis * kept + row, 1), :] = block[axis : axis + 1, :]
    pay[0:head_of(kept), :] = head[...].astype(BF16)
    lat = latent.shape[1]
    if kept < slots:
        copies[slots].wait()
    for row in range(kept):
        copies[1 + row].wait()
        block = blocks[slot_of(row, hole, kept, slots)]
        start = head_of(kept) + row * lat
        pay[start : start + lat, :] = jnp.transpose(block)


def plan_kernel(
    kept, slots, rows, homes, phases, target_in, near_in, pay, w_send_in, w_in_in, tiles, counts,
    query, send_turned, in_turned, target, near, w_send, w_in, terms, sems,
):
    loads = [
        pltpu.make_async_copy(source, ref, sems.at[index])
        for index, (source, ref) in enumerate(
            ((target_in, target), (near_in, near), (w_send_in, w_send), (w_in_in, w_in))
        )
    ]
    for load in loads:
        load.start()
    total = jnp.zeros((kept, rows), F32)
    head = pay[0 : head_of(kept), :].astype(F32)
    for axis in range(3):
        coord = head[axis * kept : axis * kept + kept, :]
        total = total + coord * coord
        for part, value in enumerate(pieces(coord * (2 * LOG2_SCALE))):
            put(terms, part * 3 + axis, kept, value)
    put(terms, 9, kept, jnp.ones((3 * kept, rows), F32))
    for part, value in enumerate(pieces(total * -LOG2_SCALE)):
        put(terms, 12 + part, kept, value)
    put(terms, 15, kept, jnp.zeros((kept, rows), F32))
    for row in range(kept):
        query[row] = features(terms, row, kept)
    for load in loads:
        load.wait()
    lat = w_send.shape[0]
    send_turned[:, 0:lat] = jnp.transpose(w_send[:, 0:lat])
    send_turned[:, lat : 2 * lat] = jnp.transpose(w_send[:, lat : 2 * lat])
    in_turned[...] = jnp.transpose(w_in[...])
    hole = first_hole(target, slots)
    sub_count, slab_count = lax.axis_size("sub"), lax.axis_size("slab")
    my_slab, my_sub = lax.axis_index("slab"), lax.axis_index("sub")
    limit = slab_count * sub_count * slots
    inverse = 65536 // slots + 1
    if any(i * inverse >> 16 != i // slots for i in range(limit)):
        raise ValueError("slot ids")
    words = [sum(home << (6 * i) for i, home in enumerate(homes[at : at + 4])) for at in (0, 4, 8)]
    for phase in range(phases):
        counts[phase] = 0

    def add(phase, entry):
        place = counts[phase]
        tiles[phase, place] = entry
        counts[phase] = place + 1

    me = my_slab * sub_count + my_sub

    def per_row(row, carry):
        slot = slot_of(row, hole, kept, slots)
        stays = lax.shift_right_arithmetic(target[slot], OSLOTS.bit_length() - 1) == me
        end = jnp.where(stays, phases - 1, phases - 2)

        @pl.when(target[slot] >= 0)
        def _():
            add(homes[MATES] // 8, row * 256 + homes[MATES] % 8 * 16 + slot)
            for k in range(near.shape[0]):
                other = near[k, slot]
                device = lax.shift_right_logical(other * inverse, 16)
                step = device // sub_count - my_slab
                word = jnp.where(step < 0, words[0], jnp.where(step == 0, words[1], words[2]))
                home = lax.shift_right_logical(word, 6 * jnp.bitwise_xor(device % sub_count, my_sub))
                phase = jnp.bitwise_and(lax.shift_right_logical(home, 3), 7)
                phase = jnp.where(phase == phases - 2, end, phase)
                line = jnp.bitwise_and(home, 7)
                add(phase, row * 256 + line * 16 + other - device * slots)

        return carry

    lax.fori_loop(0, kept, per_row, 0)
    for phase in range(phases):
        for extra in range(GROUPS[0]):
            tiles[phase, counts[phase] + extra] = kept * 256


def gather_tiles(
    kept, slots, rows, lat, phase, tiles, counts, query, lines, acc, scratch, groups=GROUPS
):
    land, feats, terms, holes = scratch
    for line, parts in enumerate(lines):
        at = 0
        for ref, start, length in parts:
            land[line, at : at + length, :] = ref[start : start + length, :]
            at += length
    put(terms, 12, kept, jnp.ones((3 * kept, rows), F32))
    put(terms, 15, kept, jnp.zeros((kept, rows), F32))
    for line, parts in enumerate(lines):
        head = parts[0][0][0 : head_of(kept), :].astype(F32)
        holes[line] = jnp.max(head[3 * kept : 3 * kept + 1, :]).astype(jnp.int32)
        total = jnp.zeros((kept, rows), F32)
        for axis in range(3):
            coord = head[axis * kept : axis * kept + kept, :]
            total = total + coord * coord
            for part in range(3):
                put(terms, part * 3 + axis, kept, coord)
        for part, value in enumerate(pieces(total * -LOG2_SCALE)):
            put(terms, 9 + part, kept, value)
        for block in range(kept):
            feats[line * kept + block] = features(terms, block, kept)

    def work(first, size):
        owns, exponents, sources = [], [], []
        for step in range(size):
            entry = tiles[phase, first + step]
            own = lax.shift_right_logical(entry, 8)
            line = jnp.bitwise_and(lax.shift_right_logical(entry, 4), 15)
            slot = jnp.bitwise_and(entry, 15)
            block = jnp.where(slot == kept, holes[line], slot) if kept < slots else slot
            owns.append(own)
            begin = pl.multiple_of(head_of(kept) + block * lat, 16)
            sources.append(land[line, pl.ds(begin, lat), :])
            exponents.append(
                mm(feats[line * kept + block], query[jnp.minimum(own, kept - 1)], left_dim=0)
            )
        results = []
        for exponent, source in zip(exponents, sources):
            wide = jnp.exp2(exponent)
            square = wide * wide
            results.append(
                (mm(source, wide.astype(BF16)), mm(source, (square * square).astype(BF16)))
            )
        for own, (first, second) in zip(owns, results):
            acc[own, 0:lat] += first
            acc[own, lat : 2 * lat] += second

    large, count = groups[0], counts[phase]
    small = groups[1] if len(groups) > 1 else 0
    whole = (count + large - 1 - small) // large
    lax.fori_loop(0, whole, lambda group, carry: work(group * large, large), None)
    left = count - whole * large
    for size, below in zip(groups[1:], (*groups[2:], 0)):
        pl.when((left > below) & (left <= size))(functools.partial(work, whole * large, size))


def lines_of(refs, parts):
    return [[(refs[index], start, length) for index, start, length in line] for line in parts]


def tiles_kernel(kept, slots, rows, lat, phase, parts, ref_count, has_earlier, tiles, counts, query, *rest):
    earlier, rest = (rest[0], rest[1:]) if has_earlier else (None, rest)
    lines, (acc, *scratch) = lines_of(rest, parts), rest[ref_count:]
    if has_earlier:
        acc[...] = earlier[...]
    else:
        acc[...] = jnp.zeros_like(acc)
    gather_tiles(kept, slots, rows, lat, phase, tiles, counts, query, lines, acc, scratch)


def update(lat, scale, send_turned, in_turned, w_out, old, turned, sums, joined, hidden, out):
    for row, (latent, total) in enumerate(zip(turned, sums)):
        message = mm(send_turned[...], total().astype(BF16)) * scale
        joined[row, 0:lat, :] = latent()
        joined[row, lat : 2 * lat, :] = message.astype(BF16)
    for row in range(len(sums)):
        before = mm(in_turned[...], joined[row])
        hidden[row] = (before * (0.5 + 0.5 * jnp.tanh(0.5 * before))).astype(BF16)
    for row in range(len(sums)):
        change = mm(hidden[row], w_out[...], left_dim=0)
        out(row, (old[row].astype(F32) + change).astype(BF16))


def owner_of(out_slot):
    return lax.shift_right_arithmetic(out_slot, OSLOTS.bit_length() - 1)


def moving_kernel(
    kept, slots, rows, lat, phase, parts, ref_count, scale, target, tiles, counts, query,
    send_turned, in_turned, w_out, latents, pay, earlier, *rest,
):
    lines, rest = lines_of(rest, parts), rest[ref_count:]
    moving_up, moving_down, acc, old, joined, hidden, loads, *scratch = rest
    hole = first_hole(target, slots)
    me = lax.axis_index("slab") * lax.axis_size("sub") + lax.axis_index("sub")
    up_row, down_row = jnp.int32(0), jnp.int32(0)
    for row in range(kept):
        out_slot = target[slot_of(row, hole, kept, slots)]
        owner = owner_of(out_slot)
        up_row = jnp.where(owner > me, row, up_row)
        down_row = jnp.where((out_slot >= 0) & (owner < me), row, down_row)
    moved = (up_row, down_row)
    copies = []
    for index, row in enumerate(moved):
        start = pl.multiple_of(slot_of(row, hole, kept, slots) * rows, rows)
        copies.append(
            pltpu.make_async_copy(latents.at[pl.ds(start, rows), :], old.at[index], loads.at[index])
        )
    for copy in copies:
        copy.start()
    for row in moved:
        acc[row] = earlier[row]
    gather_tiles(
        kept, slots, rows, lat, phase, tiles, counts, query, lines, acc, scratch, MOVING_GROUPS
    )
    for copy in copies:
        copy.wait()

    def turned_of(row):
        return lambda: pay[pl.ds(pl.multiple_of(head_of(kept) + row * lat, 16), lat), :]

    def out(index, value):
        (moving_up, moving_down)[index][...] = value

    update(
        lat, scale, send_turned, in_turned, w_out, old, [turned_of(row) for row in moved],
        [lambda row=row: acc[row] for row in moved], joined, hidden, out,
    )


def staying_kernel(
    kept, slots, rows, lat, phase, parts, ref_count, scale, target, tiles, counts, query,
    send_turned, in_turned, w_out, latents, pay, earlier, *rest,
):
    lines, rest = lines_of(rest, parts), rest[ref_count:]
    updated, acc, old, joined, hidden, loads, *scratch = rest
    hole = first_hole(target, slots)
    copies = []
    for row in range(kept):
        start = pl.multiple_of(slot_of(row, hole, kept, slots) * rows, rows)
        copies.append(
            pltpu.make_async_copy(latents.at[pl.ds(start, rows), :], old.at[row], loads.at[row])
        )
    for copy in copies:
        copy.start()
    acc[...] = earlier[...]
    gather_tiles(kept, slots, rows, lat, phase, tiles, counts, query, lines, acc, scratch)
    for copy in copies:
        copy.wait()

    def turned_of(row):
        start = head_of(kept) + row * lat
        return lambda: pay[start : start + lat, :]

    def out(row, value):
        updated[row] = value

    update(
        lat, scale, send_turned, in_turned, w_out, old, [turned_of(row) for row in range(kept)],
        [lambda row=row: acc[row] for row in range(kept)], joined, hidden, out,
    )


def place_kernel(
    kept, slots, rows, target, below_head, above_head, below, above, updated, out, sems
):
    hole = first_hole(target, slots)
    me = lax.axis_index("slab") * lax.axis_size("sub") + lax.axis_index("sub")
    copies = []
    for row in range(kept):
        out_slot = target[slot_of(row, hole, kept, slots)]
        stays = owner_of(out_slot) == me
        start = pl.multiple_of(jnp.where(stays, out_slot - me * OSLOTS, 0) * rows, rows)
        copies.append(
            (
                stays,
                pltpu.make_async_copy(
                    updated.at[row], out.at[pl.ds(start, rows), :], sems.at[row]
                ),
            )
        )
    for index, (head, block) in enumerate(((below_head, below), (above_head, above))):
        at = 3 * kept + 1 + index
        tag = jnp.max(head[0 : head_of(kept), :].astype(F32)[at : at + 1, :]).astype(jnp.int32)
        start = pl.multiple_of(jnp.maximum(tag - 1, 0) * rows, rows)
        copies.append(
            (
                tag > 0,
                pltpu.make_async_copy(block, out.at[pl.ds(start, rows), :], sems.at[kept + index]),
            )
        )
    for goes, copy in copies:
        pl.when(goes)(copy.start)
    for goes, copy in copies:
        pl.when(goes)(copy.wait)


def on_device(latent, positions, target, neighbours, w_send, w_in, w_out):
    lat = latent.shape[1]
    slots = target.shape[0]
    rows = latent.shape[0] // slots
    near_count = neighbours.shape[1]
    slab_count = lax.axis_size("slab")
    kept = slots - 1 if slab_count <= 4 else slots
    length = head_of(kept) + kept * lat
    if lax.axis_size("sub") != MATES:
        raise ValueError("sizes")
    up = [(i, i + 1) for i in range(slab_count - 1)]
    down = [(j, i) for i, j in up]
    def mate_of(value, bit):
        return lax.ppermute(value, "sub", [(i, i ^ bit) for i in range(MATES)])

    def upward(value):
        return lax.ppermute(value, "slab", up)

    def downward(value):
        return lax.ppermute(value, "slab", down)

    cut_up, cut = length - REST_UP * lat, length - REST * lat
    pay = call(
        functools.partial(pack_kernel, kept, slots, rows),
        "pack",
        jax.ShapeDtypeStruct((length, rows), BF16),
        [HB, HB, HB],
        VM,
        [
            pltpu.SMEM((slots,), jnp.int32),
            pltpu.VMEM(positions.shape, BF16),
            pltpu.VMEM((head_of(kept), rows), F32),
            pltpu.VMEM((slots, rows, lat), BF16),
            pltpu.SemaphoreType.DMA((slots + 2,)),
        ],
        in_hbm(target, latent, positions),
    )
    across = mate_of(pay, 2)
    below_own, above_own = upward(pay), downward(pay)
    pair = mate_of(pay, 1)

    homes = (10, 16, 18, 24, 0, 1, 8, 9, 11, 17, 19, 25)
    phase_count = 5
    most = kept * (near_count + 1) + GROUPS[0]
    tiles, counts, query, send_turned, in_turned = call(
        functools.partial(plan_kernel, kept, slots, rows, homes, phase_count),
        "plan",
        (
            jax.ShapeDtypeStruct((phase_count, most), jnp.int32),
            jax.ShapeDtypeStruct((phase_count,), jnp.int32),
            jax.ShapeDtypeStruct((kept, FEAT, rows), BF16),
            jax.ShapeDtypeStruct((lat, 2 * lat), BF16),
            jax.ShapeDtypeStruct((lat, 2 * lat), BF16),
        ),
        [HB, HB, VM, HB, HB],
        (SM, SM, VM, VM, VM),
        [
            pltpu.SMEM((slots,), jnp.int32),
            pltpu.SMEM((near_count, slots), jnp.int32),
            pltpu.VMEM(w_send.shape, BF16),
            pltpu.VMEM(w_in.shape, BF16),
            pltpu.VMEM((rows // 128, FEAT * kept, 128), F32),
            pltpu.SemaphoreType.DMA((4,)),
        ],
        (*in_hbm(target, neighbours.T), pay, *in_hbm(w_send, w_in)),
    )

    def scratch_for(parts):
        return [
            pltpu.VMEM((len(parts), length, rows), BF16),
            pltpu.VMEM((len(parts) * kept, FEAT, rows), BF16),
            pltpu.VMEM((rows // 128, FEAT * kept, 128), F32),
            pltpu.SMEM((len(parts),), jnp.int32),
        ]

    sums = (kept + 1, 2 * lat, rows)
    whole = lambda index: ((index, 0, length),)
    split = lambda index, other, start=0: ((index, 0, cut), (other, start, length - cut))
    split_up = lambda index, other: ((index, 0, cut_up), (other, 0, length - cut_up))

    def tiles_call(phase, parts, refs, earlier):
        earlier = [] if earlier is None else [earlier]
        return call(
            functools.partial(
                tiles_kernel, kept, slots, rows, lat, phase, parts, len(refs), bool(earlier)
            ),
            f"tiles{phase}",
            jax.ShapeDtypeStruct(sums, F32),
            [SM, SM, VM] + [VM] * (len(earlier) + len(refs)),
            VM,
            scratch_for(parts),
            (tiles, counts, query, *earlier, *refs),
        )

    partial = tiles_call(0, (whole(0), whole(1)), [pay, pair], None)
    across, partial = lax.optimization_barrier((across, partial))
    above_far, below_far = downward(across[:cut]), upward(across[:cut_up])
    across_pair = mate_of(across, 1)
    far_rest = mate_of(jnp.concatenate([below_own[cut_up:], above_own[cut:]], axis=0), 2)
    below_pair, above_pair = mate_of(below_own, 1), mate_of(above_own, 1)
    partial = tiles_call(
        1,
        (whole(0), whole(1), whole(2), whole(3)),
        [across, across_pair, below_own, above_own],
        partial,
    )
    above_far, below_far, partial = lax.optimization_barrier((above_far, below_far, partial))
    below_last, above_last = mate_of(below_far, 1), mate_of(above_far, 1)
    far_rest, below_far = lax.optimization_barrier((far_rest, below_far))
    last_rest = mate_of(far_rest, 1)
    partial = tiles_call(
        2,
        (whole(0), whole(1), split_up(2, 4), split(3, 4, length - cut_up)),
        [below_pair, above_pair, below_far, above_far, far_rest],
        partial,
    )
    scale = (rows * (near_count + 1)) ** -0.5
    last = (split_up(0, 2), split(1, 2, length - cut_up))
    last_args = (
        target, tiles, counts, query, send_turned, in_turned, w_out, latent, pay, partial,
        below_last, above_last, last_rest,
    )
    last_specs = [SM, SM, SM, VM, VM, VM, VM, HB, VM, VM, VM, VM, VM]

    def update_scratch(count):
        return [
            pltpu.VMEM(sums, F32),
            pltpu.VMEM((count, rows, lat), BF16),
            pltpu.VMEM((count, 2 * lat, rows), BF16),
            pltpu.VMEM((count, lat, rows), BF16),
            pltpu.SemaphoreType.DMA((count,)),
            *scratch_for(last),
        ]

    moving_up, moving_down = call(
        functools.partial(moving_kernel, kept, slots, rows, lat, 3, last, 3, scale),
        "moving",
        (jax.ShapeDtypeStruct((rows, lat), BF16), jax.ShapeDtypeStruct((rows, lat), BF16)),
        last_specs,
        (VM, VM),
        update_scratch(2),
        last_args,
    )
    partial, moving_up, moving_down = lax.optimization_barrier((partial, moving_up, moving_down))
    below, above = upward(moving_up), downward(moving_down)
    updated = call(
        functools.partial(staying_kernel, kept, slots, rows, lat, 4, last, 3, scale),
        "staying",
        jax.ShapeDtypeStruct((kept, rows, lat), BF16),
        last_specs,
        VM,
        update_scratch(kept),
        (*last_args[:9], partial, *last_args[10:]),
    )
    return call(
        functools.partial(place_kernel, kept, slots, rows),
        "place",
        jax.ShapeDtypeStruct((OSLOTS * rows, lat), BF16),
        [SM, VM, VM, VM, VM, VM],
        HB,
        [pltpu.SemaphoreType.DMA((kept + 2,))],
        (target, below_own, above_own, below, above, updated),
    )


def solution(mesh):
    placed = (
        P(("grp", "slab", "sub"), None),
        P(None, ("grp", "slab", "sub")),
        P(("grp", "slab", "sub")),
        P(("grp", "slab", "sub"), None),
        P(),
        P(),
        P(),
    )
    return jax.shard_map(
        on_device,
        mesh=mesh,
        in_specs=placed,
        out_specs=P(("grp", "slab", "sub"), None),
        check_vma=False,
    )
```

```python
import functools

import jax
import jax.numpy as jnp
from jax import lax
from jax.experimental import pallas as pl
from jax.experimental.pallas import tpu as pltpu
from jax.sharding import PartitionSpec as P

OSLOTS = 8
MATES = 4
GROUPS = (16, 8, 4)
FEW_GROUPS = (8, 4)
REST_UP, REST = 3, 2
INFO = 16
FEAT = 16
LOG2_SCALE = 0.7213475204444817
VMEM_LIMIT = 18 << 20
F32, BF16 = jnp.float32, jnp.bfloat16


def head_of(kept):
    return (3 * kept + 2 + 15) // 16 * 16


def mm(left, right, left_dim=1):
    dims = (((left_dim,), (0,)), ((), ()))
    return lax.dot_general(left, right, dims, preferred_element_type=F32)


def pieces(value):
    high = value.astype(BF16).astype(F32)
    rest = value - high
    middle = rest.astype(BF16).astype(F32)
    return high, middle, rest - middle


def put(terms, index, kept, value):
    for half in range(terms.shape[0]):
        terms[half, index * kept : index * kept + value.shape[0], :] = value[
            :, half * 128 : half * 128 + 128
        ]


def features(terms, index, kept):
    halves = [
        terms[half, pl.ds(index, FEAT, stride=kept), :].astype(BF16)
        for half in range(terms.shape[0])
    ]
    return jnp.concatenate(halves, axis=1)


def owner_of(out_slot):
    return lax.shift_right_arithmetic(out_slot, OSLOTS.bit_length() - 1)


def query_terms(terms, head, kept):
    rows = head.shape[1]
    total = jnp.zeros((kept, rows), F32)
    for axis in range(3):
        coord = head[axis * kept : axis * kept + kept, :]
        total = total + coord * coord
        for part, value in enumerate(pieces(coord * (2 * LOG2_SCALE))):
            put(terms, part * 3 + axis, kept, value)
    put(terms, 9, kept, jnp.ones((3 * kept, rows), F32))
    for part, value in enumerate(pieces(total * -LOG2_SCALE)):
        put(terms, 12 + part, kept, value)
    put(terms, 15, kept, jnp.zeros((kept, rows), F32))


def first_hole(target_ref, slots):
    hole = jnp.int32(slots - 1)
    for slot in reversed(range(slots)):
        hole = jnp.where(target_ref[slot] < 0, slot, hole)
    return hole


def slot_of(row, hole, kept, slots):
    return jnp.where(row == hole, slots - 1, row) if kept < slots else row


def call(kernel, name, out_shape, in_specs, out_specs, scratch, args, flops=0, limit=VMEM_LIMIT):
    return pl.pallas_call(
        kernel,
        name=name,
        out_shape=out_shape,
        in_specs=in_specs,
        out_specs=out_specs,
        scratch_shapes=scratch,
        compiler_params=pltpu.CompilerParams(vmem_limit_bytes=limit),
        cost_estimate=pl.CostEstimate(flops=flops, bytes_accessed=flops >> 9, transcendentals=0),
    )(*args)


VM = pl.BlockSpec(memory_space=pltpu.VMEM)
SM = pl.BlockSpec(memory_space=pltpu.SMEM)
HB = pl.BlockSpec(memory_space=pltpu.HBM)


def in_hbm(*arrays):
    return [pltpu.with_memory_space_constraint(array, pltpu.HBM) for array in arrays]


def pack_kernel(
    kept, slots, rows, target_in, near_in, latent, positions, pay, target, near, coords, head,
    blocks, sems,
):
    loads = [
        pltpu.make_async_copy(target_in, target, sems.at[slots + 1]),
        pltpu.make_async_copy(near_in, near, sems.at[slots + 2]),
    ]
    copies = [pltpu.make_async_copy(positions, coords, sems.at[slots])]
    for slot in range(slots):
        copies.append(
            pltpu.make_async_copy(
                latent.at[slot * rows : slot * rows + rows, :], blocks.at[slot], sems.at[slot]
            )
        )
    for copy in (*loads, *copies):
        copy.start()
    for load in loads:
        load.wait()
    hole = first_hole(target, slots)
    sub_count = lax.axis_size("sub")
    my_slab = lax.axis_index("slab")
    me = my_slab * sub_count + lax.axis_index("sub")
    lane = lax.broadcasted_iota(jnp.int32, (1, rows), 1)
    info = jnp.zeros((1, rows), jnp.int32)
    for side, device in enumerate((me + sub_count, me - sub_count)):
        tag, moving = jnp.int32(0), jnp.int32(0)
        for slot in range(slots):
            out_slot = target[slot]
            goes = (out_slot >= 0) & (owner_of(out_slot) == device)
            tag = jnp.where(goes, out_slot - device * OSLOTS + 1, tag)
            moving = jnp.where(goes, slot, moving)
        row = jnp.where(moving == slots - 1, hole, moving) if kept < slots else moving
        words = [tag, row] + [
            near[k, moving] - (my_slab - 1) * sub_count * slots for k in range(near.shape[0])
        ]
        for place, word in enumerate(words):
            info = jnp.where(lane == side * INFO + place, word, info)
    head[...] = jnp.zeros_like(head)
    head[pl.ds(3 * kept, 1), :] = jnp.full((1, rows), hole.astype(F32))
    head[pl.ds(3 * kept + 1, 1), :] = info.astype(F32)
    copies[0].wait()
    for row in range(kept):
        start = pl.multiple_of(slot_of(row, hole, kept, slots) * rows, rows)
        block = coords[:, pl.ds(start, rows)].astype(F32)
        for axis in range(3):
            head[pl.ds(axis * kept + row, 1), :] = block[axis : axis + 1, :]
    pay[0:head_of(kept), :] = head[...].astype(BF16)
    lat = latent.shape[1]
    if kept < slots:
        copies[slots].wait()
    for row in range(kept):
        copies[1 + row].wait()
        block = blocks[slot_of(row, hole, kept, slots)]
        start = head_of(kept) + row * lat
        pay[start : start + lat, :] = jnp.transpose(block)


def plan_kernel(
    kept, slots, rows, homes, phases, target_in, near_in, pay, w_send_in, w_in_in, tiles, counts,
    query, send_turned, in_turned, target, near, w_send, w_in, terms, sems,
):
    loads = [
        pltpu.make_async_copy(source, ref, sems.at[index])
        for index, (source, ref) in enumerate(
            ((target_in, target), (near_in, near), (w_send_in, w_send), (w_in_in, w_in))
        )
    ]
    for load in loads:
        load.start()
    query_terms(terms, pay[0 : head_of(kept), :].astype(F32), kept)
    for load in loads:
        load.wait()
    lat = w_send.shape[0]
    send_turned[:, 0:lat] = jnp.transpose(w_send[:, 0:lat])
    send_turned[:, lat : 2 * lat] = jnp.transpose(w_send[:, lat : 2 * lat])
    in_turned[...] = jnp.transpose(w_in[...])
    hole = first_hole(target, slots)
    sub_count, slab_count = lax.axis_size("sub"), lax.axis_size("slab")
    my_slab, my_sub = lax.axis_index("slab"), lax.axis_index("sub")
    limit = slab_count * sub_count * slots
    inverse = 65536 // slots + 1
    if any(i * inverse >> 16 != i // slots for i in range(limit)):
        raise ValueError("slot ids")
    words = [sum(home << (6 * i) for i, home in enumerate(homes[at : at + 4])) for at in (0, 4, 8)]
    for phase in range(phases):
        counts[phase] = 0

    def add(phase, entry):
        place = counts[phase]
        tiles[phase, place] = entry
        counts[phase] = place + 1

    me = my_slab * sub_count + my_sub
    for row in range(kept):
        out_slot = target[slot_of(row, hole, kept, slots)]
        own = jnp.where(owner_of(out_slot) == me, out_slot - me * OSLOTS, OSLOTS)
        query[own] = features(terms, row, kept)

    def per_slot(slot, carry):
        out_slot = target[slot]
        own = (out_slot - me * OSLOTS) * 256

        @pl.when(owner_of(out_slot) == me)
        def _():
            add(homes[MATES] // 8, own + homes[MATES] % 8 * 16 + slot)
            for k in range(near.shape[0]):
                other = near[k, slot]
                device = lax.shift_right_logical(other * inverse, 16)
                step = device // sub_count - my_slab
                word = jnp.where(step < 0, words[0], jnp.where(step == 0, words[1], words[2]))
                home = lax.shift_right_logical(word, 6 * jnp.bitwise_xor(device % sub_count, my_sub))
                phase = jnp.bitwise_and(lax.shift_right_logical(home, 3), 7)
                line = jnp.bitwise_and(home, 7)
                add(phase, own + line * 16 + other - device * slots)

        return carry

    lax.fori_loop(0, slots, per_slot, 0)
    for phase in range(phases):
        for extra in range(GROUPS[0]):
            tiles[phase, counts[phase] + extra] = OSLOTS * 256


def gather_tiles(
    kept, slots, rows, lat, phase, tiles, counts, query, lines, acc, scratch, groups=GROUPS
):
    land, feats, terms, holes = scratch
    for line, parts in enumerate(lines):
        at = 0
        for ref, start, length in parts:
            land[line, at : at + length, :] = ref[start : start + length, :]
            at += length
    put(terms, 12, kept, jnp.ones((3 * kept, rows), F32))
    put(terms, 15, kept, jnp.zeros((kept, rows), F32))
    for line, parts in enumerate(lines):
        head = parts[0][0][0 : head_of(kept), :].astype(F32)
        holes[line] = jnp.max(head[3 * kept : 3 * kept + 1, :]).astype(jnp.int32)
        total = jnp.zeros((kept, rows), F32)
        for axis in range(3):
            coord = head[axis * kept : axis * kept + kept, :]
            total = total + coord * coord
            for part in range(3):
                put(terms, part * 3 + axis, kept, coord)
        for part, value in enumerate(pieces(total * -LOG2_SCALE)):
            put(terms, 9 + part, kept, value)
        for block in range(kept):
            feats[line * kept + block] = features(terms, block, kept)

    def work(first, size):
        owns, exponents, sources = [], [], []
        for step in range(size):
            entry = tiles[phase, first + step]
            own = lax.shift_right_logical(entry, 8)
            line = jnp.bitwise_and(lax.shift_right_logical(entry, 4), 15)
            slot = jnp.bitwise_and(entry, 15)
            block = jnp.where(slot == kept, holes[line], slot) if kept < slots else slot
            owns.append(own)
            begin = pl.multiple_of(head_of(kept) + block * lat, 16)
            sources.append(land[line, pl.ds(begin, lat), :])
            exponents.append(
                mm(feats[line * kept + block], query[own], left_dim=0)
            )
        results = []
        for exponent, source in zip(exponents, sources):
            wide = jnp.exp2(exponent)
            square = wide * wide
            results.append(
                (mm(source, wide.astype(BF16)), mm(source, (square * square).astype(BF16)))
            )
        for own, (first, second) in zip(owns, results):
            acc[own, 0:lat] += first
            acc[own, lat : 2 * lat] += second

    large, count = groups[0], counts[phase]
    small = groups[1] if len(groups) > 1 else 0
    whole = (count + large - 1 - small) // large
    lax.fori_loop(0, whole, lambda group, carry: work(group * large, large), None)
    left = count - whole * large
    for size, below in zip(groups[1:], (*groups[2:], 0)):
        pl.when((left > below) & (left <= size))(functools.partial(work, whole * large, size))


def lines_of(refs, parts):
    return [[(refs[index], start, length) for index, start, length in line] for line in parts]


def tiles_kernel(kept, slots, rows, lat, phase, parts, ref_count, has_earlier, tiles, counts, query, *rest):
    earlier, rest = (rest[0], rest[1:]) if has_earlier else (None, rest)
    lines, (acc, *scratch) = lines_of(rest, parts), rest[ref_count:]
    if has_earlier:
        acc[...] = earlier[...]
    else:
        acc[...] = jnp.zeros_like(acc)
    gather_tiles(kept, slots, rows, lat, phase, tiles, counts, query, lines, acc, scratch)


def arrivals_kernel(
    kept, slots, rows, lat, homes, phases, parts, ref_count, tiles_in, counts_in, query_in,
    send_turned, below, above, *rest,
):
    refs, rest = rest[:ref_count], rest[ref_count:]
    tiles, counts, query, arrived, beyond, acc, few, few_counts, few_query, *scratch = rest
    terms = scratch[2]
    my_sub = lax.axis_index("sub")
    query[...] = query_in[...]
    for phase in range(phases):
        count = counts_in[phase]
        counts[phase] = count

        def keep(place, carry, phase=phase):
            tiles[phase, place] = tiles_in[phase, place]
            return carry

        lax.fori_loop(0, count, keep, 0)
    few_counts[0] = 0

    def add(phase, entry):
        place = counts[phase]
        tiles[phase, place] = entry
        counts[phase] = place + 1

    def word_of(words, mate):
        return lax.shift_right_logical(words, 6 * mate)

    near_count = INFO // 2
    plane = MATES * slots
    inverse = 65536 // slots + 1
    own_words = sum(home << (6 * i) for i, home in enumerate((12, 13, 8, 9)))
    for side, ref in enumerate((below, above)):
        head = ref[0 : head_of(kept), :].astype(F32)
        query_terms(terms, head, kept)
        info = head[3 * kept + 1 : 3 * kept + 2, :]
        lane = lax.broadcasted_iota(jnp.int32, info.shape, 1)

        def read(place, info=info, lane=lane):
            return jnp.sum(jnp.where(lane == place, info, 0.0)).astype(jnp.int32)

        tag, row = read(side * INFO), read(side * INFO + 1)
        codes = [read(side * INFO + 2 + k) for k in range(near_count)]
        own = jnp.where(tag > 0, tag - 1, OSLOTS)
        arrived[2 * side] = own
        arrived[2 * side + 1] = row
        query[own] = features(terms, row, kept)
        line_words = sum(home << (6 * i) for i, home in enumerate(homes[8 * side : 8 * side + 4]))

        @pl.when(tag > 0)
        def _(own=own, row=row, codes=codes, side=side, line_words=line_words):
            home = homes[8 * side]
            add(home // 8, own * 256 + home % 8 * 16 + row)
            for code in codes:
                device = lax.shift_right_logical(code * inverse, 16)
                slot = code - device * slots
                mate = jnp.bitwise_xor(jnp.bitwise_and(device, MATES - 1), my_sub)
                step = lax.shift_right_logical(device, 2) - 1
                word = jnp.where(step == 0, word_of(line_words, mate), word_of(own_words, mate))
                phase = jnp.bitwise_and(lax.shift_right_logical(word, 3), 7)
                line = jnp.bitwise_and(word, 7)

                @pl.when(step != 2 * side - 1)
                def _(phase=phase, line=line, slot=slot):
                    add(phase, own * 256 + line * 16 + slot)

        other = 1 - side
        tag, row = read(other * INFO), read(other * INFO + 1)
        codes = [read(other * INFO + 2 + k) for k in range(near_count)]
        few_query[side] = features(terms, row, kept)

        @pl.when(tag > 0)
        def _(codes=codes, side=side):
            for code in codes:
                device = lax.shift_right_logical(code * inverse, 16)
                slot = code - device * slots
                mate = jnp.bitwise_xor(jnp.bitwise_and(device, MATES - 1), my_sub)
                step = lax.shift_right_logical(device, 2) - 1

                @pl.when(step == 1 - 2 * side)
                def _(slot=slot, mate=mate):
                    place = few_counts[0]
                    few[0, place] = side * 256 + mate * 16 + slot
                    few_counts[0] = place + 1

    few_query[2] = few_query[0]
    for extra in range(GROUPS[0]):
        few[0, few_counts[0] + extra] = 2 * 256
        for phase in range(phases):
            tiles[phase, counts[phase] + extra] = OSLOTS * 256
    acc[...] = jnp.zeros_like(acc)
    gather_tiles(
        kept, slots, rows, lat, 0, few, few_counts, few_query, lines_of(refs, parts), acc, scratch,
        FEW_GROUPS,
    )
    if beyond.shape[0] == 1:
        upper = lax.axis_index("slab") * 2 >= lax.axis_size("slab")
        sides = [jnp.where(upper, 0, 1)]
    else:
        sides = [0, 1]
    for place, side in enumerate(sides):
        beyond[place] = mm(send_turned[...], acc[side].astype(BF16)).astype(BF16)


def last_kernel(
    kept, slots, rows, lat, phase, parts, ref_count, ways, scale, target, tiles, counts, arrived, query,
    send_turned, in_turned, w_out, pay, below, above, earlier, *rest,
):
    passed, rest = rest[:ways], rest[ways:]
    lines, rest = lines_of(rest, parts), rest[ref_count:]
    out, acc, sums, joined, hidden, updated, stores, *scratch = rest
    acc[...] = earlier[...]
    gather_tiles(kept, slots, rows, lat, phase, tiles, counts, query, lines, acc, scratch)
    hole = first_hole(target, slots)
    me = lax.axis_index("slab") * lax.axis_size("sub") + lax.axis_index("sub")
    for row in range(kept):
        out_slot = target[slot_of(row, hole, kept, slots)]
        own = jnp.where(owner_of(out_slot) == me, out_slot - me * OSLOTS, OSLOTS)
        start = head_of(kept) + row * lat
        joined[own, 0:lat, :] = pay[start : start + lat, :]
    for side, ref in enumerate((below, above)):
        start = pl.multiple_of(head_of(kept) + arrived[2 * side + 1] * lat, 16)
        joined[arrived[2 * side], 0:lat, :] = ref[pl.ds(start, lat), :]
    for own in range(OSLOTS):
        sums[own] = mm(send_turned[...], acc[own].astype(BF16))
    if ways == 1:
        upper = lax.axis_index("slab") * 2 >= lax.axis_size("slab")
        places = [jnp.where(upper, 0, 2)]
    else:
        places = [0, 2]
    for place, ref in zip(places, passed):
        sums[arrived[place]] += ref[...].astype(F32)
    for own in range(OSLOTS):
        joined[own, lat : 2 * lat, :] = (sums[own] * scale).astype(BF16)
    for own in range(OSLOTS):
        before = mm(in_turned[...], joined[own])
        hidden[own] = (before * (0.5 + 0.5 * jnp.tanh(0.5 * before))).astype(BF16)
    copies = []
    for own in range(OSLOTS):
        change = mm(hidden[own], w_out[...], left_dim=0)
        old = jnp.transpose(joined[own, 0:lat, :])
        updated[own] = (old.astype(F32) + change).astype(BF16)
        copies.append(
            pltpu.make_async_copy(
                updated.at[own], out.at[own * rows : own * rows + rows, :], stores.at[own]
            )
        )
        copies[-1].start()
    for copy in copies:
        copy.wait()


def on_device(latent, positions, target, neighbours, w_send, w_in, w_out):
    lat = latent.shape[1]
    slots = target.shape[0]
    rows = latent.shape[0] // slots
    near_count = neighbours.shape[1]
    slab_count = lax.axis_size("slab")
    kept = slots - 1 if slab_count <= 4 else slots
    length = head_of(kept) + kept * lat
    if lax.axis_size("sub") != MATES:
        raise ValueError("sizes")
    up = [(i, i + 1) for i in range(slab_count - 1)]
    down = [(j, i) for i, j in up]
    def mate_of(value, bit):
        return lax.ppermute(value, "sub", [(i, i ^ bit) for i in range(MATES)])

    def upward(value):
        return lax.ppermute(value, "slab", up)

    def downward(value):
        return lax.ppermute(value, "slab", down)

    cut_up, cut = length - REST_UP * lat, length - REST * lat
    pay = call(
        functools.partial(pack_kernel, kept, slots, rows),
        "pack",
        jax.ShapeDtypeStruct((length, rows), BF16),
        [HB, HB, HB, HB],
        VM,
        [
            pltpu.SMEM((slots,), jnp.int32),
            pltpu.SMEM((near_count, slots), jnp.int32),
            pltpu.VMEM(positions.shape, BF16),
            pltpu.VMEM((head_of(kept), rows), F32),
            pltpu.VMEM((slots, rows, lat), BF16),
            pltpu.SemaphoreType.DMA((slots + 3,)),
        ],
        in_hbm(target, neighbours.T, latent, positions),
    )
    across = mate_of(pay, 2)
    below_own, above_own = upward(pay), downward(pay)
    pair = mate_of(pay, 1)

    homes = (10, 16, 18, 24, 0, 1, 8, 9, 11, 17, 19, 25)
    phase_count = 4
    most = OSLOTS * (near_count + 1) + GROUPS[0]
    tiles, counts, query, send_turned, in_turned = call(
        functools.partial(plan_kernel, kept, slots, rows, homes, phase_count),
        "plan",
        (
            jax.ShapeDtypeStruct((phase_count, most), jnp.int32),
            jax.ShapeDtypeStruct((phase_count,), jnp.int32),
            jax.ShapeDtypeStruct((OSLOTS + 1, FEAT, rows), BF16),
            jax.ShapeDtypeStruct((lat, 2 * lat), BF16),
            jax.ShapeDtypeStruct((lat, 2 * lat), BF16),
        ),
        [HB, HB, VM, HB, HB],
        (SM, SM, VM, VM, VM),
        [
            pltpu.SMEM((slots,), jnp.int32),
            pltpu.SMEM((near_count, slots), jnp.int32),
            pltpu.VMEM(w_send.shape, BF16),
            pltpu.VMEM(w_in.shape, BF16),
            pltpu.VMEM((rows // 128, FEAT * kept, 128), F32),
            pltpu.SemaphoreType.DMA((4,)),
        ],
        (*in_hbm(target, neighbours.T), pay, *in_hbm(w_send, w_in)),
    )

    def scratch_for(parts):
        return [
            pltpu.VMEM((len(parts), length, rows), BF16),
            pltpu.VMEM((len(parts) * kept, FEAT, rows), BF16),
            pltpu.VMEM((rows // 128, FEAT * kept, 128), F32),
            pltpu.SMEM((len(parts),), jnp.int32),
        ]

    sums = (OSLOTS + 1, 2 * lat, rows)
    whole = lambda index: ((index, 0, length),)
    split = lambda index, other, start=0: ((index, 0, cut), (other, start, length - cut))
    split_up = lambda index, other: ((index, 0, cut_up), (other, 0, length - cut_up))

    def tiles_call(phase, parts, refs, earlier):
        earlier = [] if earlier is None else [earlier]
        return call(
            functools.partial(
                tiles_kernel, kept, slots, rows, lat, phase, parts, len(refs), bool(earlier)
            ),
            f"tiles{phase}",
            jax.ShapeDtypeStruct(sums, F32),
            [SM, SM, VM] + [VM] * (len(earlier) + len(refs)),
            VM,
            scratch_for(parts),
            (tiles, counts, query, *earlier, *refs),
        )

    partial = tiles_call(0, (whole(0), whole(1)), [pay, pair], None)
    across, partial = lax.optimization_barrier((across, partial))
    above_far, below_far = downward(across[:cut]), upward(across[:cut_up])
    across_pair = mate_of(across, 1)
    far_rest = mate_of(jnp.concatenate([below_own[cut_up:], above_own[cut:]], axis=0), 2)
    below_pair, above_pair = mate_of(below_own, 1), mate_of(above_own, 1)
    ways = 1 if slab_count <= 4 else 2
    tiles, counts, query, arrived, beyond = call(
        functools.partial(
            arrivals_kernel, kept, slots, rows, lat, homes, phase_count,
            tuple(whole(index) for index in range(4)), 4,
        ),
        "arrivals",
        (
            jax.ShapeDtypeStruct((phase_count, most), jnp.int32),
            jax.ShapeDtypeStruct((phase_count,), jnp.int32),
            jax.ShapeDtypeStruct((OSLOTS + 1, FEAT, rows), BF16),
            jax.ShapeDtypeStruct((4,), jnp.int32),
            jax.ShapeDtypeStruct((ways, lat, rows), BF16),
        ),
        [SM, SM] + [VM] * 8,
        (SM, SM, VM, SM, VM),
        [
            pltpu.VMEM((3, 2 * lat, rows), F32),
            pltpu.SMEM((1, 2 * near_count + GROUPS[0]), jnp.int32),
            pltpu.SMEM((1,), jnp.int32),
            pltpu.VMEM((3, FEAT, rows), BF16),
            *scratch_for(range(4)),
        ],
        (
            tiles, counts, query, send_turned, below_own, above_own, pay, pair, across,
            across_pair,
        ),
    )
    two_up = [(i, i + 2) for i in range(slab_count - 2)]
    two_down = [(j, i) for i, j in two_up]
    if ways == 1:
        passed = [lax.ppermute(beyond[0], "slab", two_up + two_down)]
    else:
        passed = [
            lax.ppermute(beyond[1], "slab", two_up), lax.ppermute(beyond[0], "slab", two_down)
        ]
    partial = tiles_call(
        1,
        tuple(whole(index) for index in range(6)),
        [across, across_pair, below_own, above_own, pay, pair],
        partial,
    )
    above_far, below_far, partial = lax.optimization_barrier((above_far, below_far, partial))
    below_last, above_last = mate_of(below_far, 1), mate_of(above_far, 1)
    far_rest, below_far = lax.optimization_barrier((far_rest, below_far))
    last_rest = mate_of(far_rest, 1)
    partial = tiles_call(
        2,
        (whole(0), whole(1), split_up(2, 4), split(3, 4, length - cut_up)),
        [below_pair, above_pair, below_far, above_far, far_rest],
        partial,
    )
    scale = (rows * (near_count + 1)) ** -0.5
    last = (split_up(0, 2), split(1, 2, length - cut_up))
    return call(
        functools.partial(last_kernel, kept, slots, rows, lat, 3, last, 3, ways, scale),
        "last",
        jax.ShapeDtypeStruct((OSLOTS * rows, lat), BF16),
        [SM, SM, SM, SM] + [VM] * (11 + ways),
        HB,
        [
            pltpu.VMEM(sums, F32),
            pltpu.VMEM((OSLOTS + 1, lat, rows), F32),
            pltpu.VMEM((OSLOTS + 1, 2 * lat, rows), BF16),
            pltpu.VMEM((OSLOTS, lat, rows), BF16),
            pltpu.VMEM((OSLOTS, rows, lat), BF16),
            pltpu.SemaphoreType.DMA((OSLOTS,)),
            *scratch_for(last),
        ],
        (
            target, tiles, counts, arrived, query, send_turned, in_turned, w_out, pay, below_own,
            above_own, partial, *passed, below_last, above_last, last_rest,
        ),
    )


def solution(mesh):
    placed = (
        P(("grp", "slab", "sub"), None),
        P(None, ("grp", "slab", "sub")),
        P(("grp", "slab", "sub")),
        P(("grp", "slab", "sub"), None),
        P(),
        P(),
        P(),
    )
    return jax.shard_map(
        on_device,
        mesh=mesh,
        in_specs=placed,
        out_specs=P(("grp", "slab", "sub"), None),
        check_vma=False,
    )
```

```python
import functools

import jax
import jax.numpy as jnp
from jax import lax
from jax.experimental import pallas as pl
from jax.experimental.pallas import tpu as pltpu
from jax.sharding import PartitionSpec as P

OSLOTS = 8
MATES = 4
GROUPS = (16, 8, 4)
FEW_GROUPS = (8, 4)
REST_UP, REST = 3, 2
INFO = 16
FEAT = 16
LOG2_SCALE = 0.7213475204444817
VMEM_LIMIT = 18 << 20
F32, BF16 = jnp.float32, jnp.bfloat16


def head_of(kept):
    return (3 * kept + 2 + 15) // 16 * 16


def mm(left, right, left_dim=1):
    dims = (((left_dim,), (0,)), ((), ()))
    return lax.dot_general(left, right, dims, preferred_element_type=F32)


def pieces(value):
    high = value.astype(BF16).astype(F32)
    rest = value - high
    middle = rest.astype(BF16).astype(F32)
    return high, middle, rest - middle


def put(terms, index, kept, value):
    for half in range(terms.shape[0]):
        terms[half, index * kept : index * kept + value.shape[0], :] = value[
            :, half * 128 : half * 128 + 128
        ]


def features(terms, index, kept):
    halves = [
        terms[half, pl.ds(index, FEAT, stride=kept), :].astype(BF16)
        for half in range(terms.shape[0])
    ]
    return jnp.concatenate(halves, axis=1)


def owner_of(out_slot):
    return lax.shift_right_arithmetic(out_slot, OSLOTS.bit_length() - 1)


def first_step():
    return 1 - 2 * (lax.axis_index("slab") % 2)


def places_of_partners():
    is_above = (first_step() + 1) // 2
    return is_above, 1 - is_above


def query_terms(terms, head, kept):
    rows = head.shape[1]
    total = jnp.zeros((kept, rows), F32)
    for axis in range(3):
        coord = head[axis * kept : axis * kept + kept, :]
        total = total + coord * coord
        for part, value in enumerate(pieces(coord * (2 * LOG2_SCALE))):
            put(terms, part * 3 + axis, kept, value)
    put(terms, 9, kept, jnp.ones((3 * kept, rows), F32))
    for part, value in enumerate(pieces(total * -LOG2_SCALE)):
        put(terms, 12 + part, kept, value)
    put(terms, 15, kept, jnp.zeros((kept, rows), F32))


def first_hole(target_ref, slots):
    hole = jnp.int32(slots - 1)
    for slot in reversed(range(slots)):
        hole = jnp.where(target_ref[slot] < 0, slot, hole)
    return hole


def slot_of(row, hole, kept, slots):
    return jnp.where(row == hole, slots - 1, row) if kept < slots else row


def call(kernel, name, out_shape, in_specs, out_specs, scratch, args, flops=0, limit=VMEM_LIMIT):
    return pl.pallas_call(
        kernel,
        name=name,
        out_shape=out_shape,
        in_specs=in_specs,
        out_specs=out_specs,
        scratch_shapes=scratch,
        compiler_params=pltpu.CompilerParams(vmem_limit_bytes=limit),
        cost_estimate=pl.CostEstimate(flops=flops, bytes_accessed=flops >> 9, transcendentals=0),
    )(*args)


VM = pl.BlockSpec(memory_space=pltpu.VMEM)
SM = pl.BlockSpec(memory_space=pltpu.SMEM)
HB = pl.BlockSpec(memory_space=pltpu.HBM)


def in_hbm(*arrays):
    return [pltpu.with_memory_space_constraint(array, pltpu.HBM) for array in arrays]


def pack_kernel(
    kept, slots, rows, target_in, near_in, latent, positions, pay, target, near, coords, head,
    blocks, sems,
):
    loads = [
        pltpu.make_async_copy(target_in, target, sems.at[slots + 1]),
        pltpu.make_async_copy(near_in, near, sems.at[slots + 2]),
    ]
    copies = [pltpu.make_async_copy(positions, coords, sems.at[slots])]
    for slot in range(slots):
        copies.append(
            pltpu.make_async_copy(
                latent.at[slot * rows : slot * rows + rows, :], blocks.at[slot], sems.at[slot]
            )
        )
    for copy in (*loads, *copies):
        copy.start()
    for load in loads:
        load.wait()
    hole = first_hole(target, slots)
    sub_count = lax.axis_size("sub")
    my_slab = lax.axis_index("slab")
    me = my_slab * sub_count + lax.axis_index("sub")
    lane = lax.broadcasted_iota(jnp.int32, (1, rows), 1)
    info = jnp.zeros((1, rows), jnp.int32)
    for side, device in enumerate((me + sub_count, me - sub_count)):
        tag, moving = jnp.int32(0), jnp.int32(0)
        for slot in range(slots):
            out_slot = target[slot]
            goes = (out_slot >= 0) & (owner_of(out_slot) == device)
            tag = jnp.where(goes, out_slot - device * OSLOTS + 1, tag)
            moving = jnp.where(goes, slot, moving)
        row = jnp.where(moving == slots - 1, hole, moving) if kept < slots else moving
        words = [tag, row] + [
            near[k, moving] - (my_slab - 1) * sub_count * slots for k in range(near.shape[0])
        ]
        for place, word in enumerate(words):
            info = jnp.where(lane == side * INFO + place, word, info)
    head[...] = jnp.zeros_like(head)
    head[pl.ds(3 * kept, 1), :] = jnp.full((1, rows), hole.astype(F32))
    head[pl.ds(3 * kept + 1, 1), :] = info.astype(F32)
    copies[0].wait()
    for row in range(kept):
        start = pl.multiple_of(slot_of(row, hole, kept, slots) * rows, rows)
        block = coords[:, pl.ds(start, rows)].astype(F32)
        for axis in range(3):
            head[pl.ds(axis * kept + row, 1), :] = block[axis : axis + 1, :]
    pay[0:head_of(kept), :] = head[...].astype(BF16)
    lat = latent.shape[1]
    if kept < slots:
        copies[slots].wait()
    for row in range(kept):
        copies[1 + row].wait()
        block = blocks[slot_of(row, hole, kept, slots)]
        start = head_of(kept) + row * lat
        pay[start : start + lat, :] = jnp.transpose(block)


def plan_kernel(
    kept, slots, rows, homes, phases, target_in, near_in, pay, w_send_in, w_in_in, tiles, counts,
    query, send_turned, in_turned, target, near, w_send, w_in, terms, sems,
):
    loads = [
        pltpu.make_async_copy(source, ref, sems.at[index])
        for index, (source, ref) in enumerate(
            ((target_in, target), (near_in, near), (w_send_in, w_send), (w_in_in, w_in))
        )
    ]
    for load in loads:
        load.start()
    query_terms(terms, pay[0 : head_of(kept), :].astype(F32), kept)
    for load in loads:
        load.wait()
    lat = w_send.shape[0]
    send_turned[:, 0:lat] = jnp.transpose(w_send[:, 0:lat])
    send_turned[:, lat : 2 * lat] = jnp.transpose(w_send[:, lat : 2 * lat])
    in_turned[...] = jnp.transpose(w_in[...])
    hole = first_hole(target, slots)
    sub_count, slab_count = lax.axis_size("sub"), lax.axis_size("slab")
    my_slab, my_sub = lax.axis_index("slab"), lax.axis_index("sub")
    limit = slab_count * sub_count * slots
    inverse = 65536 // slots + 1
    if any(i * inverse >> 16 != i // slots for i in range(limit)):
        raise ValueError("slot ids")
    words = [sum(home << (6 * i) for i, home in enumerate(homes[at : at + 4])) for at in (0, 4, 8)]
    for phase in range(phases):
        counts[phase] = 0

    def add(phase, entry):
        place = counts[phase]
        tiles[phase, place] = entry
        counts[phase] = place + 1

    me = my_slab * sub_count + my_sub
    first = first_step()
    for row in range(kept):
        out_slot = target[slot_of(row, hole, kept, slots)]
        own = jnp.where(owner_of(out_slot) == me, out_slot - me * OSLOTS, OSLOTS)
        query[own] = features(terms, row, kept)

    def per_slot(slot, carry):
        out_slot = target[slot]
        own = (out_slot - me * OSLOTS) * 256

        @pl.when(owner_of(out_slot) == me)
        def _():
            add(homes[MATES] // 8, own + homes[MATES] % 8 * 16 + slot)
            for k in range(near.shape[0]):
                other = near[k, slot]
                device = lax.shift_right_logical(other * inverse, 16)
                step = device // sub_count - my_slab
                word = jnp.where(step == first, words[0], jnp.where(step == 0, words[1], words[2]))
                home = lax.shift_right_logical(word, 6 * jnp.bitwise_xor(device % sub_count, my_sub))
                phase = jnp.bitwise_and(lax.shift_right_logical(home, 3), 7)
                line = jnp.bitwise_and(home, 7)
                add(phase, own + line * 16 + other - device * slots)

        return carry

    lax.fori_loop(0, slots, per_slot, 0)
    for phase in range(phases):
        for extra in range(GROUPS[0]):
            tiles[phase, counts[phase] + extra] = OSLOTS * 256


def gather_tiles(
    kept, slots, rows, lat, phase, tiles, counts, query, lines, acc, scratch, groups=GROUPS
):
    land, feats, terms, holes = scratch
    for line, parts in enumerate(lines):
        at = 0
        for ref, start, length in parts:
            land[line, at : at + length, :] = ref[start : start + length, :]
            at += length
    put(terms, 12, kept, jnp.ones((3 * kept, rows), F32))
    put(terms, 15, kept, jnp.zeros((kept, rows), F32))
    for line, parts in enumerate(lines):
        head = parts[0][0][0 : head_of(kept), :].astype(F32)
        holes[line] = jnp.max(head[3 * kept : 3 * kept + 1, :]).astype(jnp.int32)
        total = jnp.zeros((kept, rows), F32)
        for axis in range(3):
            coord = head[axis * kept : axis * kept + kept, :]
            total = total + coord * coord
            for part in range(3):
                put(terms, part * 3 + axis, kept, coord)
        for part, value in enumerate(pieces(total * -LOG2_SCALE)):
            put(terms, 9 + part, kept, value)
        for block in range(kept):
            feats[line * kept + block] = features(terms, block, kept)

    def work(first, size):
        owns, exponents, sources = [], [], []
        for step in range(size):
            entry = tiles[phase, first + step]
            own = lax.shift_right_logical(entry, 8)
            line = jnp.bitwise_and(lax.shift_right_logical(entry, 4), 15)
            slot = jnp.bitwise_and(entry, 15)
            block = jnp.where(slot == kept, holes[line], slot) if kept < slots else slot
            owns.append(own)
            begin = pl.multiple_of(head_of(kept) + block * lat, 16)
            sources.append(land[line, pl.ds(begin, lat), :])
            exponents.append(
                mm(feats[line * kept + block], query[own], left_dim=0)
            )
        results = []
        for exponent, source in zip(exponents, sources):
            wide = jnp.exp2(exponent)
            square = wide * wide
            results.append(
                (mm(source, wide.astype(BF16)), mm(source, (square * square).astype(BF16)))
            )
        for own, (first, second) in zip(owns, results):
            acc[own, 0:lat] += first
            acc[own, lat : 2 * lat] += second

    large, count = groups[0], counts[phase]
    small = groups[1] if len(groups) > 1 else 0
    whole = (count + large - 1 - small) // large
    lax.fori_loop(0, whole, lambda group, carry: work(group * large, large), None)
    left = count - whole * large
    for size, below in zip(groups[1:], (*groups[2:], 0)):
        pl.when((left > below) & (left <= size))(functools.partial(work, whole * large, size))


def lines_of(refs, parts):
    return [[(refs[index], start, length) for index, start, length in line] for line in parts]


def tiles_kernel(kept, slots, rows, lat, phase, parts, ref_count, has_earlier, tiles, counts, query, *rest):
    earlier, rest = (rest[0], rest[1:]) if has_earlier else (None, rest)
    lines, (acc, *scratch) = lines_of(rest, parts), rest[ref_count:]
    if has_earlier:
        acc[...] = earlier[...]
    else:
        acc[...] = jnp.zeros_like(acc)
    gather_tiles(kept, slots, rows, lat, phase, tiles, counts, query, lines, acc, scratch)


def arrivals_kernel(
    kept, slots, rows, lat, homes, phases, parts, ref_count, tiles_in, counts_in, query_in,
    send_turned, first, second, *rest,
):
    refs, rest = rest[:ref_count], rest[ref_count:]
    tiles, counts, query, arrived, beyond, acc, few, few_counts, few_query, *scratch = rest
    terms = scratch[2]
    my_sub = lax.axis_index("sub")
    query[...] = query_in[...]
    for phase in range(phases):
        count = counts_in[phase]
        counts[phase] = count

        def keep(place, carry, phase=phase):
            tiles[phase, place] = tiles_in[phase, place]
            return carry

        lax.fori_loop(0, count, keep, 0)
    few_counts[0] = 0

    def add(phase, entry):
        place = counts[phase]
        tiles[phase, place] = entry
        counts[phase] = place + 1

    def word_of(words, mate):
        return lax.shift_right_logical(words, 6 * mate)

    near_count = INFO // 2
    plane = MATES * slots
    inverse = 65536 // slots + 1
    own_words = sum(home << (6 * i) for i, home in enumerate((12, 13, 8, 9)))
    below_place, above_place = places_of_partners()
    for index, ref in enumerate((first, second)):
        side = jnp.where(below_place == index, 0, 1)
        head = ref[0 : head_of(kept), :].astype(F32)
        query_terms(terms, head, kept)
        info = head[3 * kept + 1 : 3 * kept + 2, :]
        lane = lax.broadcasted_iota(jnp.int32, info.shape, 1)

        def read(place, info=info, lane=lane):
            return jnp.sum(jnp.where(lane == place, info, 0.0)).astype(jnp.int32)

        tag, row = read(side * INFO), read(side * INFO + 1)
        codes = [read(side * INFO + 2 + k) for k in range(near_count)]
        own = jnp.where(tag > 0, tag - 1, OSLOTS)
        arrived[2 * index] = own
        arrived[2 * index + 1] = row
        query[own] = features(terms, row, kept)
        line_words = sum(home << (6 * i) for i, home in enumerate(homes[8 * index : 8 * index + 4]))

        @pl.when(tag > 0)
        def _(own=own, row=row, codes=codes, side=side, index=index, line_words=line_words):
            home = homes[8 * index]
            add(home // 8, own * 256 + home % 8 * 16 + row)
            for code in codes:
                device = lax.shift_right_logical(code * inverse, 16)
                slot = code - device * slots
                mate = jnp.bitwise_xor(jnp.bitwise_and(device, MATES - 1), my_sub)
                step = lax.shift_right_logical(device, 2) - 1
                word = jnp.where(step == 0, word_of(line_words, mate), word_of(own_words, mate))
                phase = jnp.bitwise_and(lax.shift_right_logical(word, 3), 7)
                line = jnp.bitwise_and(word, 7)

                @pl.when(step != 2 * side - 1)
                def _(phase=phase, line=line, slot=slot):
                    add(phase, own * 256 + line * 16 + slot)

        other = 1 - side
        tag, row = read(other * INFO), read(other * INFO + 1)
        codes = [read(other * INFO + 2 + k) for k in range(near_count)]
        few_query[index] = features(terms, row, kept)

        @pl.when(tag > 0)
        def _(codes=codes, side=side, index=index):
            for code in codes:
                device = lax.shift_right_logical(code * inverse, 16)
                slot = code - device * slots
                mate = jnp.bitwise_xor(jnp.bitwise_and(device, MATES - 1), my_sub)
                step = lax.shift_right_logical(device, 2) - 1

                @pl.when(step == 1 - 2 * side)
                def _(slot=slot, mate=mate, index=index):
                    place = few_counts[0]
                    few[0, place] = index * 256 + mate * 16 + slot
                    few_counts[0] = place + 1

    few_query[2] = few_query[0]
    for extra in range(GROUPS[0]):
        few[0, few_counts[0] + extra] = 2 * 256
        for phase in range(phases):
            tiles[phase, counts[phase] + extra] = OSLOTS * 256
    acc[...] = jnp.zeros_like(acc)
    gather_tiles(
        kept, slots, rows, lat, 0, few, few_counts, few_query, lines_of(refs, parts), acc, scratch,
        FEW_GROUPS,
    )
    if beyond.shape[0] == 1:
        upper = lax.axis_index("slab") * 2 >= lax.axis_size("slab")
        chosen = [jnp.where(upper, below_place, above_place)]
    else:
        chosen = [below_place, above_place]
    for place, index in enumerate(chosen):
        beyond[place] = mm(send_turned[...], acc[index].astype(BF16)).astype(BF16)


def last_kernel(
    kept, slots, rows, lat, phase, parts, ref_count, ways, scale, target, tiles, counts, arrived, query,
    send_turned, in_turned, w_out, pay, first, second, earlier, *rest,
):
    passed, rest = rest[:ways], rest[ways:]
    lines, rest = lines_of(rest, parts), rest[ref_count:]
    out, acc, sums, joined, hidden, updated, stores, *scratch = rest
    acc[...] = earlier[...]
    gather_tiles(kept, slots, rows, lat, phase, tiles, counts, query, lines, acc, scratch)
    hole = first_hole(target, slots)
    me = lax.axis_index("slab") * lax.axis_size("sub") + lax.axis_index("sub")
    for row in range(kept):
        out_slot = target[slot_of(row, hole, kept, slots)]
        own = jnp.where(owner_of(out_slot) == me, out_slot - me * OSLOTS, OSLOTS)
        start = head_of(kept) + row * lat
        joined[own, 0:lat, :] = pay[start : start + lat, :]
    for index, ref in enumerate((first, second)):
        start = pl.multiple_of(head_of(kept) + arrived[2 * index + 1] * lat, 16)
        joined[arrived[2 * index], 0:lat, :] = ref[pl.ds(start, lat), :]
    for own in range(OSLOTS):
        sums[own] = mm(send_turned[...], acc[own].astype(BF16))
    below_place, above_place = places_of_partners()
    if ways == 1:
        upper = lax.axis_index("slab") * 2 >= lax.axis_size("slab")
        chosen = [jnp.where(upper, below_place, above_place)]
    else:
        chosen = [below_place, above_place]
    for index, ref in zip(chosen, passed):
        sums[arrived[2 * index]] += ref[...].astype(F32)
    for own in range(OSLOTS):
        joined[own, lat : 2 * lat, :] = (sums[own] * scale).astype(BF16)
    for own in range(OSLOTS):
        before = mm(in_turned[...], joined[own])
        hidden[own] = (before * (0.5 + 0.5 * jnp.tanh(0.5 * before))).astype(BF16)
    copies = []
    for own in range(OSLOTS):
        change = mm(hidden[own], w_out[...], left_dim=0)
        old = jnp.transpose(joined[own, 0:lat, :])
        updated[own] = (old.astype(F32) + change).astype(BF16)
        copies.append(
            pltpu.make_async_copy(
                updated.at[own], out.at[own * rows : own * rows + rows, :], stores.at[own]
            )
        )
        copies[-1].start()
    for copy in copies:
        copy.wait()


def on_device(latent, positions, target, neighbours, w_send, w_in, w_out):
    lat = latent.shape[1]
    slots = target.shape[0]
    rows = latent.shape[0] // slots
    near_count = neighbours.shape[1]
    slab_count = lax.axis_size("slab")
    kept = slots - 1 if slab_count <= 4 else slots
    length = head_of(kept) + kept * lat
    if lax.axis_size("sub") != MATES:
        raise ValueError("sizes")
    pairs = [[(i, i + 1) for i in range(begin, slab_count - 1, 2)] for begin in (0, 1)]
    pairs = [some + [(j, i) for i, j in some] for some in pairs]
    def mate_of(value, bit):
        return lax.ppermute(value, "sub", [(i, i ^ bit) for i in range(MATES)])

    def swap_first(value):
        return lax.ppermute(value, "slab", pairs[0])

    def swap_second(value):
        return lax.ppermute(value, "slab", pairs[1])

    cut_up, cut = length - REST_UP * lat, length - REST * lat
    pay = call(
        functools.partial(pack_kernel, kept, slots, rows),
        "pack",
        jax.ShapeDtypeStruct((length, rows), BF16),
        [HB, HB, HB, HB],
        VM,
        [
            pltpu.SMEM((slots,), jnp.int32),
            pltpu.SMEM((near_count, slots), jnp.int32),
            pltpu.VMEM(positions.shape, BF16),
            pltpu.VMEM((head_of(kept), rows), F32),
            pltpu.VMEM((slots, rows, lat), BF16),
            pltpu.SemaphoreType.DMA((slots + 3,)),
        ],
        in_hbm(target, neighbours.T, latent, positions),
    )
    across = mate_of(pay, 2)
    first_own, second_own = swap_first(pay), swap_second(pay)
    pair = mate_of(pay, 1)

    homes = (10, 16, 18, 24, 0, 1, 8, 9, 11, 17, 19, 25)
    phase_count = 4
    most = OSLOTS * (near_count + 1) + GROUPS[0]
    tiles, counts, query, send_turned, in_turned = call(
        functools.partial(plan_kernel, kept, slots, rows, homes, phase_count),
        "plan",
        (
            jax.ShapeDtypeStruct((phase_count, most), jnp.int32),
            jax.ShapeDtypeStruct((phase_count,), jnp.int32),
            jax.ShapeDtypeStruct((OSLOTS + 1, FEAT, rows), BF16),
            jax.ShapeDtypeStruct((lat, 2 * lat), BF16),
            jax.ShapeDtypeStruct((lat, 2 * lat), BF16),
        ),
        [HB, HB, VM, HB, HB],
        (SM, SM, VM, VM, VM),
        [
            pltpu.SMEM((slots,), jnp.int32),
            pltpu.SMEM((near_count, slots), jnp.int32),
            pltpu.VMEM(w_send.shape, BF16),
            pltpu.VMEM(w_in.shape, BF16),
            pltpu.VMEM((rows // 128, FEAT * kept, 128), F32),
            pltpu.SemaphoreType.DMA((4,)),
        ],
        (*in_hbm(target, neighbours.T), pay, *in_hbm(w_send, w_in)),
    )

    def scratch_for(parts):
        return [
            pltpu.VMEM((len(parts), length, rows), BF16),
            pltpu.VMEM((len(parts) * kept, FEAT, rows), BF16),
            pltpu.VMEM((rows // 128, FEAT * kept, 128), F32),
            pltpu.SMEM((len(parts),), jnp.int32),
        ]

    sums = (OSLOTS + 1, 2 * lat, rows)
    whole = lambda index: ((index, 0, length),)
    split = lambda index, other, start=0: ((index, 0, cut), (other, start, length - cut))
    split_up = lambda index, other: ((index, 0, cut_up), (other, 0, length - cut_up))

    def tiles_call(phase, parts, refs, earlier):
        earlier = [] if earlier is None else [earlier]
        return call(
            functools.partial(
                tiles_kernel, kept, slots, rows, lat, phase, parts, len(refs), bool(earlier)
            ),
            f"tiles{phase}",
            jax.ShapeDtypeStruct(sums, F32),
            [SM, SM, VM] + [VM] * (len(earlier) + len(refs)),
            VM,
            scratch_for(parts),
            (tiles, counts, query, *earlier, *refs),
        )

    partial = tiles_call(0, (whole(0), whole(1)), [pay, pair], None)
    across, partial = lax.optimization_barrier((across, partial))
    second_far, first_far = swap_second(across[:cut]), swap_first(across[:cut_up])
    across_pair = mate_of(across, 1)
    far_rest = mate_of(jnp.concatenate([first_own[cut_up:], second_own[cut:]], axis=0), 2)
    first_pair, second_pair = mate_of(first_own, 1), mate_of(second_own, 1)
    ways = 1 if slab_count <= 4 else 2
    tiles, counts, query, arrived, beyond = call(
        functools.partial(
            arrivals_kernel, kept, slots, rows, lat, homes, phase_count,
            tuple(whole(index) for index in range(4)), 4,
        ),
        "arrivals",
        (
            jax.ShapeDtypeStruct((phase_count, most), jnp.int32),
            jax.ShapeDtypeStruct((phase_count,), jnp.int32),
            jax.ShapeDtypeStruct((OSLOTS + 1, FEAT, rows), BF16),
            jax.ShapeDtypeStruct((4,), jnp.int32),
            jax.ShapeDtypeStruct((ways, lat, rows), BF16),
        ),
        [SM, SM] + [VM] * 8,
        (SM, SM, VM, SM, VM),
        [
            pltpu.VMEM((3, 2 * lat, rows), F32),
            pltpu.SMEM((1, 2 * near_count + GROUPS[0]), jnp.int32),
            pltpu.SMEM((1,), jnp.int32),
            pltpu.VMEM((3, FEAT, rows), BF16),
            *scratch_for(range(4)),
        ],
        (
            tiles, counts, query, send_turned, first_own, second_own, pay, pair, across,
            across_pair,
        ),
    )
    two_up = [(i, i + 2) for i in range(slab_count - 2)]
    two_down = [(j, i) for i, j in two_up]
    if ways == 1:
        passed = [lax.ppermute(beyond[0], "slab", two_up + two_down)]
    else:
        passed = [
            lax.ppermute(beyond[1], "slab", two_up), lax.ppermute(beyond[0], "slab", two_down)
        ]
    partial = tiles_call(
        1,
        tuple(whole(index) for index in range(6)),
        [across, across_pair, first_own, second_own, pay, pair],
        partial,
    )
    second_far, first_far, partial = lax.optimization_barrier((second_far, first_far, partial))
    first_last, second_last = mate_of(first_far, 1), mate_of(second_far, 1)
    far_rest, first_far = lax.optimization_barrier((far_rest, first_far))
    last_rest = mate_of(far_rest, 1)
    partial = tiles_call(
        2,
        (whole(0), whole(1), split_up(2, 4), split(3, 4, length - cut_up)),
        [first_pair, second_pair, first_far, second_far, far_rest],
        partial,
    )
    scale = (rows * (near_count + 1)) ** -0.5
    last = (split_up(0, 2), split(1, 2, length - cut_up))
    return call(
        functools.partial(last_kernel, kept, slots, rows, lat, 3, last, 3, ways, scale),
        "last",
        jax.ShapeDtypeStruct((OSLOTS * rows, lat), BF16),
        [SM, SM, SM, SM] + [VM] * (11 + ways),
        HB,
        [
            pltpu.VMEM(sums, F32),
            pltpu.VMEM((OSLOTS + 1, lat, rows), F32),
            pltpu.VMEM((OSLOTS + 1, 2 * lat, rows), BF16),
            pltpu.VMEM((OSLOTS, lat, rows), BF16),
            pltpu.VMEM((OSLOTS, rows, lat), BF16),
            pltpu.SemaphoreType.DMA((OSLOTS,)),
            *scratch_for(last),
        ],
        (
            target, tiles, counts, arrived, query, send_turned, in_turned, w_out, pay, first_own,
            second_own, partial, *passed, first_last, second_last, last_rest,
        ),
    )


def solution(mesh):
    placed = (
        P(("grp", "slab", "sub"), None),
        P(None, ("grp", "slab", "sub")),
        P(("grp", "slab", "sub")),
        P(("grp", "slab", "sub"), None),
        P(),
        P(),
        P(),
    )
    return jax.shard_map(
        on_device,
        mesh=mesh,
        in_specs=placed,
        out_specs=P(("grp", "slab", "sub"), None),
        check_vma=False,
    )
```

```python
import functools

import jax
import jax.numpy as jnp
from jax import lax
from jax.experimental import pallas as pl
from jax.experimental.pallas import tpu as pltpu
from jax.sharding import PartitionSpec as P

OSLOTS = 8
MATES = 4
GROUPS = (16, 8, 4)
FEW_GROUPS = (8, 4)
REST_UP, REST = 3, 3
INFO = 16
FEAT = 16
LOG2_SCALE = 0.7213475204444817
VMEM_LIMIT = 18 << 20
F32, BF16 = jnp.float32, jnp.bfloat16


def head_of(kept):
    return (3 * kept + 2 + 15) // 16 * 16


def mm(left, right, left_dim=1):
    dims = (((left_dim,), (0,)), ((), ()))
    return lax.dot_general(left, right, dims, preferred_element_type=F32)


def pieces(value):
    high = value.astype(BF16).astype(F32)
    rest = value - high
    middle = rest.astype(BF16).astype(F32)
    return high, middle, rest - middle


def put(terms, index, kept, value):
    for half in range(terms.shape[0]):
        terms[half, index * kept : index * kept + value.shape[0], :] = value[
            :, half * 128 : half * 128 + 128
        ]


def features(terms, index, kept):
    halves = [
        terms[half, pl.ds(index, FEAT, stride=kept), :].astype(BF16)
        for half in range(terms.shape[0])
    ]
    return jnp.concatenate(halves, axis=1)


def owner_of(out_slot):
    return lax.shift_right_arithmetic(out_slot, OSLOTS.bit_length() - 1)


def first_step():
    return 1 - 2 * (lax.axis_index("slab") % 2)


def places_of_partners():
    is_above = (first_step() + 1) // 2
    return is_above, 1 - is_above


def query_terms(terms, head, kept):
    rows = head.shape[1]
    total = jnp.zeros((kept, rows), F32)
    for axis in range(3):
        coord = head[axis * kept : axis * kept + kept, :]
        total = total + coord * coord
        for part, value in enumerate(pieces(coord * (2 * LOG2_SCALE))):
            put(terms, part * 3 + axis, kept, value)
    put(terms, 9, kept, jnp.ones((3 * kept, rows), F32))
    for part, value in enumerate(pieces(total * -LOG2_SCALE)):
        put(terms, 12 + part, kept, value)
    put(terms, 15, kept, jnp.zeros((kept, rows), F32))


def first_hole(target_ref, slots):
    hole = jnp.int32(slots - 1)
    for slot in reversed(range(slots)):
        hole = jnp.where(target_ref[slot] < 0, slot, hole)
    return hole


def slot_of(row, hole, kept, slots):
    return jnp.where(row == hole, slots - 1, row) if kept < slots else row


def call(kernel, name, out_shape, in_specs, out_specs, scratch, args, flops=0, limit=VMEM_LIMIT):
    return pl.pallas_call(
        kernel,
        name=name,
        out_shape=out_shape,
        in_specs=in_specs,
        out_specs=out_specs,
        scratch_shapes=scratch,
        compiler_params=pltpu.CompilerParams(vmem_limit_bytes=limit),
        cost_estimate=pl.CostEstimate(flops=flops, bytes_accessed=flops >> 9, transcendentals=0),
    )(*args)


VM = pl.BlockSpec(memory_space=pltpu.VMEM)
SM = pl.BlockSpec(memory_space=pltpu.SMEM)
HB = pl.BlockSpec(memory_space=pltpu.HBM)
AN = pl.BlockSpec(memory_space=pl.ANY)


def in_hbm(*arrays):
    return [pltpu.with_memory_space_constraint(array, pltpu.HBM) for array in arrays]


def pack_kernel(
    kept, slots, rows, target_in, near_in, latent, positions, pay, target, near, coords, head,
    blocks, sems,
):
    loads = [
        pltpu.make_async_copy(target_in, target, sems.at[slots + 1]),
        pltpu.make_async_copy(near_in, near, sems.at[slots + 2]),
    ]
    copies = [pltpu.make_async_copy(positions, coords, sems.at[slots])]
    for slot in range(slots):
        copies.append(
            pltpu.make_async_copy(
                latent.at[slot * rows : slot * rows + rows, :], blocks.at[slot], sems.at[slot]
            )
        )
    for copy in (*loads, *copies):
        copy.start()
    for load in loads:
        load.wait()
    hole = first_hole(target, slots)
    sub_count = lax.axis_size("sub")
    my_slab = lax.axis_index("slab")
    me = my_slab * sub_count + lax.axis_index("sub")
    lane = lax.broadcasted_iota(jnp.int32, (1, rows), 1)
    info = jnp.zeros((1, rows), jnp.int32)
    for side, device in enumerate((me + sub_count, me - sub_count)):
        tag, moving = jnp.int32(0), jnp.int32(0)
        for slot in range(slots):
            out_slot = target[slot]
            goes = (out_slot >= 0) & (owner_of(out_slot) == device)
            tag = jnp.where(goes, out_slot - device * OSLOTS + 1, tag)
            moving = jnp.where(goes, slot, moving)
        row = jnp.where(moving == slots - 1, hole, moving) if kept < slots else moving
        words = [tag, row] + [
            near[k, moving] - (my_slab - 1) * sub_count * slots for k in range(near.shape[0])
        ]
        for place, word in enumerate(words):
            info = jnp.where(lane == side * INFO + place, word, info)
    head[...] = jnp.zeros_like(head)
    head[pl.ds(3 * kept, 1), :] = jnp.full((1, rows), hole.astype(F32))
    head[pl.ds(3 * kept + 1, 1), :] = info.astype(F32)
    copies[0].wait()
    for row in range(kept):
        start = pl.multiple_of(slot_of(row, hole, kept, slots) * rows, rows)
        block = coords[:, pl.ds(start, rows)].astype(F32)
        for axis in range(3):
            head[pl.ds(axis * kept + row, 1), :] = block[axis : axis + 1, :]
    pay[0:head_of(kept), :] = head[...].astype(BF16)
    lat = latent.shape[1]
    if kept < slots:
        copies[slots].wait()
    for row in range(kept):
        copies[1 + row].wait()
        block = blocks[slot_of(row, hole, kept, slots)]
        start = head_of(kept) + row * lat
        pay[start : start + lat, :] = jnp.transpose(block)


def plan_kernel(
    kept, slots, rows, homes, phases, target_in, near_in, pay, w_send_in, w_in_in, tiles, counts,
    query, send_turned, in_turned, target, near, w_send, w_in, terms, sems,
):
    loads = [
        pltpu.make_async_copy(source, ref, sems.at[index])
        for index, (source, ref) in enumerate(
            ((target_in, target), (near_in, near), (w_send_in, w_send), (w_in_in, w_in))
        )
    ]
    for load in loads:
        load.start()
    query_terms(terms, pay[0 : head_of(kept), :].astype(F32), kept)
    for load in loads:
        load.wait()
    lat = w_send.shape[0]
    send_turned[:, 0:lat] = jnp.transpose(w_send[:, 0:lat])
    send_turned[:, lat : 2 * lat] = jnp.transpose(w_send[:, lat : 2 * lat])
    in_turned[...] = jnp.transpose(w_in[...])
    hole = first_hole(target, slots)
    sub_count, slab_count = lax.axis_size("sub"), lax.axis_size("slab")
    my_slab, my_sub = lax.axis_index("slab"), lax.axis_index("sub")
    limit = slab_count * sub_count * slots
    inverse = 65536 // slots + 1
    if any(i * inverse >> 16 != i // slots for i in range(limit)):
        raise ValueError("slot ids")
    words = [sum(home << (6 * i) for i, home in enumerate(homes[at : at + 4])) for at in (0, 4, 8)]
    for phase in range(phases):
        counts[phase] = 0

    def add(phase, entry):
        place = counts[phase]
        tiles[phase, place] = entry
        counts[phase] = place + 1

    me = my_slab * sub_count + my_sub
    first = first_step()
    for row in range(kept):
        out_slot = target[slot_of(row, hole, kept, slots)]
        own = jnp.where(owner_of(out_slot) == me, out_slot - me * OSLOTS, OSLOTS)
        query[own] = features(terms, row, kept)

    def per_slot(slot, carry):
        out_slot = target[slot]
        own = (out_slot - me * OSLOTS) * 256

        @pl.when(owner_of(out_slot) == me)
        def _():
            add(homes[MATES] // 8, own + homes[MATES] % 8 * 16 + slot)
            for k in range(near.shape[0]):
                other = near[k, slot]
                device = lax.shift_right_logical(other * inverse, 16)
                step = device // sub_count - my_slab
                word = jnp.where(step == first, words[0], jnp.where(step == 0, words[1], words[2]))
                home = lax.shift_right_logical(word, 6 * jnp.bitwise_xor(device % sub_count, my_sub))
                phase = jnp.bitwise_and(lax.shift_right_logical(home, 3), 7)
                line = jnp.bitwise_and(home, 7)
                add(phase, own + line * 16 + other - device * slots)

        return carry

    lax.fori_loop(0, slots, per_slot, 0)
    for phase in range(phases):
        for extra in range(GROUPS[0]):
            tiles[phase, counts[phase] + extra] = OSLOTS * 256


def gather_tiles(
    kept, slots, rows, lat, phase, tiles, counts, query, lines, acc, scratch, groups=GROUPS,
    ready=lambda: None,
):
    land, feats, terms, holes = scratch
    for line, parts in enumerate(lines):
        at = 0
        for ref, start, length in parts:
            land[line, at : at + length, :] = ref[start : start + length, :]
            at += length
    put(terms, 12, kept, jnp.ones((3 * kept, rows), F32))
    put(terms, 15, kept, jnp.zeros((kept, rows), F32))
    for line, parts in enumerate(lines):
        head = parts[0][0][0 : head_of(kept), :].astype(F32)
        holes[line] = jnp.max(head[3 * kept : 3 * kept + 1, :]).astype(jnp.int32)
        total = jnp.zeros((kept, rows), F32)
        for axis in range(3):
            coord = head[axis * kept : axis * kept + kept, :]
            total = total + coord * coord
            for part in range(3):
                put(terms, part * 3 + axis, kept, coord)
        for part, value in enumerate(pieces(total * -LOG2_SCALE)):
            put(terms, 9 + part, kept, value)
        for block in range(kept):
            feats[line * kept + block] = features(terms, block, kept)

    ready()

    def work(first, size):
        owns, exponents, sources = [], [], []
        for step in range(size):
            entry = tiles[phase, first + step]
            own = lax.shift_right_logical(entry, 8)
            line = jnp.bitwise_and(lax.shift_right_logical(entry, 4), 15)
            slot = jnp.bitwise_and(entry, 15)
            block = jnp.where(slot == kept, holes[line], slot) if kept < slots else slot
            owns.append(own)
            begin = pl.multiple_of(head_of(kept) + block * lat, 16)
            sources.append(land[line, pl.ds(begin, lat), :])
            exponents.append(
                mm(feats[line * kept + block], query[own], left_dim=0)
            )
        results = []
        for exponent, source in zip(exponents, sources):
            wide = jnp.exp2(exponent)
            square = wide * wide
            results.append(
                (mm(source, wide.astype(BF16)), mm(source, (square * square).astype(BF16)))
            )
        for own, (first, second) in zip(owns, results):
            acc[own, 0:lat] += first
            acc[own, lat : 2 * lat] += second

    large, count = groups[0], counts[phase]
    small = groups[1] if len(groups) > 1 else 0
    whole = (count + large - 1 - small) // large
    lax.fori_loop(0, whole, lambda group, carry: work(group * large, large), None)
    left = count - whole * large
    for size, below in zip(groups[1:], (*groups[2:], 0)):
        pl.when((left > below) & (left <= size))(functools.partial(work, whole * large, size))


def lines_of(refs, parts):
    return [[(refs[index], start, length) for index, start, length in line] for line in parts]


def to_smem(pairs, sems):
    copies = [
        pltpu.make_async_copy(source, ref, sems.at[index])
        for index, (source, ref) in enumerate(pairs)
    ]
    for copy in copies:
        copy.start()

    def ready():
        for copy in copies:
            copy.wait()

    return ready


def tiles_kernel(
    kept, slots, rows, lat, phase, parts, ref_count, has_earlier, tiles_in, counts_in, query, *rest
):
    earlier, rest = (rest[0], rest[1:]) if has_earlier else (None, rest)
    lines, (acc, tiles, counts, sems, *scratch) = lines_of(rest, parts), rest[ref_count:]
    ready = to_smem(((tiles_in, tiles), (counts_in, counts)), sems)
    if has_earlier:
        acc[...] = earlier[...]
    else:
        acc[...] = jnp.zeros_like(acc)
    gather_tiles(
        kept, slots, rows, lat, phase, tiles, counts, query, lines, acc, scratch, ready=ready
    )


def arrivals_kernel(
    kept, slots, rows, lat, homes, phases, parts, ref_count, tiles_in, counts_in, query_in,
    send_turned, first, second, *rest,
):
    refs, rest = rest[:ref_count], rest[ref_count:]
    tiles, counts, query, arrived, beyond, acc, few, few_counts, few_query, *scratch = rest
    terms = scratch[2]
    my_sub = lax.axis_index("sub")
    query[...] = query_in[...]
    for phase in range(phases):
        count = counts_in[phase]
        counts[phase] = count

        def keep(place, carry, phase=phase):
            tiles[phase, place] = tiles_in[phase, place]
            return carry

        lax.fori_loop(0, count, keep, 0)
    few_counts[0] = 0

    def add(phase, entry):
        place = counts[phase]
        tiles[phase, place] = entry
        counts[phase] = place + 1

    def word_of(words, mate):
        return lax.shift_right_logical(words, 6 * mate)

    near_count = INFO // 2
    plane = MATES * slots
    inverse = 65536 // slots + 1
    own_words = sum(home << (6 * i) for i, home in enumerate((12, 13, 8, 9)))
    below_place, above_place = places_of_partners()
    for index, ref in enumerate((first, second)):
        side = jnp.where(below_place == index, 0, 1)
        head = ref[0 : head_of(kept), :].astype(F32)
        query_terms(terms, head, kept)
        info = head[3 * kept + 1 : 3 * kept + 2, :]
        lane = lax.broadcasted_iota(jnp.int32, info.shape, 1)

        def read(place, info=info, lane=lane):
            return jnp.sum(jnp.where(lane == place, info, 0.0)).astype(jnp.int32)

        tag, row = read(side * INFO), read(side * INFO + 1)
        codes = [read(side * INFO + 2 + k) for k in range(near_count)]
        own = jnp.where(tag > 0, tag - 1, OSLOTS)
        arrived[2 * index] = own
        arrived[2 * index + 1] = row
        query[own] = features(terms, row, kept)
        line_words = sum(home << (6 * i) for i, home in enumerate(homes[8 * index : 8 * index + 4]))

        @pl.when(tag > 0)
        def _(own=own, row=row, codes=codes, side=side, index=index, line_words=line_words):
            home = homes[8 * index]
            add(home // 8, own * 256 + home % 8 * 16 + row)
            for code in codes:
                device = lax.shift_right_logical(code * inverse, 16)
                slot = code - device * slots
                mate = jnp.bitwise_xor(jnp.bitwise_and(device, MATES - 1), my_sub)
                step = lax.shift_right_logical(device, 2) - 1
                word = jnp.where(step == 0, word_of(line_words, mate), word_of(own_words, mate))
                phase = jnp.bitwise_and(lax.shift_right_logical(word, 3), 7)
                line = jnp.bitwise_and(word, 7)

                @pl.when(step != 2 * side - 1)
                def _(phase=phase, line=line, slot=slot):
                    add(phase, own * 256 + line * 16 + slot)

        other = 1 - side
        tag, row = read(other * INFO), read(other * INFO + 1)
        codes = [read(other * INFO + 2 + k) for k in range(near_count)]
        few_query[index] = features(terms, row, kept)

        @pl.when(tag > 0)
        def _(codes=codes, side=side, index=index):
            for code in codes:
                device = lax.shift_right_logical(code * inverse, 16)
                slot = code - device * slots
                mate = jnp.bitwise_xor(jnp.bitwise_and(device, MATES - 1), my_sub)
                step = lax.shift_right_logical(device, 2) - 1

                @pl.when(step == 1 - 2 * side)
                def _(slot=slot, mate=mate, index=index):
                    place = few_counts[0]
                    few[0, place] = index * 256 + mate * 16 + slot
                    few_counts[0] = place + 1

    few_query[2] = few_query[0]
    for extra in range(GROUPS[0]):
        few[0, few_counts[0] + extra] = 2 * 256
        for phase in range(phases):
            tiles[phase, counts[phase] + extra] = OSLOTS * 256
    acc[...] = jnp.zeros_like(acc)
    gather_tiles(
        kept, slots, rows, lat, 0, few, few_counts, few_query, lines_of(refs, parts), acc, scratch,
        FEW_GROUPS,
    )
    if beyond.shape[0] == 1:
        upper = lax.axis_index("slab") * 2 >= lax.axis_size("slab")
        chosen = [jnp.where(upper, below_place, above_place)]
    else:
        chosen = [below_place, above_place]
    for place, index in enumerate(chosen):
        beyond[place] = mm(send_turned[...], acc[index].astype(BF16)).astype(BF16)


def last_kernel(
    kept, slots, rows, lat, phase, parts, ref_count, ways, scale, target_in, tiles_in, counts_in,
    arrived_in, query, send_turned, in_turned, w_out, pay, first, second, earlier, *rest,
):
    passed, rest = rest[:ways], rest[ways:]
    lines, rest = lines_of(rest, parts), rest[ref_count:]
    out, target, tiles, counts, arrived, sems, acc, sums, joined, hidden, updated, stores, *scratch = rest
    ready = to_smem(
        ((target_in, target), (tiles_in, tiles), (counts_in, counts), (arrived_in, arrived)), sems
    )
    acc[...] = earlier[...]
    gather_tiles(
        kept, slots, rows, lat, phase, tiles, counts, query, lines, acc, scratch, ready=ready
    )
    hole = first_hole(target, slots)
    me = lax.axis_index("slab") * lax.axis_size("sub") + lax.axis_index("sub")
    for row in range(kept):
        out_slot = target[slot_of(row, hole, kept, slots)]
        own = jnp.where(owner_of(out_slot) == me, out_slot - me * OSLOTS, OSLOTS)
        start = head_of(kept) + row * lat
        joined[own, 0:lat, :] = pay[start : start + lat, :]
    for index, ref in enumerate((first, second)):
        start = pl.multiple_of(head_of(kept) + arrived[2 * index + 1] * lat, 16)
        joined[arrived[2 * index], 0:lat, :] = ref[pl.ds(start, lat), :]
    for own in range(OSLOTS):
        sums[own] = mm(send_turned[...], acc[own].astype(BF16))
    below_place, above_place = places_of_partners()
    if ways == 1:
        upper = lax.axis_index("slab") * 2 >= lax.axis_size("slab")
        chosen = [jnp.where(upper, below_place, above_place)]
    else:
        chosen = [below_place, above_place]
    for index, ref in zip(chosen, passed):
        sums[arrived[2 * index]] += ref[...].astype(F32)
    for own in range(OSLOTS):
        joined[own, lat : 2 * lat, :] = (sums[own] * scale).astype(BF16)
    for own in range(OSLOTS):
        before = mm(in_turned[...], joined[own])
        hidden[own] = (before * (0.5 + 0.5 * jnp.tanh(0.5 * before))).astype(BF16)
    copies = []
    out_turned = jnp.transpose(w_out[...])
    for own in range(OSLOTS):
        new = joined[own, 0:lat, :].astype(F32) + mm(out_turned, hidden[own])
        updated[own] = jnp.transpose(new.astype(BF16))
        copies.append(
            pltpu.make_async_copy(
                updated.at[own], out.at[own * rows : own * rows + rows, :], stores.at[own]
            )
        )
        copies[-1].start()
    for copy in copies:
        copy.wait()


def on_device(latent, positions, target, neighbours, w_send, w_in, w_out):
    lat = latent.shape[1]
    slots = target.shape[0]
    rows = latent.shape[0] // slots
    near_count = neighbours.shape[1]
    slab_count = lax.axis_size("slab")
    kept = slots - 1 if slab_count <= 4 else slots
    length = head_of(kept) + kept * lat
    if lax.axis_size("sub") != MATES:
        raise ValueError("sizes")
    pairs = [[(i, i + 1) for i in range(begin, slab_count - 1, 2)] for begin in (0, 1)]
    pairs = [some + [(j, i) for i, j in some] for some in pairs]
    def mate_of(value, bit):
        return lax.ppermute(value, "sub", [(i, i ^ bit) for i in range(MATES)])

    def swap_first(value):
        return lax.ppermute(value, "slab", pairs[0])

    def swap_second(value):
        return lax.ppermute(value, "slab", pairs[1])

    cut_up, cut = length - REST_UP * lat, length - REST * lat
    pay = call(
        functools.partial(pack_kernel, kept, slots, rows),
        "pack",
        jax.ShapeDtypeStruct((length, rows), BF16),
        [HB, HB, HB, HB],
        VM,
        [
            pltpu.SMEM((slots,), jnp.int32),
            pltpu.SMEM((near_count, slots), jnp.int32),
            pltpu.VMEM(positions.shape, BF16),
            pltpu.VMEM((head_of(kept), rows), F32),
            pltpu.VMEM((slots, rows, lat), BF16),
            pltpu.SemaphoreType.DMA((slots + 3,)),
        ],
        in_hbm(target, neighbours.T, latent, positions),
    )
    across = mate_of(pay, 2)
    first_own, second_own = swap_first(pay), swap_second(pay)
    pair = mate_of(pay, 1)

    homes = (10, 16, 18, 24, 0, 1, 8, 9, 11, 17, 19, 25)
    phase_count = 4
    most = OSLOTS * (near_count + 1) + GROUPS[0]
    tiles, counts, query, send_turned, in_turned = call(
        functools.partial(plan_kernel, kept, slots, rows, homes, phase_count),
        "plan",
        (
            jax.ShapeDtypeStruct((phase_count, most), jnp.int32),
            jax.ShapeDtypeStruct((phase_count,), jnp.int32),
            jax.ShapeDtypeStruct((OSLOTS + 1, FEAT, rows), BF16),
            jax.ShapeDtypeStruct((lat, 2 * lat), BF16),
            jax.ShapeDtypeStruct((lat, 2 * lat), BF16),
        ),
        [HB, HB, VM, HB, HB],
        (SM, SM, VM, VM, VM),
        [
            pltpu.SMEM((slots,), jnp.int32),
            pltpu.SMEM((near_count, slots), jnp.int32),
            pltpu.VMEM(w_send.shape, BF16),
            pltpu.VMEM(w_in.shape, BF16),
            pltpu.VMEM((rows // 128, FEAT * kept, 128), F32),
            pltpu.SemaphoreType.DMA((4,)),
        ],
        (*in_hbm(target, neighbours.T), pay, *in_hbm(w_send, w_in)),
    )

    def scratch_for(parts):
        return [
            pltpu.VMEM((len(parts), length, rows), BF16),
            pltpu.VMEM((len(parts) * kept, FEAT, rows), BF16),
            pltpu.VMEM((rows // 128, FEAT * kept, 128), F32),
            pltpu.SMEM((len(parts),), jnp.int32),
        ]

    sums = (OSLOTS + 1, 2 * lat, rows)
    whole = lambda index: ((index, 0, length),)
    split = lambda index, other, start=0: ((index, 0, cut), (other, start, length - cut))
    split_up = lambda index, other: ((index, 0, cut_up), (other, 0, length - cut_up))

    def tiles_call(phase, parts, refs, earlier):
        earlier = [] if earlier is None else [earlier]
        return call(
            functools.partial(
                tiles_kernel, kept, slots, rows, lat, phase, parts, len(refs), bool(earlier)
            ),
            f"tiles{phase}",
            jax.ShapeDtypeStruct(sums, F32),
            [AN, AN, VM] + [VM] * (len(earlier) + len(refs)),
            VM,
            [
                pltpu.SMEM((phase_count, most), jnp.int32),
                pltpu.SMEM((phase_count,), jnp.int32),
                pltpu.SemaphoreType.DMA((2,)),
                *scratch_for(parts),
            ],
            (tiles, counts, query, *earlier, *refs),
        )

    partial = tiles_call(0, (whole(0), whole(1)), [pay, pair], None)
    across, partial = lax.optimization_barrier((across, partial))
    first_far, second_far = swap_first(across[:cut_up]), swap_second(across[:cut])
    across_pair = mate_of(across, 1)
    far_rest = mate_of(jnp.concatenate([first_own[cut_up:], second_own[cut:]], axis=0), 2)
    first_pair, second_pair = mate_of(first_own, 1), mate_of(second_own, 1)
    ways = 1 if slab_count <= 4 else 2
    tiles, counts, query, arrived, beyond = call(
        functools.partial(
            arrivals_kernel, kept, slots, rows, lat, homes, phase_count,
            tuple(whole(index) for index in range(4)), 4,
        ),
        "arrivals",
        (
            jax.ShapeDtypeStruct((phase_count, most), jnp.int32),
            jax.ShapeDtypeStruct((phase_count,), jnp.int32),
            jax.ShapeDtypeStruct((OSLOTS + 1, FEAT, rows), BF16),
            jax.ShapeDtypeStruct((4,), jnp.int32),
            jax.ShapeDtypeStruct((ways, lat, rows), BF16),
        ),
        [SM, SM] + [VM] * 8,
        (SM, SM, VM, SM, VM),
        [
            pltpu.VMEM((3, 2 * lat, rows), F32),
            pltpu.SMEM((1, 2 * near_count + GROUPS[0]), jnp.int32),
            pltpu.SMEM((1,), jnp.int32),
            pltpu.VMEM((3, FEAT, rows), BF16),
            *scratch_for(range(4)),
        ],
        (
            tiles, counts, query, send_turned, first_own, second_own, pay, pair, across,
            across_pair,
        ),
    )
    two_up = [(i, i + 2) for i in range(slab_count - 2)]
    two_down = [(j, i) for i, j in two_up]
    if ways == 1:
        passed = [lax.ppermute(beyond[0], "slab", two_up + two_down)]
    else:
        passed = [
            lax.ppermute(beyond[1], "slab", two_up), lax.ppermute(beyond[0], "slab", two_down)
        ]
    partial = tiles_call(
        1,
        tuple(whole(index) for index in range(6)),
        [across, across_pair, first_own, second_own, pay, pair],
        partial,
    )
    first_far, second_far, partial = lax.optimization_barrier((first_far, second_far, partial))
    first_last, second_last = mate_of(first_far, 1), mate_of(second_far, 1)
    far_rest, first_far = lax.optimization_barrier((far_rest, first_far))
    last_rest = mate_of(far_rest, 1)
    partial = tiles_call(
        2,
        (whole(0), whole(1), split_up(2, 4), split(3, 4, length - cut_up)),
        [first_pair, second_pair, first_far, second_far, far_rest],
        partial,
    )
    scale = (rows * (near_count + 1)) ** -0.5
    last = (split_up(0, 2), split(1, 2, length - cut_up))
    return call(
        functools.partial(last_kernel, kept, slots, rows, lat, 3, last, 3, ways, scale),
        "last",
        jax.ShapeDtypeStruct((OSLOTS * rows, lat), BF16),
        [AN, AN, AN, AN] + [VM] * (11 + ways),
        HB,
        [
            pltpu.SMEM((slots,), jnp.int32),
            pltpu.SMEM((phase_count, most), jnp.int32),
            pltpu.SMEM((phase_count,), jnp.int32),
            pltpu.SMEM((4,), jnp.int32),
            pltpu.SemaphoreType.DMA((4,)),
            pltpu.VMEM(sums, F32),
            pltpu.VMEM((OSLOTS + 1, lat, rows), F32),
            pltpu.VMEM((OSLOTS + 1, 2 * lat, rows), BF16),
            pltpu.VMEM((OSLOTS, lat, rows), BF16),
            pltpu.VMEM((OSLOTS, rows, lat), BF16),
            pltpu.SemaphoreType.DMA((OSLOTS,)),
            *scratch_for(last),
        ],
        (
            target, tiles, counts, arrived, query, send_turned, in_turned, w_out, pay, first_own,
            second_own, partial, *passed, first_last, second_last, last_rest,
        ),
    )


def solution(mesh):
    placed = (
        P(("grp", "slab", "sub"), None),
        P(None, ("grp", "slab", "sub")),
        P(("grp", "slab", "sub")),
        P(("grp", "slab", "sub"), None),
        P(),
        P(),
        P(),
    )
    return jax.shard_map(
        on_device,
        mesh=mesh,
        in_specs=placed,
        out_specs=P(("grp", "slab", "sub"), None),
        check_vma=False,
    )
```

```python
import functools

import jax
import jax.numpy as jnp
from jax import lax
from jax.experimental import pallas as pl
from jax.experimental.pallas import tpu as pltpu
from jax.sharding import PartitionSpec as P

OSLOTS = 8
MATES = 4
GROUPS = (16, 8, 4)
FEW_GROUPS = (8, 4)
REST_UP, REST = 3, 3
INFO = 16
FEAT = 16
LOG2_SCALE = 0.7213475204444817
VMEM_LIMIT = 18 << 20
F32, BF16 = jnp.float32, jnp.bfloat16


def head_of(kept):
    return (3 * kept + 2 + 15) // 16 * 16


def mm(left, right, left_dim=1):
    dims = (((left_dim,), (0,)), ((), ()))
    return lax.dot_general(left, right, dims, preferred_element_type=F32)


def pieces(value):
    high = value.astype(BF16).astype(F32)
    rest = value - high
    middle = rest.astype(BF16).astype(F32)
    return high, middle, rest - middle


def put(terms, index, kept, value):
    for half in range(terms.shape[0]):
        terms[half, index * kept : index * kept + value.shape[0], :] = value[
            :, half * 128 : half * 128 + 128
        ]


def features(terms, index, kept):
    halves = [
        terms[half, pl.ds(index, FEAT, stride=kept), :].astype(BF16)
        for half in range(terms.shape[0])
    ]
    return jnp.concatenate(halves, axis=1)


def owner_of(out_slot):
    return lax.shift_right_arithmetic(out_slot, OSLOTS.bit_length() - 1)


def first_step():
    return 1 - 2 * (lax.axis_index("slab") % 2)


def places_of_partners():
    is_above = (first_step() + 1) // 2
    return is_above, 1 - is_above


def query_terms(terms, head, kept):
    rows = head.shape[1]
    total = jnp.zeros((kept, rows), F32)
    for axis in range(3):
        coord = head[axis * kept : axis * kept + kept, :]
        total = total + coord * coord
        for part, value in enumerate(pieces(coord * (2 * LOG2_SCALE))):
            put(terms, part * 3 + axis, kept, value)
    put(terms, 9, kept, jnp.ones((3 * kept, rows), F32))
    for part, value in enumerate(pieces(total * -LOG2_SCALE)):
        put(terms, 12 + part, kept, value)
    put(terms, 15, kept, jnp.zeros((kept, rows), F32))


def first_hole(target_ref, slots):
    hole = jnp.int32(slots - 1)
    for slot in reversed(range(slots)):
        hole = jnp.where(target_ref[slot] < 0, slot, hole)
    return hole


def slot_of(row, hole, kept, slots):
    return jnp.where(row == hole, slots - 1, row) if kept < slots else row


def call(kernel, name, out_shape, in_specs, out_specs, scratch, args, flops=0, limit=VMEM_LIMIT):
    return pl.pallas_call(
        kernel,
        name=name,
        out_shape=out_shape,
        in_specs=in_specs,
        out_specs=out_specs,
        scratch_shapes=scratch,
        compiler_params=pltpu.CompilerParams(vmem_limit_bytes=limit),
        cost_estimate=pl.CostEstimate(flops=flops, bytes_accessed=flops >> 9, transcendentals=0),
    )(*args)


VM = pl.BlockSpec(memory_space=pltpu.VMEM)
SM = pl.BlockSpec(memory_space=pltpu.SMEM)
HB = pl.BlockSpec(memory_space=pltpu.HBM)
AN = pl.BlockSpec(memory_space=pl.ANY)


def in_hbm(*arrays):
    return [pltpu.with_memory_space_constraint(array, pltpu.HBM) for array in arrays]


def pack_kernel(
    kept, slots, rows, target_in, near_in, latent, positions, pay, target, near, coords, head,
    blocks, sems,
):
    loads = [
        pltpu.make_async_copy(target_in, target, sems.at[slots + 1]),
        pltpu.make_async_copy(near_in, near, sems.at[slots + 2]),
    ]
    copies = [pltpu.make_async_copy(positions, coords, sems.at[slots])]
    for slot in range(slots):
        copies.append(
            pltpu.make_async_copy(
                latent.at[slot * rows : slot * rows + rows, :], blocks.at[slot], sems.at[slot]
            )
        )
    for copy in (*loads, *copies):
        copy.start()
    for load in loads:
        load.wait()
    hole = first_hole(target, slots)
    sub_count = lax.axis_size("sub")
    my_slab = lax.axis_index("slab")
    me = my_slab * sub_count + lax.axis_index("sub")
    lane = lax.broadcasted_iota(jnp.int32, (1, rows), 1)
    info = jnp.zeros((1, rows), jnp.int32)
    for side, device in enumerate((me + sub_count, me - sub_count)):
        tag, moving = jnp.int32(0), jnp.int32(0)
        for slot in range(slots):
            out_slot = target[slot]
            goes = (out_slot >= 0) & (owner_of(out_slot) == device)
            tag = jnp.where(goes, out_slot - device * OSLOTS + 1, tag)
            moving = jnp.where(goes, slot, moving)
        row = jnp.where(moving == slots - 1, hole, moving) if kept < slots else moving
        words = [tag, row] + [
            near[k, moving] - (my_slab - 1) * sub_count * slots for k in range(near.shape[0])
        ]
        for place, word in enumerate(words):
            info = jnp.where(lane == side * INFO + place, word, info)
    head[...] = jnp.zeros_like(head)
    head[pl.ds(3 * kept, 1), :] = jnp.full((1, rows), hole.astype(F32))
    head[pl.ds(3 * kept + 1, 1), :] = info.astype(F32)
    copies[0].wait()
    for row in range(kept):
        start = pl.multiple_of(slot_of(row, hole, kept, slots) * rows, rows)
        block = coords[:, pl.ds(start, rows)].astype(F32)
        for axis in range(3):
            head[pl.ds(axis * kept + row, 1), :] = block[axis : axis + 1, :]
    pay[0:head_of(kept), :] = head[...].astype(BF16)
    lat = latent.shape[1]
    for row in range(kept):
        copies[1 + row].wait()
        start = head_of(kept) + row * lat
        pay[start : start + lat, :] = jnp.transpose(blocks[row])
    if kept < slots:
        copies[slots].wait()

        @pl.when(hole < kept)
        def _():
            start = pl.multiple_of(head_of(kept) + hole * lat, 16)
            pay[pl.ds(start, lat), :] = jnp.transpose(blocks[slots - 1])


def plan_kernel(
    kept, slots, rows, homes, phases, target_in, near_in, pay, w_send_in, w_in_in, tiles, counts,
    query, send_turned, in_turned, target, near, w_send, w_in, terms, sems,
):
    loads = [
        pltpu.make_async_copy(source, ref, sems.at[index])
        for index, (source, ref) in enumerate(
            ((target_in, target), (near_in, near), (w_send_in, w_send), (w_in_in, w_in))
        )
    ]
    for load in loads:
        load.start()
    query_terms(terms, pay[0 : head_of(kept), :].astype(F32), kept)
    for load in loads:
        load.wait()
    lat = w_send.shape[0]
    send_turned[:, 0:lat] = jnp.transpose(w_send[:, 0:lat])
    send_turned[:, lat : 2 * lat] = jnp.transpose(w_send[:, lat : 2 * lat])
    in_turned[...] = jnp.transpose(w_in[...])
    hole = first_hole(target, slots)
    sub_count, slab_count = lax.axis_size("sub"), lax.axis_size("slab")
    my_slab, my_sub = lax.axis_index("slab"), lax.axis_index("sub")
    limit = slab_count * sub_count * slots
    inverse = 65536 // slots + 1
    if any(i * inverse >> 16 != i // slots for i in range(limit)):
        raise ValueError("slot ids")
    words = [sum(home << (6 * i) for i, home in enumerate(homes[at : at + 4])) for at in (0, 4, 8)]
    for phase in range(phases):
        counts[phase] = 0

    def add(phase, entry):
        place = counts[phase]
        tiles[phase, place] = entry
        counts[phase] = place + 1

    me = my_slab * sub_count + my_sub
    first = first_step()
    for row in range(kept):
        out_slot = target[slot_of(row, hole, kept, slots)]
        own = jnp.where(owner_of(out_slot) == me, out_slot - me * OSLOTS, OSLOTS)
        query[own] = features(terms, row, kept)

    def per_slot(slot, carry):
        out_slot = target[slot]
        own = (out_slot - me * OSLOTS) * 256

        @pl.when(owner_of(out_slot) == me)
        def _():
            add(homes[MATES] // 8, own + homes[MATES] % 8 * 16 + slot)
            for k in range(near.shape[0]):
                other = near[k, slot]
                device = lax.shift_right_logical(other * inverse, 16)
                step = device // sub_count - my_slab
                word = jnp.where(step == first, words[0], jnp.where(step == 0, words[1], words[2]))
                home = lax.shift_right_logical(word, 6 * jnp.bitwise_xor(device % sub_count, my_sub))
                phase = jnp.bitwise_and(lax.shift_right_logical(home, 3), 7)
                line = jnp.bitwise_and(home, 7)
                add(phase, own + line * 16 + other - device * slots)

        return carry

    lax.fori_loop(0, slots, per_slot, 0)
    for phase in range(phases):
        for extra in range(GROUPS[0]):
            tiles[phase, counts[phase] + extra] = OSLOTS * 256


def gather_tiles(
    kept, slots, rows, lat, phase, tiles, counts, query, lines, acc, scratch, groups=GROUPS,
    ready=lambda: None,
):
    land, feats, terms, holes = scratch
    for line, parts in enumerate(lines):
        at = 0
        for ref, start, length in parts:
            land[line, at : at + length, :] = ref[start : start + length, :]
            at += length
    put(terms, 12, kept, jnp.ones((3 * kept, rows), F32))
    put(terms, 15, kept, jnp.zeros((kept, rows), F32))
    for line, parts in enumerate(lines):
        head = parts[0][0][0 : head_of(kept), :].astype(F32)
        holes[line] = jnp.max(head[3 * kept : 3 * kept + 1, :]).astype(jnp.int32)
        total = jnp.zeros((kept, rows), F32)
        for axis in range(3):
            coord = head[axis * kept : axis * kept + kept, :]
            total = total + coord * coord
            for part in range(3):
                put(terms, part * 3 + axis, kept, coord)
        for part, value in enumerate(pieces(total * -LOG2_SCALE)):
            put(terms, 9 + part, kept, value)
        for block in range(kept):
            feats[line * kept + block] = features(terms, block, kept)

    ready()

    def work(first, size):
        owns, exponents, sources = [], [], []
        for step in range(size):
            entry = tiles[phase, first + step]
            own = lax.shift_right_logical(entry, 8)
            line = jnp.bitwise_and(lax.shift_right_logical(entry, 4), 15)
            slot = jnp.bitwise_and(entry, 15)
            block = jnp.where(slot == kept, holes[line], slot) if kept < slots else slot
            owns.append(own)
            begin = pl.multiple_of(head_of(kept) + block * lat, 16)
            sources.append(land[line, pl.ds(begin, lat), :])
            exponents.append(
                mm(feats[line * kept + block], query[own], left_dim=0)
            )
        results = []
        for exponent, source in zip(exponents, sources):
            wide = jnp.exp2(exponent)
            square = wide * wide
            results.append(
                (mm(source, wide.astype(BF16)), mm(source, (square * square).astype(BF16)))
            )
        for own, (first, second) in zip(owns, results):
            acc[own, 0:lat] += first
            acc[own, lat : 2 * lat] += second

    large, count = groups[0], counts[phase]
    small = groups[1] if len(groups) > 1 else 0
    whole = (count + large - 1 - small) // large
    lax.fori_loop(0, whole, lambda group, carry: work(group * large, large), None)
    left = count - whole * large
    for size, below in zip(groups[1:], (*groups[2:], 0)):
        pl.when((left > below) & (left <= size))(functools.partial(work, whole * large, size))


def lines_of(refs, parts):
    return [[(refs[index], start, length) for index, start, length in line] for line in parts]


def to_smem(pairs, sems):
    copies = [
        pltpu.make_async_copy(source, ref, sems.at[index])
        for index, (source, ref) in enumerate(pairs)
    ]
    for copy in copies:
        copy.start()

    def ready():
        for copy in copies:
            copy.wait()

    return ready


def tiles_kernel(
    kept, slots, rows, lat, phase, parts, ref_count, has_earlier, tiles_in, counts_in, query, *rest
):
    earlier, rest = (rest[0], rest[1:]) if has_earlier else (None, rest)
    lines, (acc, tiles, counts, sems, *scratch) = lines_of(rest, parts), rest[ref_count:]
    ready = to_smem(((tiles_in, tiles), (counts_in, counts)), sems)
    if has_earlier:
        acc[...] = earlier[...]
    else:
        acc[...] = jnp.zeros_like(acc)
    gather_tiles(
        kept, slots, rows, lat, phase, tiles, counts, query, lines, acc, scratch, ready=ready
    )


def arrivals_kernel(
    kept, slots, rows, lat, homes, phases, parts, ref_count, tiles_in, counts_in, query_in,
    send_turned, first, second, *rest,
):
    refs, rest = rest[:ref_count], rest[ref_count:]
    tiles, counts, query, arrived, beyond, acc, few, few_counts, few_query, *scratch = rest
    terms = scratch[2]
    my_sub = lax.axis_index("sub")
    query[...] = query_in[...]
    for phase in range(phases):
        count = counts_in[phase]
        counts[phase] = count

        def keep(place, carry, phase=phase):
            tiles[phase, place] = tiles_in[phase, place]
            return carry

        lax.fori_loop(0, count, keep, 0)
    few_counts[0] = 0

    def add(phase, entry):
        place = counts[phase]
        tiles[phase, place] = entry
        counts[phase] = place + 1

    def word_of(words, mate):
        return lax.shift_right_logical(words, 6 * mate)

    near_count = INFO // 2
    plane = MATES * slots
    inverse = 65536 // slots + 1
    own_words = sum(home << (6 * i) for i, home in enumerate((12, 13, 8, 9)))
    below_place, above_place = places_of_partners()
    for index, ref in enumerate((first, second)):
        side = jnp.where(below_place == index, 0, 1)
        head = ref[0 : head_of(kept), :].astype(F32)
        query_terms(terms, head, kept)
        info = head[3 * kept + 1 : 3 * kept + 2, :]
        lane = lax.broadcasted_iota(jnp.int32, info.shape, 1)

        def read(place, info=info, lane=lane):
            return jnp.sum(jnp.where(lane == place, info, 0.0)).astype(jnp.int32)

        tag, row = read(side * INFO), read(side * INFO + 1)
        codes = [read(side * INFO + 2 + k) for k in range(near_count)]
        own = jnp.where(tag > 0, tag - 1, OSLOTS)
        arrived[2 * index] = own
        arrived[2 * index + 1] = row
        query[own] = features(terms, row, kept)
        line_words = sum(home << (6 * i) for i, home in enumerate(homes[8 * index : 8 * index + 4]))

        @pl.when(tag > 0)
        def _(own=own, row=row, codes=codes, side=side, index=index, line_words=line_words):
            home = homes[8 * index]
            add(home // 8, own * 256 + home % 8 * 16 + row)
            for code in codes:
                device = lax.shift_right_logical(code * inverse, 16)
                slot = code - device * slots
                mate = jnp.bitwise_xor(jnp.bitwise_and(device, MATES - 1), my_sub)
                step = lax.shift_right_logical(device, 2) - 1
                word = jnp.where(step == 0, word_of(line_words, mate), word_of(own_words, mate))
                phase = jnp.bitwise_and(lax.shift_right_logical(word, 3), 7)
                line = jnp.bitwise_and(word, 7)

                @pl.when(step != 2 * side - 1)
                def _(phase=phase, line=line, slot=slot):
                    add(phase, own * 256 + line * 16 + slot)

        other = 1 - side
        tag, row = read(other * INFO), read(other * INFO + 1)
        codes = [read(other * INFO + 2 + k) for k in range(near_count)]
        few_query[index] = features(terms, row, kept)

        @pl.when(tag > 0)
        def _(codes=codes, side=side, index=index):
            for code in codes:
                device = lax.shift_right_logical(code * inverse, 16)
                slot = code - device * slots
                mate = jnp.bitwise_xor(jnp.bitwise_and(device, MATES - 1), my_sub)
                step = lax.shift_right_logical(device, 2) - 1

                @pl.when(step == 1 - 2 * side)
                def _(slot=slot, mate=mate, index=index):
                    place = few_counts[0]
                    few[0, place] = index * 256 + mate * 16 + slot
                    few_counts[0] = place + 1

    few_query[2] = few_query[0]
    for extra in range(GROUPS[0]):
        few[0, few_counts[0] + extra] = 2 * 256
        for phase in range(phases):
            tiles[phase, counts[phase] + extra] = OSLOTS * 256
    acc[...] = jnp.zeros_like(acc)
    gather_tiles(
        kept, slots, rows, lat, 0, few, few_counts, few_query, lines_of(refs, parts), acc, scratch,
        FEW_GROUPS,
    )
    if beyond.shape[0] == 1:
        upper = lax.axis_index("slab") * 2 >= lax.axis_size("slab")
        chosen = [jnp.where(upper, below_place, above_place)]
    else:
        chosen = [below_place, above_place]
    for place, index in enumerate(chosen):
        beyond[place] = mm(send_turned[...], acc[index].astype(BF16)).astype(BF16)


def last_kernel(
    kept, slots, rows, lat, phase, parts, ref_count, ways, scale, target_in, tiles_in, counts_in,
    arrived_in, query, send_turned, in_turned, w_out, pay, first, second, earlier, *rest,
):
    passed, rest = rest[:ways], rest[ways:]
    lines, rest = lines_of(rest, parts), rest[ref_count:]
    out, target, tiles, counts, arrived, sems, acc, sums, joined, hidden, updated, stores, *scratch = rest
    ready = to_smem(
        ((target_in, target), (tiles_in, tiles), (counts_in, counts), (arrived_in, arrived)), sems
    )
    acc[...] = earlier[...]
    gather_tiles(
        kept, slots, rows, lat, phase, tiles, counts, query, lines, acc, scratch, ready=ready
    )
    hole = first_hole(target, slots)
    me = lax.axis_index("slab") * lax.axis_size("sub") + lax.axis_index("sub")
    for row in range(kept):
        out_slot = target[slot_of(row, hole, kept, slots)]
        own = jnp.where(owner_of(out_slot) == me, out_slot - me * OSLOTS, OSLOTS)
        start = head_of(kept) + row * lat
        joined[own, 0:lat, :] = pay[start : start + lat, :]
    for index, ref in enumerate((first, second)):
        start = pl.multiple_of(head_of(kept) + arrived[2 * index + 1] * lat, 16)
        joined[arrived[2 * index], 0:lat, :] = ref[pl.ds(start, lat), :]
    for own in range(OSLOTS):
        sums[own] = mm(send_turned[...], acc[own].astype(BF16))
    below_place, above_place = places_of_partners()
    if ways == 1:
        upper = lax.axis_index("slab") * 2 >= lax.axis_size("slab")
        chosen = [jnp.where(upper, below_place, above_place)]
    else:
        chosen = [below_place, above_place]
    for index, ref in zip(chosen, passed):
        sums[arrived[2 * index]] += ref[...].astype(F32)
    for own in range(OSLOTS):
        joined[own, lat : 2 * lat, :] = (sums[own] * scale).astype(BF16)
    for own in range(OSLOTS):
        before = mm(in_turned[...], joined[own])
        hidden[own] = (before * (0.5 + 0.5 * jnp.tanh(0.5 * before))).astype(BF16)
    copies = []
    out_turned = jnp.transpose(w_out[...])
    for own in range(OSLOTS):
        new = joined[own, 0:lat, :].astype(F32) + mm(out_turned, hidden[own])
        updated[own] = jnp.transpose(new.astype(BF16))
        copies.append(
            pltpu.make_async_copy(
                updated.at[own], out.at[own * rows : own * rows + rows, :], stores.at[own]
            )
        )
        copies[-1].start()
    for copy in copies:
        copy.wait()


def on_device(latent, positions, target, neighbours, w_send, w_in, w_out):
    lat = latent.shape[1]
    slots = target.shape[0]
    rows = latent.shape[0] // slots
    near_count = neighbours.shape[1]
    slab_count = lax.axis_size("slab")
    kept = slots - 1 if slab_count <= 4 else slots
    length = head_of(kept) + kept * lat
    if lax.axis_size("sub") != MATES:
        raise ValueError("sizes")
    pairs = [[(i, i + 1) for i in range(begin, slab_count - 1, 2)] for begin in (0, 1)]
    pairs = [some + [(j, i) for i, j in some] for some in pairs]
    def mate_of(value, bit):
        return lax.ppermute(value, "sub", [(i, i ^ bit) for i in range(MATES)])

    def swap_first(value):
        return lax.ppermute(value, "slab", pairs[0])

    def swap_second(value):
        return lax.ppermute(value, "slab", pairs[1])

    cut_up, cut = length - REST_UP * lat, length - REST * lat
    pay = call(
        functools.partial(pack_kernel, kept, slots, rows),
        "pack",
        jax.ShapeDtypeStruct((length, rows), BF16),
        [HB, HB, HB, HB],
        VM,
        [
            pltpu.SMEM((slots,), jnp.int32),
            pltpu.SMEM((near_count, slots), jnp.int32),
            pltpu.VMEM(positions.shape, BF16),
            pltpu.VMEM((head_of(kept), rows), F32),
            pltpu.VMEM((slots, rows, lat), BF16),
            pltpu.SemaphoreType.DMA((slots + 3,)),
        ],
        in_hbm(target, neighbours.T, latent, positions),
    )
    across = mate_of(pay, 2)
    first_own, second_own = swap_first(pay), swap_second(pay)
    pair = mate_of(pay, 1)

    homes = (10, 16, 18, 24, 0, 1, 8, 9, 11, 17, 19, 25)
    phase_count = 4
    most = OSLOTS * (near_count + 1) + GROUPS[0]
    tiles, counts, query, send_turned, in_turned = call(
        functools.partial(plan_kernel, kept, slots, rows, homes, phase_count),
        "plan",
        (
            jax.ShapeDtypeStruct((phase_count, most), jnp.int32),
            jax.ShapeDtypeStruct((phase_count,), jnp.int32),
            jax.ShapeDtypeStruct((OSLOTS + 1, FEAT, rows), BF16),
            jax.ShapeDtypeStruct((lat, 2 * lat), BF16),
            jax.ShapeDtypeStruct((lat, 2 * lat), BF16),
        ),
        [HB, HB, VM, HB, HB],
        (SM, SM, VM, VM, VM),
        [
            pltpu.SMEM((slots,), jnp.int32),
            pltpu.SMEM((near_count, slots), jnp.int32),
            pltpu.VMEM(w_send.shape, BF16),
            pltpu.VMEM(w_in.shape, BF16),
            pltpu.VMEM((rows // 128, FEAT * kept, 128), F32),
            pltpu.SemaphoreType.DMA((4,)),
        ],
        (*in_hbm(target, neighbours.T), pay, *in_hbm(w_send, w_in)),
    )

    def scratch_for(parts):
        return [
            pltpu.VMEM((len(parts), length, rows), BF16),
            pltpu.VMEM((len(parts) * kept, FEAT, rows), BF16),
            pltpu.VMEM((rows // 128, FEAT * kept, 128), F32),
            pltpu.SMEM((len(parts),), jnp.int32),
        ]

    sums = (OSLOTS + 1, 2 * lat, rows)
    whole = lambda index: ((index, 0, length),)
    split = lambda index, other, start=0: ((index, 0, cut), (other, start, length - cut))
    split_up = lambda index, other: ((index, 0, cut_up), (other, 0, length - cut_up))

    def tiles_call(phase, parts, refs, earlier):
        earlier = [] if earlier is None else [earlier]
        return call(
            functools.partial(
                tiles_kernel, kept, slots, rows, lat, phase, parts, len(refs), bool(earlier)
            ),
            f"tiles{phase}",
            jax.ShapeDtypeStruct(sums, F32),
            [AN, AN, VM] + [VM] * (len(earlier) + len(refs)),
            VM,
            [
                pltpu.SMEM((phase_count, most), jnp.int32),
                pltpu.SMEM((phase_count,), jnp.int32),
                pltpu.SemaphoreType.DMA((2,)),
                *scratch_for(parts),
            ],
            (tiles, counts, query, *earlier, *refs),
        )

    partial = tiles_call(0, (whole(0), whole(1)), [pay, pair], None)
    across, partial = lax.optimization_barrier((across, partial))
    first_far, second_far = swap_first(across[:cut_up]), swap_second(across[:cut])
    across_pair = mate_of(across, 1)
    far_rest = mate_of(jnp.concatenate([first_own[cut_up:], second_own[cut:]], axis=0), 2)
    first_pair, second_pair = mate_of(first_own, 1), mate_of(second_own, 1)
    ways = 1 if slab_count <= 4 else 2
    tiles, counts, query, arrived, beyond = call(
        functools.partial(
            arrivals_kernel, kept, slots, rows, lat, homes, phase_count,
            tuple(whole(index) for index in range(4)), 4,
        ),
        "arrivals",
        (
            jax.ShapeDtypeStruct((phase_count, most), jnp.int32),
            jax.ShapeDtypeStruct((phase_count,), jnp.int32),
            jax.ShapeDtypeStruct((OSLOTS + 1, FEAT, rows), BF16),
            jax.ShapeDtypeStruct((4,), jnp.int32),
            jax.ShapeDtypeStruct((ways, lat, rows), BF16),
        ),
        [SM, SM] + [VM] * 8,
        (SM, SM, VM, SM, VM),
        [
            pltpu.VMEM((3, 2 * lat, rows), F32),
            pltpu.SMEM((1, 2 * near_count + GROUPS[0]), jnp.int32),
            pltpu.SMEM((1,), jnp.int32),
            pltpu.VMEM((3, FEAT, rows), BF16),
            *scratch_for(range(4)),
        ],
        (
            tiles, counts, query, send_turned, first_own, second_own, pay, pair, across,
            across_pair,
        ),
    )
    two_up = [(i, i + 2) for i in range(slab_count - 2)]
    two_down = [(j, i) for i, j in two_up]
    if ways == 1:
        passed = [lax.ppermute(beyond[0], "slab", two_up + two_down)]
    else:
        passed = [
            lax.ppermute(beyond[1], "slab", two_up), lax.ppermute(beyond[0], "slab", two_down)
        ]
    partial = tiles_call(
        1,
        tuple(whole(index) for index in range(6)),
        [across, across_pair, first_own, second_own, pay, pair],
        partial,
    )
    first_far, second_far, partial = lax.optimization_barrier((first_far, second_far, partial))
    first_last, second_last = mate_of(first_far, 1), mate_of(second_far, 1)
    last_rest = mate_of(far_rest, 1)
    partial = tiles_call(
        2,
        (whole(0), whole(1), split_up(2, 4), split(3, 4, length - cut_up)),
        [first_pair, second_pair, first_far, second_far, far_rest],
        partial,
    )
    scale = (rows * (near_count + 1)) ** -0.5
    last = (split_up(0, 2), split(1, 2, length - cut_up))
    return call(
        functools.partial(last_kernel, kept, slots, rows, lat, 3, last, 3, ways, scale),
        "last",
        jax.ShapeDtypeStruct((OSLOTS * rows, lat), BF16),
        [AN, AN, AN, AN] + [VM] * (11 + ways),
        HB,
        [
            pltpu.SMEM((slots,), jnp.int32),
            pltpu.SMEM((phase_count, most), jnp.int32),
            pltpu.SMEM((phase_count,), jnp.int32),
            pltpu.SMEM((4,), jnp.int32),
            pltpu.SemaphoreType.DMA((4,)),
            pltpu.VMEM(sums, F32),
            pltpu.VMEM((OSLOTS + 1, lat, rows), F32),
            pltpu.VMEM((OSLOTS + 1, 2 * lat, rows), BF16),
            pltpu.VMEM((OSLOTS, lat, rows), BF16),
            pltpu.VMEM((OSLOTS, rows, lat), BF16),
            pltpu.SemaphoreType.DMA((OSLOTS,)),
            *scratch_for(last),
        ],
        (
            target, tiles, counts, arrived, query, send_turned, in_turned, w_out, pay, first_own,
            second_own, partial, *passed, first_last, second_last, last_rest,
        ),
    )


def solution(mesh):
    placed = (
        P(("grp", "slab", "sub"), None),
        P(None, ("grp", "slab", "sub")),
        P(("grp", "slab", "sub")),
        P(("grp", "slab", "sub"), None),
        P(),
        P(),
        P(),
    )
    return jax.shard_map(
        on_device,
        mesh=mesh,
        in_specs=placed,
        out_specs=P(("grp", "slab", "sub"), None),
        check_vma=False,
    )
```

```python
import functools

import jax
import jax.numpy as jnp
from jax import lax
from jax.experimental import pallas as pl
from jax.experimental.pallas import tpu as pltpu
from jax.sharding import PartitionSpec as P

OSLOTS = 8
MATES = 4
GROUPS = (16, 12, 8, 4)
FEW_GROUPS = (8, 4)
REST_UP, REST = 3, 3
INFO = 16
FEAT = 16
LOG2_SCALE = 0.7213475204444817
VMEM_LIMIT = 18 << 20
F32, BF16 = jnp.float32, jnp.bfloat16


def head_of(kept):
    return (3 * kept + 2 + 15) // 16 * 16


def mm(left, right, left_dim=1):
    dims = (((left_dim,), (0,)), ((), ()))
    return lax.dot_general(left, right, dims, preferred_element_type=F32)


def pieces(value):
    high = value.astype(BF16).astype(F32)
    rest = value - high
    middle = rest.astype(BF16).astype(F32)
    return high, middle, rest - middle


def put(terms, index, kept, value):
    for half in range(terms.shape[0]):
        terms[half, index * kept : index * kept + value.shape[0], :] = value[
            :, half * 128 : half * 128 + 128
        ]


def features(terms, index, kept):
    halves = [
        terms[half, pl.ds(index, FEAT, stride=kept), :].astype(BF16)
        for half in range(terms.shape[0])
    ]
    return jnp.concatenate(halves, axis=1)


def owner_of(out_slot):
    return lax.shift_right_arithmetic(out_slot, OSLOTS.bit_length() - 1)


def first_step():
    return 1 - 2 * (lax.axis_index("slab") % 2)


def places_of_partners():
    is_above = (first_step() + 1) // 2
    return is_above, 1 - is_above


def query_terms(terms, head, kept):
    rows = head.shape[1]
    total = jnp.zeros((kept, rows), F32)
    for axis in range(3):
        coord = head[axis * kept : axis * kept + kept, :]
        total = total + coord * coord
        for part, value in enumerate(pieces(coord * (2 * LOG2_SCALE))):
            put(terms, part * 3 + axis, kept, value)
    put(terms, 9, kept, jnp.ones((3 * kept, rows), F32))
    for part, value in enumerate(pieces(total * -LOG2_SCALE)):
        put(terms, 12 + part, kept, value)
    put(terms, 15, kept, jnp.zeros((kept, rows), F32))


def first_hole(target_ref, slots):
    hole = jnp.int32(slots - 1)
    for slot in reversed(range(slots)):
        hole = jnp.where(target_ref[slot] < 0, slot, hole)
    return hole


def slot_of(row, hole, kept, slots):
    return jnp.where(row == hole, slots - 1, row) if kept < slots else row


def call(kernel, name, out_shape, in_specs, out_specs, scratch, args, flops=0, limit=VMEM_LIMIT):
    return pl.pallas_call(
        kernel,
        name=name,
        out_shape=out_shape,
        in_specs=in_specs,
        out_specs=out_specs,
        scratch_shapes=scratch,
        compiler_params=pltpu.CompilerParams(vmem_limit_bytes=limit),
        cost_estimate=pl.CostEstimate(flops=flops, bytes_accessed=flops >> 9, transcendentals=0),
    )(*args)


VM = pl.BlockSpec(memory_space=pltpu.VMEM)
SM = pl.BlockSpec(memory_space=pltpu.SMEM)
HB = pl.BlockSpec(memory_space=pltpu.HBM)
AN = pl.BlockSpec(memory_space=pl.ANY)


def in_hbm(*arrays):
    return [pltpu.with_memory_space_constraint(array, pltpu.HBM) for array in arrays]


def pack_kernel(
    kept, slots, rows, target_in, near_in, latent, positions, pay, target, near, coords, head,
    blocks, sems,
):
    loads = [
        pltpu.make_async_copy(target_in, target, sems.at[slots + 1]),
        pltpu.make_async_copy(near_in, near, sems.at[slots + 2]),
    ]
    copies = [pltpu.make_async_copy(positions, coords, sems.at[slots])]
    for slot in range(slots):
        copies.append(
            pltpu.make_async_copy(
                latent.at[slot * rows : slot * rows + rows, :], blocks.at[slot], sems.at[slot]
            )
        )
    for copy in (*loads, *copies):
        copy.start()
    for load in loads:
        load.wait()
    hole = first_hole(target, slots)
    sub_count = lax.axis_size("sub")
    my_slab = lax.axis_index("slab")
    me = my_slab * sub_count + lax.axis_index("sub")
    lane = lax.broadcasted_iota(jnp.int32, (1, rows), 1)
    info = jnp.zeros((1, rows), jnp.int32)
    for side, device in enumerate((me + sub_count, me - sub_count)):
        tag, moving = jnp.int32(0), jnp.int32(0)
        for slot in range(slots):
            out_slot = target[slot]
            goes = (out_slot >= 0) & (owner_of(out_slot) == device)
            tag = jnp.where(goes, out_slot - device * OSLOTS + 1, tag)
            moving = jnp.where(goes, slot, moving)
        row = jnp.where(moving == slots - 1, hole, moving) if kept < slots else moving
        words = [tag, row] + [
            near[k, moving] - (my_slab - 1) * sub_count * slots for k in range(near.shape[0])
        ]
        for place, word in enumerate(words):
            info = jnp.where(lane == side * INFO + place, word, info)
    head[...] = jnp.zeros_like(head)
    head[pl.ds(3 * kept, 1), :] = jnp.full((1, rows), hole.astype(F32))
    head[pl.ds(3 * kept + 1, 1), :] = info.astype(F32)
    copies[0].wait()
    for row in range(kept):
        start = pl.multiple_of(slot_of(row, hole, kept, slots) * rows, rows)
        block = coords[:, pl.ds(start, rows)].astype(F32)
        for axis in range(3):
            head[pl.ds(axis * kept + row, 1), :] = block[axis : axis + 1, :]
    pay[0:head_of(kept), :] = head[...].astype(BF16)
    lat = latent.shape[1]
    for row in range(kept):
        copies[1 + row].wait()
        start = head_of(kept) + row * lat
        pay[start : start + lat, :] = jnp.transpose(blocks[row])
    if kept < slots:
        copies[slots].wait()

        @pl.when(hole < kept)
        def _():
            start = pl.multiple_of(head_of(kept) + hole * lat, 16)
            pay[pl.ds(start, lat), :] = jnp.transpose(blocks[slots - 1])


def plan_kernel(
    kept, slots, rows, homes, phases, target_in, near_in, pay, w_send_in, w_in_in, tiles, counts,
    query, send_turned, in_turned, target, near, w_send, w_in, terms, sems,
):
    loads = [
        pltpu.make_async_copy(source, ref, sems.at[index])
        for index, (source, ref) in enumerate(
            ((target_in, target), (near_in, near), (w_send_in, w_send), (w_in_in, w_in))
        )
    ]
    for load in loads:
        load.start()
    query_terms(terms, pay[0 : head_of(kept), :].astype(F32), kept)
    for load in loads:
        load.wait()
    lat = w_send.shape[0]
    send_turned[:, 0:lat] = jnp.transpose(w_send[:, 0:lat])
    send_turned[:, lat : 2 * lat] = jnp.transpose(w_send[:, lat : 2 * lat])
    in_turned[...] = jnp.transpose(w_in[...])
    hole = first_hole(target, slots)
    sub_count, slab_count = lax.axis_size("sub"), lax.axis_size("slab")
    my_slab, my_sub = lax.axis_index("slab"), lax.axis_index("sub")
    limit = slab_count * sub_count * slots
    inverse = 65536 // slots + 1
    if any(i * inverse >> 16 != i // slots for i in range(limit)):
        raise ValueError("slot ids")
    words = [sum(home << (6 * i) for i, home in enumerate(homes[at : at + 4])) for at in (0, 4, 8)]
    for phase in range(phases):
        counts[phase] = 0

    def add(phase, entry):
        place = counts[phase]
        tiles[phase, place] = entry
        counts[phase] = place + 1

    me = my_slab * sub_count + my_sub
    first = first_step()
    for row in range(kept):
        out_slot = target[slot_of(row, hole, kept, slots)]
        own = jnp.where(owner_of(out_slot) == me, out_slot - me * OSLOTS, OSLOTS)
        query[own] = features(terms, row, kept)

    def per_slot(slot, carry):
        out_slot = target[slot]
        own = (out_slot - me * OSLOTS) * 256

        @pl.when(owner_of(out_slot) == me)
        def _():
            add(homes[MATES] // 8, own + homes[MATES] % 8 * 16 + slot)
            for k in range(near.shape[0]):
                other = near[k, slot]
                device = lax.shift_right_logical(other * inverse, 16)
                step = device // sub_count - my_slab
                word = jnp.where(step == first, words[0], jnp.where(step == 0, words[1], words[2]))
                home = lax.shift_right_logical(word, 6 * jnp.bitwise_xor(device % sub_count, my_sub))
                phase = jnp.bitwise_and(lax.shift_right_logical(home, 3), 7)
                line = jnp.bitwise_and(home, 7)
                add(phase, own + line * 16 + other - device * slots)

        return carry

    lax.fori_loop(0, slots, per_slot, 0)
    for phase in range(phases):
        for extra in range(GROUPS[0]):
            tiles[phase, counts[phase] + extra] = OSLOTS * 256


def gather_tiles(
    kept, slots, rows, lat, phase, tiles, counts, query, lines, acc, scratch, groups=GROUPS,
    ready=lambda: None,
):
    land, feats, terms, holes = scratch
    for line, parts in enumerate(lines):
        at = 0
        for ref, start, length in parts:
            land[line, at : at + length, :] = ref[start : start + length, :]
            at += length
    put(terms, 12, kept, jnp.ones((3 * kept, rows), F32))
    put(terms, 15, kept, jnp.zeros((kept, rows), F32))
    for line, parts in enumerate(lines):
        head = parts[0][0][0 : head_of(kept), :].astype(F32)
        holes[line] = jnp.max(head[3 * kept : 3 * kept + 1, :]).astype(jnp.int32)
        total = jnp.zeros((kept, rows), F32)
        for axis in range(3):
            coord = head[axis * kept : axis * kept + kept, :]
            total = total + coord * coord
            for part in range(3):
                put(terms, part * 3 + axis, kept, coord)
        for part, value in enumerate(pieces(total * -LOG2_SCALE)):
            put(terms, 9 + part, kept, value)
        for block in range(kept):
            feats[line * kept + block] = features(terms, block, kept)

    ready()

    def work(first, size):
        owns, exponents, sources = [], [], []
        for step in range(size):
            entry = tiles[phase, first + step]
            own = lax.shift_right_logical(entry, 8)
            line = jnp.bitwise_and(lax.shift_right_logical(entry, 4), 15)
            slot = jnp.bitwise_and(entry, 15)
            block = jnp.where(slot == kept, holes[line], slot) if kept < slots else slot
            owns.append(own)
            begin = pl.multiple_of(head_of(kept) + block * lat, 16)
            sources.append(land[line, pl.ds(begin, lat), :])
            exponents.append(
                mm(feats[line * kept + block], query[own], left_dim=0)
            )
        results = []
        for exponent, source in zip(exponents, sources):
            wide = jnp.exp2(exponent)
            square = wide * wide
            results.append(
                (mm(source, wide.astype(BF16)), mm(source, (square * square).astype(BF16)))
            )
        for own, (first, second) in zip(owns, results):
            acc[own, 0:lat] += first
            acc[own, lat : 2 * lat] += second

    large, count = groups[0], counts[phase]
    small = groups[1] if len(groups) > 1 else 0
    whole = (count + large - 1 - small) // large
    lax.fori_loop(0, whole, lambda group, carry: work(group * large, large), None)
    left = count - whole * large
    for size, below in zip(groups[1:], (*groups[2:], 0)):
        pl.when((left > below) & (left <= size))(functools.partial(work, whole * large, size))


def lines_of(refs, parts):
    return [[(refs[index], start, length) for index, start, length in line] for line in parts]


def to_smem(pairs, sems):
    copies = [
        pltpu.make_async_copy(source, ref, sems.at[index])
        for index, (source, ref) in enumerate(pairs)
    ]
    for copy in copies:
        copy.start()

    def ready():
        for copy in copies:
            copy.wait()

    return ready


def tiles_kernel(
    kept, slots, rows, lat, phase, parts, ref_count, has_earlier, tiles_in, counts_in, query, *rest
):
    earlier, rest = (rest[0], rest[1:]) if has_earlier else (None, rest)
    lines, (acc, tiles, counts, sems, *scratch) = lines_of(rest, parts), rest[ref_count:]
    ready = to_smem(((tiles_in, tiles), (counts_in, counts)), sems)
    if has_earlier:
        acc[...] = earlier[...]
    else:
        acc[...] = jnp.zeros_like(acc)
    gather_tiles(
        kept, slots, rows, lat, phase, tiles, counts, query, lines, acc, scratch, ready=ready
    )


def arrivals_kernel(
    kept, slots, rows, lat, homes, phases, parts, ref_count, tiles_in, counts_in, query_in,
    send_turned, first, second, *rest,
):
    refs, rest = rest[:ref_count], rest[ref_count:]
    tiles, counts, query, arrived, beyond, acc, few, few_counts, few_query, *scratch = rest
    terms = scratch[2]
    my_sub = lax.axis_index("sub")
    query[...] = query_in[...]
    for phase in range(phases):
        count = counts_in[phase]
        counts[phase] = count

        def keep(place, carry, phase=phase):
            tiles[phase, place] = tiles_in[phase, place]
            return carry

        lax.fori_loop(0, count, keep, 0)
    few_counts[0] = 0

    def add(phase, entry):
        place = counts[phase]
        tiles[phase, place] = entry
        counts[phase] = place + 1

    def word_of(words, mate):
        return lax.shift_right_logical(words, 6 * mate)

    near_count = INFO // 2
    plane = MATES * slots
    inverse = 65536 // slots + 1
    own_words = sum(home << (6 * i) for i, home in enumerate((12, 13, 8, 9)))
    below_place, above_place = places_of_partners()
    for index, ref in enumerate((first, second)):
        side = jnp.where(below_place == index, 0, 1)
        head = ref[0 : head_of(kept), :].astype(F32)
        query_terms(terms, head, kept)
        info = head[3 * kept + 1 : 3 * kept + 2, :]
        lane = lax.broadcasted_iota(jnp.int32, info.shape, 1)

        def read(place, info=info, lane=lane):
            return jnp.sum(jnp.where(lane == place, info, 0.0)).astype(jnp.int32)

        tag, row = read(side * INFO), read(side * INFO + 1)
        codes = [read(side * INFO + 2 + k) for k in range(near_count)]
        own = jnp.where(tag > 0, tag - 1, OSLOTS)
        arrived[2 * index] = own
        arrived[2 * index + 1] = row
        query[own] = features(terms, row, kept)
        line_words = sum(home << (6 * i) for i, home in enumerate(homes[8 * index : 8 * index + 4]))

        @pl.when(tag > 0)
        def _(own=own, row=row, codes=codes, side=side, index=index, line_words=line_words):
            home = homes[8 * index]
            add(home // 8, own * 256 + home % 8 * 16 + row)
            for code in codes:
                device = lax.shift_right_logical(code * inverse, 16)
                slot = code - device * slots
                mate = jnp.bitwise_xor(jnp.bitwise_and(device, MATES - 1), my_sub)
                step = lax.shift_right_logical(device, 2) - 1
                word = jnp.where(step == 0, word_of(line_words, mate), word_of(own_words, mate))
                phase = jnp.bitwise_and(lax.shift_right_logical(word, 3), 7)
                line = jnp.bitwise_and(word, 7)

                @pl.when(step != 2 * side - 1)
                def _(phase=phase, line=line, slot=slot):
                    add(phase, own * 256 + line * 16 + slot)

        other = 1 - side
        tag, row = read(other * INFO), read(other * INFO + 1)
        codes = [read(other * INFO + 2 + k) for k in range(near_count)]
        few_query[index] = features(terms, row, kept)

        @pl.when(tag > 0)
        def _(codes=codes, side=side, index=index):
            for code in codes:
                device = lax.shift_right_logical(code * inverse, 16)
                slot = code - device * slots
                mate = jnp.bitwise_xor(jnp.bitwise_and(device, MATES - 1), my_sub)
                step = lax.shift_right_logical(device, 2) - 1

                @pl.when(step == 1 - 2 * side)
                def _(slot=slot, mate=mate, index=index):
                    place = few_counts[0]
                    few[0, place] = index * 256 + mate * 16 + slot
                    few_counts[0] = place + 1

    few_query[2] = few_query[0]
    for extra in range(GROUPS[0]):
        few[0, few_counts[0] + extra] = 2 * 256
        for phase in range(phases):
            tiles[phase, counts[phase] + extra] = OSLOTS * 256
    acc[...] = jnp.zeros_like(acc)
    gather_tiles(
        kept, slots, rows, lat, 0, few, few_counts, few_query, lines_of(refs, parts), acc, scratch,
        FEW_GROUPS,
    )
    if beyond.shape[0] == 1:
        upper = lax.axis_index("slab") * 2 >= lax.axis_size("slab")
        chosen = [jnp.where(upper, below_place, above_place)]
    else:
        chosen = [below_place, above_place]
    for place, index in enumerate(chosen):
        beyond[place] = mm(send_turned[...], acc[index].astype(BF16)).astype(BF16)


def last_kernel(
    kept, slots, rows, lat, phase, parts, ref_count, ways, scale, target_in, tiles_in, counts_in,
    arrived_in, query, send_turned, in_turned, w_out, pay, first, second, earlier, *rest,
):
    passed, rest = rest[:ways], rest[ways:]
    lines, rest = lines_of(rest, parts), rest[ref_count:]
    out, target, tiles, counts, arrived, sems, acc, sums, joined, hidden, updated, stores, *scratch = rest
    ready = to_smem(
        ((target_in, target), (tiles_in, tiles), (counts_in, counts), (arrived_in, arrived)), sems
    )
    acc[...] = earlier[...]
    gather_tiles(
        kept, slots, rows, lat, phase, tiles, counts, query, lines, acc, scratch, ready=ready
    )
    hole = first_hole(target, slots)
    me = lax.axis_index("slab") * lax.axis_size("sub") + lax.axis_index("sub")
    for row in range(kept):
        out_slot = target[slot_of(row, hole, kept, slots)]
        own = jnp.where(owner_of(out_slot) == me, out_slot - me * OSLOTS, OSLOTS)
        start = head_of(kept) + row * lat
        joined[own, 0:lat, :] = pay[start : start + lat, :]
    for index, ref in enumerate((first, second)):
        start = pl.multiple_of(head_of(kept) + arrived[2 * index + 1] * lat, 16)
        joined[arrived[2 * index], 0:lat, :] = ref[pl.ds(start, lat), :]
    for own in range(OSLOTS):
        sums[own] = mm(send_turned[...], acc[own].astype(BF16))
    below_place, above_place = places_of_partners()
    if ways == 1:
        upper = lax.axis_index("slab") * 2 >= lax.axis_size("slab")
        chosen = [jnp.where(upper, below_place, above_place)]
    else:
        chosen = [below_place, above_place]
    for index, ref in zip(chosen, passed):
        sums[arrived[2 * index]] += ref[...].astype(F32)
    for own in range(OSLOTS):
        joined[own, lat : 2 * lat, :] = (sums[own] * scale).astype(BF16)
    for own in range(OSLOTS):
        before = mm(in_turned[...], joined[own])
        hidden[own] = (before * (0.5 + 0.5 * jnp.tanh(0.5 * before))).astype(BF16)
    copies = []
    out_turned = jnp.transpose(w_out[...])
    for own in range(OSLOTS):
        new = joined[own, 0:lat, :].astype(F32) + mm(out_turned, hidden[own])
        updated[own] = jnp.transpose(new.astype(BF16))
        copies.append(
            pltpu.make_async_copy(
                updated.at[own], out.at[own * rows : own * rows + rows, :], stores.at[own]
            )
        )
        copies[-1].start()
    for copy in copies:
        copy.wait()


def on_device(latent, positions, target, neighbours, w_send, w_in, w_out):
    lat = latent.shape[1]
    slots = target.shape[0]
    rows = latent.shape[0] // slots
    near_count = neighbours.shape[1]
    slab_count = lax.axis_size("slab")
    kept = slots - 1 if slab_count <= 4 else slots
    length = head_of(kept) + kept * lat
    if lax.axis_size("sub") != MATES:
        raise ValueError("sizes")
    pairs = [[(i, i + 1) for i in range(begin, slab_count - 1, 2)] for begin in (0, 1)]
    pairs = [some + [(j, i) for i, j in some] for some in pairs]
    def mate_of(value, bit):
        return lax.ppermute(value, "sub", [(i, i ^ bit) for i in range(MATES)])

    def swap_first(value):
        return lax.ppermute(value, "slab", pairs[0])

    def swap_second(value):
        return lax.ppermute(value, "slab", pairs[1])

    cut_up, cut = length - REST_UP * lat, length - REST * lat
    pay = call(
        functools.partial(pack_kernel, kept, slots, rows),
        "pack",
        jax.ShapeDtypeStruct((length, rows), BF16),
        [HB, HB, HB, HB],
        VM,
        [
            pltpu.SMEM((slots,), jnp.int32),
            pltpu.SMEM((near_count, slots), jnp.int32),
            pltpu.VMEM(positions.shape, BF16),
            pltpu.VMEM((head_of(kept), rows), F32),
            pltpu.VMEM((slots, rows, lat), BF16),
            pltpu.SemaphoreType.DMA((slots + 3,)),
        ],
        in_hbm(target, neighbours.T, latent, positions),
    )
    across = mate_of(pay, 2)
    first_own, second_own = swap_first(pay), swap_second(pay)
    pair = mate_of(pay, 1)

    homes = (10, 16, 18, 24, 0, 1, 8, 9, 11, 17, 19, 25)
    phase_count = 4
    most = OSLOTS * (near_count + 1) + GROUPS[0]
    tiles, counts, query, send_turned, in_turned = call(
        functools.partial(plan_kernel, kept, slots, rows, homes, phase_count),
        "plan",
        (
            jax.ShapeDtypeStruct((phase_count, most), jnp.int32),
            jax.ShapeDtypeStruct((phase_count,), jnp.int32),
            jax.ShapeDtypeStruct((OSLOTS + 1, FEAT, rows), BF16),
            jax.ShapeDtypeStruct((lat, 2 * lat), BF16),
            jax.ShapeDtypeStruct((lat, 2 * lat), BF16),
        ),
        [HB, HB, VM, HB, HB],
        (SM, SM, VM, VM, VM),
        [
            pltpu.SMEM((slots,), jnp.int32),
            pltpu.SMEM((near_count, slots), jnp.int32),
            pltpu.VMEM(w_send.shape, BF16),
            pltpu.VMEM(w_in.shape, BF16),
            pltpu.VMEM((rows // 128, FEAT * kept, 128), F32),
            pltpu.SemaphoreType.DMA((4,)),
        ],
        (*in_hbm(target, neighbours.T), pay, *in_hbm(w_send, w_in)),
    )

    def scratch_for(parts):
        return [
            pltpu.VMEM((len(parts), length, rows), BF16),
            pltpu.VMEM((len(parts) * kept, FEAT, rows), BF16),
            pltpu.VMEM((rows // 128, FEAT * kept, 128), F32),
            pltpu.SMEM((len(parts),), jnp.int32),
        ]

    sums = (OSLOTS + 1, 2 * lat, rows)
    whole = lambda index: ((index, 0, length),)
    split = lambda index, other, start=0: ((index, 0, cut), (other, start, length - cut))
    split_up = lambda index, other: ((index, 0, cut_up), (other, 0, length - cut_up))

    def tiles_call(phase, parts, refs, earlier):
        earlier = [] if earlier is None else [earlier]
        return call(
            functools.partial(
                tiles_kernel, kept, slots, rows, lat, phase, parts, len(refs), bool(earlier)
            ),
            f"tiles{phase}",
            jax.ShapeDtypeStruct(sums, F32),
            [AN, AN, VM] + [VM] * (len(earlier) + len(refs)),
            VM,
            [
                pltpu.SMEM((phase_count, most), jnp.int32),
                pltpu.SMEM((phase_count,), jnp.int32),
                pltpu.SemaphoreType.DMA((2,)),
                *scratch_for(parts),
            ],
            (tiles, counts, query, *earlier, *refs),
        )

    partial = tiles_call(0, (whole(0), whole(1)), [pay, pair], None)
    across, partial = lax.optimization_barrier((across, partial))
    first_far, second_far = swap_first(across[:cut_up]), swap_second(across[:cut])
    across_pair = mate_of(across, 1)
    far_rest = mate_of(jnp.concatenate([first_own[cut_up:], second_own[cut:]], axis=0), 2)
    first_pair, second_pair = mate_of(first_own, 1), mate_of(second_own, 1)
    ways = 1 if slab_count <= 4 else 2
    tiles, counts, query, arrived, beyond = call(
        functools.partial(
            arrivals_kernel, kept, slots, rows, lat, homes, phase_count,
            tuple(whole(index) for index in range(4)), 4,
        ),
        "arrivals",
        (
            jax.ShapeDtypeStruct((phase_count, most), jnp.int32),
            jax.ShapeDtypeStruct((phase_count,), jnp.int32),
            jax.ShapeDtypeStruct((OSLOTS + 1, FEAT, rows), BF16),
            jax.ShapeDtypeStruct((4,), jnp.int32),
            jax.ShapeDtypeStruct((ways, lat, rows), BF16),
        ),
        [SM, SM] + [VM] * 8,
        (SM, SM, VM, SM, VM),
        [
            pltpu.VMEM((3, 2 * lat, rows), F32),
            pltpu.SMEM((1, 2 * near_count + GROUPS[0]), jnp.int32),
            pltpu.SMEM((1,), jnp.int32),
            pltpu.VMEM((3, FEAT, rows), BF16),
            *scratch_for(range(4)),
        ],
        (
            tiles, counts, query, send_turned, first_own, second_own, pay, pair, across,
            across_pair,
        ),
    )
    two_up = [(i, i + 2) for i in range(slab_count - 2)]
    two_down = [(j, i) for i, j in two_up]
    if ways == 1:
        passed = [lax.ppermute(beyond[0], "slab", two_up + two_down)]
    else:
        passed = [
            lax.ppermute(beyond[1], "slab", two_up), lax.ppermute(beyond[0], "slab", two_down)
        ]
    partial = tiles_call(
        1,
        tuple(whole(index) for index in range(6)),
        [across, across_pair, first_own, second_own, pay, pair],
        partial,
    )
    first_far, second_far, partial = lax.optimization_barrier((first_far, second_far, partial))
    first_last, second_last = mate_of(first_far, 1), mate_of(second_far, 1)
    last_rest = mate_of(far_rest, 1)
    partial = tiles_call(
        2,
        (whole(0), whole(1), split_up(2, 4), split(3, 4, length - cut_up)),
        [first_pair, second_pair, first_far, second_far, far_rest],
        partial,
    )
    scale = (rows * (near_count + 1)) ** -0.5
    last = (split_up(0, 2), split(1, 2, length - cut_up))
    return call(
        functools.partial(last_kernel, kept, slots, rows, lat, 3, last, 3, ways, scale),
        "last",
        jax.ShapeDtypeStruct((OSLOTS * rows, lat), BF16),
        [AN, AN, AN, AN] + [VM] * (11 + ways),
        HB,
        [
            pltpu.SMEM((slots,), jnp.int32),
            pltpu.SMEM((phase_count, most), jnp.int32),
            pltpu.SMEM((phase_count,), jnp.int32),
            pltpu.SMEM((4,), jnp.int32),
            pltpu.SemaphoreType.DMA((4,)),
            pltpu.VMEM(sums, F32),
            pltpu.VMEM((OSLOTS + 1, lat, rows), F32),
            pltpu.VMEM((OSLOTS + 1, 2 * lat, rows), BF16),
            pltpu.VMEM((OSLOTS, lat, rows), BF16),
            pltpu.VMEM((OSLOTS, rows, lat), BF16),
            pltpu.SemaphoreType.DMA((OSLOTS,)),
            *scratch_for(last),
        ],
        (
            target, tiles, counts, arrived, query, send_turned, in_turned, w_out, pay, first_own,
            second_own, partial, *passed, first_last, second_last, last_rest,
        ),
    )


def solution(mesh):
    placed = (
        P(("grp", "slab", "sub"), None),
        P(None, ("grp", "slab", "sub")),
        P(("grp", "slab", "sub")),
        P(("grp", "slab", "sub"), None),
        P(),
        P(),
        P(),
    )
    return jax.shard_map(
        on_device,
        mesh=mesh,
        in_specs=placed,
        out_specs=P(("grp", "slab", "sub"), None),
        check_vma=False,
    )
```
